256 devices in a mesh: tm: 16 (over z_hi, y), tensor: 8 (over x, core), dp: 2 (over z_lo).
Axes of the slice: x: 4, y: 4, z: 8 (z_hi: 4, z_lo: 2; z = z_hi * 2 + z_lo), core: 2. Of those that a mesh axis runs over, the one named last changes fastest.
Arguments:
- inputs: bfloat16 [2, 16384, 1536], P('dp', 'tm'), may hold values from -6 to 6
- grad_blocks: bfloat16 [2, 1024, 128, 1536], P('dp', 'tm', 'tensor'), may hold values from -6 to 6
- block_device: int32 [2, 1024, 1], P('dp'), may hold values from 0 to 15; in each aligned block of 64 rows (0 to 63, 64 to 127, ..., all dimensions but the last counted through in order) at most 5 rows name the same one
- block_sub: int32 [2, 1024], P('dp'), may hold values from 0 to 7
- block_rows: int32 [2, 1024], P('dp'), may hold values from 1 to 128
- seg_lengths: int32 [2, 22], P('dp'), may hold values from 1 to 750, 16384 in all within a row
- value_weight: bfloat16 [1536, 1536], P('tensor'), may hold values from -0.15625 to 0.15625
- gate_weight: bfloat16 [1536, 1536], P('tensor'), may hold values from -0.15625 to 0.15625
- out_weight: bfloat16 [1536, 1536], P('tensor'), may hold values from -0.15625 to 0.15625
- conv_kernel: bfloat16 [31, 1536], P(None, 'tensor'), may hold values from -1 to 1
- norm_gain: float32 [1536], replicated, may hold values from 0.5 to 1.5
Outputs:
- input_grad: bfloat16 [2, 16384, 1536], P('dp', ('tm', 'tensor'))
- value_grad: float32 [1536, 1536], P('tensor', ('tm', 'dp'))
- gate_grad: float32 [1536, 1536], P('tensor', ('tm', 'dp'))
- out_grad: float32 [1536, 1536], P('tensor', ('tm', 'dp'))
- kernel_grad: float32 [31, 1536], P(None, 'tensor')
- gain_grad: float32 [1536], replicated
The draws below stay inside these ranges and needn't reach their ends.
Inputs may be any that keep to these rules, and one draw needn't show every extreme that they name: `block_device`: for each group and tm index t, among the 64 blocks t * 64 to (t + 1) * 64 - 1 no value appears more than 5 times; in some of these runs a value appears exactly 5 times. `seg_lengths`: the 22 lengths of each group sum to 16384; the largest is 750.
All inputs are finite; a program needn't handle non-finite values.
Results may differ from the reference program's by a relative error of at most 0.03.
Values may be sent and summed in bfloat16 or wider, within the bound.
A program may use at most 128 MiB of HBM per device.

```python
import math
import jax
import jax.numpy as jnp
import numpy as np
from jax import lax

D = 1536
KERNEL = 31
ROWS_BLK = 128
SEG_MAX = 750
FRAMES = 16384
SEGS = 22
FB_DEV = 8
BLK_DEV = 64
NBLK = 1024
CAP = 5
N_TM = 16
N_DP = 2


def place_ends(drawn, own_key, low, top_value):
    spot = [jax.random.randint(jax.random.fold_in(own_key, axis), (), 0, length) for axis, length in enumerate(drawn.shape)]
    widest = drawn.shape.index(max(drawn.shape))
    neighbour = spot[:widest] + [(spot[widest] + 1) % drawn.shape[widest]] + spot[widest + 1:]
    return drawn.at[tuple(spot)].set(low).at[tuple(neighbour)].set(top_value)


def block_scale(rng, dims, shards, low, largest):
    def one(axis_at, shards_of):
        draws = jax.random.uniform(jax.random.fold_in(jax.random.fold_in(rng, 6), axis_at), (shards_of,), jnp.float32, low / len(shards), largest / len(shards))
        return jnp.repeat(jnp.exp(draws), dims[axis_at] // shards_of).reshape((-1,) + (1,) * (len(dims) - axis_at - 1))

    gain = one(*shards[0])
    for cut in shards[1:]:
        gain = gain * one(*cut)
    return gain


def length_profile(number_of, total, limit, skew):
    loads = [(1 << 20) // math.isqrt(standing ** skew) + 1 for standing in range(2, number_of + 1)]
    rest, holding = total - limit - (number_of - 1), [1] * (number_of - 1)
    while rest > 0:
        movable = [i for i in range(number_of - 1) if holding[i] < limit]
        whole, left = sum([loads[i] for i in movable]), rest
        for i in movable:
            extra = min(limit - holding[i], max(1, left * loads[i] // whole), rest)
            holding[i] = holding[i] + extra
            rest = rest - extra
    return np.array([limit] + holding)


def ragged(key, count, total, bound, lean):
    if count == 2:
        one = jax.random.randint(key, (), max(1, total - bound), min(bound, total - 1) + 1)
        return jnp.stack([one, total - one])
    tallies = jnp.asarray(length_profile(count, total, bound, lean), jnp.int32)
    pairs = (count - 1) // 2
    giver, receiver = tallies[1:1 + 2 * pairs:2], tallies[2:2 + 2 * pairs:2]
    slack = jnp.minimum(giver - 1, bound - receiver)
    passed = jax.random.randint(jax.random.fold_in(key, 1), (pairs,), 0, 1 << 20) % (slack + 1)
    tallies = tallies.at[1:1 + 2 * pairs:2].set(giver - passed).at[2:2 + 2 * pairs:2].set(receiver + passed)
    return tallies[jax.random.permutation(jax.random.fold_in(key, 2), count)]


def shared_out(own_key, own, number, rows, amount, top, bound, slope):
    sequence = jax.random.permutation(own_key, amount)
    packed, common = shares(amount, rows * top, bound, slope, True), shares(amount, rows * top, bound, slope, False)
    places = jnp.arange(amount)

    def named(sizes, rotation):
        used = int((sizes > 0).sum())
        fixed = max(1, used // 4)
        passed = fixed + (places - fixed + rotation * (used - fixed)) % max(1, amount - fixed)
        return jnp.zeros((amount,), jnp.int32).at[sequence[jnp.where(places < fixed, places, passed)]].set(jnp.asarray(sizes, jnp.int32))

    sizes = jnp.where(number % 4 == 0, named(packed, number // 4), named(common, number - number // 4 - 1))
    mixed = jax.random.permutation(jax.random.fold_in(own, 3), amount)
    source_of, receiver = mixed[0:amount // 2 * 2:2], mixed[1:amount // 2 * 2:2]
    slack = jnp.minimum(sizes[source_of] - 1, bound - sizes[receiver]) // 2
    slack = jnp.where((source_of == sequence[0]) | (receiver == sequence[0]) | (sizes[receiver] == 0), 0, jnp.maximum(slack, 0))
    passed = jax.random.randint(jax.random.fold_in(own, 4), (amount // 2,), 0, 1 << 20) % (slack + 1)
    sizes = sizes.at[source_of].add(-passed).at[receiver].add(passed)
    items = jnp.searchsorted(jnp.cumsum(sizes), jnp.arange(rows * top), side="right").astype(jnp.int32)
    grid = items.reshape(top, rows).T
    grid = grid[jax.random.permutation(jax.random.fold_in(own, 1), rows)]
    rotation = jax.random.randint(jax.random.fold_in(own, 2), (rows, 1), 0, top)
    return jnp.take_along_axis(grid, (jnp.arange(top)[None, :] + rotation) % top, axis=1)


def shares(amount, total, limit, skew, full):
    weights = [(1 << 20) // math.isqrt(grade ** skew) + 1 for grade in range(1, amount + 1)]
    largest = limit if full else min(limit, max(-(-total // amount), total * weights[0] // sum(weights)))
    least = 1 if total - largest >= amount - 1 else 0
    given, rest = [largest] + [least] * (amount - 1), total - largest - least * (amount - 1)
    while rest > 0:
        candidates = [i for i in range(1, amount) if given[i] < largest] or [i for i in range(1, amount) if given[i] < limit]
        pool, remaining = sum([weights[i] for i in candidates]), rest
        for i in candidates:
            addition = min(limit - given[i], max(1, remaining * weights[i] // pool), rest)
            given[i] = given[i] + addition
            rest = rest - addition
    return np.array(given)


def bell_draw(key, extent, scale, bound, split=(), kind=jnp.bfloat16):
    values = scale * jax.random.normal(key, extent, jnp.float32)
    if split:
        values = values * block_scale(key, extent, split, -0.22, 0.18)
    return jnp.clip(values, -bound, bound).astype(kind)


def setup_inputs(seed: int = 0) -> dict:
    streams_of = jax.random.split(jax.random.key(seed), 12)
    inputs = bell_draw(streams_of[0], (N_DP, FRAMES, D), 1.0, 6.0, ((0, 2), (1, 16)))
    grad_blocks = bell_draw(streams_of[1], (N_DP, NBLK, ROWS_BLK, D), 1.0, 6.0, ((0, 2), (1, 16), (2, 8)))
    block_device_keys = jax.random.split(jax.random.fold_in(streams_of[2], 1), N_DP * NBLK // BLK_DEV)
    block_device_turns = jax.random.permutation(jax.random.fold_in(streams_of[2], 3), N_DP * NBLK // BLK_DEV)
    block_device = jax.vmap(lambda own, number: shared_out(jax.random.fold_in(streams_of[2], 2), own, number, BLK_DEV, N_TM, 1, CAP, 2))(block_device_keys, block_device_turns).reshape((N_DP, NBLK, 1))
    block_sub = place_ends(jax.random.randint(streams_of[3], (N_DP, NBLK), 0, FB_DEV), jax.random.fold_in(streams_of[3], 1), 0, FB_DEV - 1).astype(jnp.int32)
    block_rows = place_ends(jax.random.randint(streams_of[4], (N_DP, NBLK), 1, ROWS_BLK + 1), jax.random.fold_in(streams_of[4], 1), 1, ROWS_BLK).astype(jnp.int32)
    seg_lengths = jax.vmap(lambda own: ragged(own, SEGS, FRAMES, SEG_MAX, 2))(jax.random.split(streams_of[5], N_DP)).reshape((N_DP, SEGS)).astype(jnp.int32)
    value_weight = bell_draw(streams_of[6], (D, D), D ** -0.5, 0.15625, ((0, 8),))
    gate_weight = bell_draw(streams_of[7], (D, D), D ** -0.5, 0.15625, ((0, 8),))
    out_weight = bell_draw(streams_of[8], (D, D), D ** -0.5, 0.15625, ((0, 8),))
    conv_kernel = bell_draw(streams_of[9], (KERNEL, D), KERNEL ** -0.5, 1.0, ((1, 8),))
    norm_gain = jnp.clip(1.0 + 0.1 * jax.random.normal(streams_of[10], (D,), jnp.float32), 0.5, 1.5)
    return dict(inputs=inputs, grad_blocks=grad_blocks, block_device=block_device, block_sub=block_sub, block_rows=block_rows, seg_lengths=seg_lengths, value_weight=value_weight, gate_weight=gate_weight, out_weight=out_weight, conv_kernel=conv_kernel, norm_gain=norm_gain)


epsilon = 1e-05

def segment_of(lengths, first, count, total):
    position = first + jnp.arange(count, dtype=jnp.int32)
    bounds = jnp.cumsum(lengths).astype(jnp.int32)
    labels = lax.optimization_barrier(jnp.sum((position[:, None] >= bounds[None, :]).astype(jnp.int32), axis=1))
    inside = (position >= 0) & (position < total)
    return jnp.where(inside, labels, -1).astype(jnp.int32)

def contract_last(left, right):
    return lax.dot_general(left, right, (((1,), (1,)), ((), ())), preferred_element_type=jnp.float32)

def reference(inputs, grad_blocks, block_device, block_sub, block_rows, seg_lengths, value_weight, gate_weight, out_weight, conv_kernel, norm_gain):
    half = KERNEL // 2
    factor = 1.0 / math.sqrt(N_DP * FRAMES)
    kern_f32 = conv_kernel.astype(jnp.float32)
    value_sum = jnp.zeros((D, D), jnp.float32)
    gate_sum = jnp.zeros((D, D), jnp.float32)
    out_sum = jnp.zeros((D, D), jnp.float32)
    kernel_sum = jnp.zeros((KERNEL, D), jnp.float32)
    gain_sum = jnp.zeros((D,), jnp.float32)
    results = []
    for replica in range(N_DP):
        frames_f32 = inputs[replica].astype(jnp.float32)
        centered = frames_f32 - lax.optimization_barrier(jnp.mean(frames_f32, axis=1, keepdims=True))
        inv_std = lax.rsqrt(lax.optimization_barrier(jnp.mean(centered * centered, axis=1, keepdims=True)) + epsilon)
        normed = centered * inv_std
        norm_out = (normed * norm_gain).astype(jnp.bfloat16)
        value_lin = contract_last(norm_out, value_weight)
        gate_lin = contract_last(norm_out, gate_weight)
        gate_sig = jax.nn.sigmoid(gate_lin)
        glu_out = (value_lin * gate_sig).astype(jnp.bfloat16)
        labels = segment_of(seg_lengths[replica], -half, FRAMES + 2 * half, FRAMES)
        centre = labels[half:half + FRAMES]
        glu_wide = jnp.pad(glu_out.astype(jnp.float32), ((half, half), (0, 0)))
        near_masks = [(labels[offset:offset + FRAMES] == centre).astype(jnp.float32)[:, None] for offset in range(KERNEL)]
        conv_out = jnp.zeros((FRAMES, D), jnp.float32)
        for offset in range(KERNEL):
            conv_out = conv_out + kern_f32[offset] * glu_wide[offset:offset + FRAMES] * near_masks[offset]
        conv_sig = jax.nn.sigmoid(conv_out)
        swish_out = (conv_out * conv_sig).astype(jnp.bfloat16)
        targets = block_device[replica, :, 0] * FB_DEV + block_sub[replica]
        live_rows = (jnp.arange(ROWS_BLK, dtype=jnp.int32)[None, :] < block_rows[replica][:, None]).astype(jnp.float32)
        masked = grad_blocks[replica].astype(jnp.float32) * live_rows[:, :, None]
        routed = jax.ops.segment_sum(masked, targets, num_segments=FRAMES // ROWS_BLK)
        out_cot = routed.reshape(FRAMES, D).astype(jnp.bfloat16)
        out_sum = out_sum + jnp.dot(swish_out.T, out_cot, preferred_element_type=jnp.float32)
        swish_cot = contract_last(out_cot, out_weight)
        conv_cot = swish_cot * conv_sig * (1.0 + conv_out * (1.0 - conv_sig))
        cot_wide = jnp.pad(conv_cot, ((half, half), (0, 0)))
        glu_cot = jnp.zeros((FRAMES, D), jnp.float32)
        kern_rows = []
        for offset in range(KERNEL):
            kern_rows.append(lax.optimization_barrier(jnp.sum(conv_cot * glu_wide[offset:offset + FRAMES] * near_masks[offset], axis=0)))
            mirror = KERNEL - 1 - offset
            glu_cot = glu_cot + kern_f32[offset] * cot_wide[mirror:mirror + FRAMES] * near_masks[mirror]
        kernel_sum = kernel_sum + jnp.stack(kern_rows)
        value_cot = (glu_cot * gate_sig).astype(jnp.bfloat16)
        gate_cot = (glu_cot * value_lin * gate_sig * (1.0 - gate_sig)).astype(jnp.bfloat16)
        value_sum = value_sum + jnp.dot(value_cot.T, norm_out, preferred_element_type=jnp.float32)
        gate_sum = gate_sum + jnp.dot(gate_cot.T, norm_out, preferred_element_type=jnp.float32)
        norm_cot = jnp.dot(value_cot, value_weight, preferred_element_type=jnp.float32) + jnp.dot(gate_cot, gate_weight, preferred_element_type=jnp.float32)
        scaled_cot = norm_cot * norm_gain
        gain_sum = gain_sum + lax.optimization_barrier(jnp.sum(norm_cot * normed, axis=0))
        input_f32 = out_cot.astype(jnp.float32) + inv_std * (scaled_cot - lax.optimization_barrier(jnp.mean(scaled_cot, axis=1, keepdims=True)) - normed * lax.optimization_barrier(jnp.mean(scaled_cot * normed, axis=1, keepdims=True)))
        results.append(input_f32.astype(jnp.bfloat16))
    return (jnp.stack(results), value_sum * factor, gate_sum * factor, out_sum * factor, kernel_sum * factor, gain_sum * factor)
```

```python
import math

import jax
import jax.numpy as jnp
from jax import lax
from jax.experimental import pallas as pl
from jax.experimental.pallas import tpu as pltpu
from jax.sharding import PartitionSpec as P

KERNEL = 31
ROWS_BLK = 128


epsilon = 1e-05


def with_halo(cells, sides, width):
    for axis, dim in sides:
        count = lax.axis_size(axis)
        ends = count - 1
        head = lax.slice_in_dim(cells, 0, width, axis=dim)
        tail = lax.slice_in_dim(cells, cells.shape[dim] - width, cells.shape[dim], axis=dim)
        cells = jnp.concatenate(
            [
                lax.ppermute(tail, axis, [(i, (i + 1) % count) for i in range(ends)]),
                cells,
                lax.ppermute(head, axis, [((i + 1) % count, i) for i in range(ends)]),
            ],
            axis=dim,
        )
    return cells


def segment_of(lengths, first, count, total):
    position = first + jnp.arange(count, dtype=jnp.int32)
    bounds = jnp.cumsum(lengths)
    labels = jnp.sum((position[:, None] >= bounds[None, :]).astype(jnp.int32), axis=1)
    inside = (position >= 0) & (position < total)
    return jnp.where(inside, labels, -1)


def contract_last(left, right):
    return lax.dot_general(
        left, right, (((1,), (1,)), ((), ())), preferred_element_type=jnp.float32
    )


def norm_backward(full_cot, norm_cot, normed, inv_std, norm_gain):
    scaled_cot = norm_cot * norm_gain
    return full_cot.astype(jnp.float32) + inv_std * (
        scaled_cot
        - jnp.mean(scaled_cot, axis=1, keepdims=True)
        - normed * jnp.mean(scaled_cot * normed, axis=1, keepdims=True)
    )


def places():
    tm, te, dp = (lax.axis_index("tm"), lax.axis_index("tensor"), lax.axis_index("dp"))
    return tm, te, dp


def y_peer(step):
    tm, te, dp = places()
    return {"tm": (tm // 4) * 4 + (tm + step) % 4, "tensor": te, "dp": dp}


def z_peer(step):
    tm, te, dp = places()
    there = ((tm // 4) * 2 + dp + step) % 8
    return {"tm": (there // 2) * 4 + tm % 4, "tensor": te, "dp": there % 2}


def t_peer(step):
    tm, te, dp = places()
    return {"tm": tm, "tensor": (te + step) % 8, "dp": dp}


def x_peer(step):
    tm, te, dp = places()
    return {"tm": tm, "tensor": (te + 2 * step) % 8, "dp": dp}


def sibling():
    tm, te, dp = places()
    return {"tm": tm, "tensor": (te // 2) * 2 + 1 - te % 2, "dp": dp}


class Copies:
    def __init__(self, send_sems, recv_sems):
        self.send_sems, self.recv_sems = send_sems, recv_sems
        self.made = []

    def send(self, src, dst, to):
        at = len(self.made)
        copy = pltpu.make_async_remote_copy(
            src_ref=src,
            dst_ref=dst,
            send_sem=self.send_sems.at[at],
            recv_sem=self.recv_sems.at[at],
            device_id=to,
            device_id_type=pl.DeviceIdType.MESH,
        )
        copy.start()
        self.made.append(copy)
        return copy

    def finish(self):
        for copy in self.made:
            copy.wait_send()


def meet(peers):
    barrier = pltpu.get_barrier_semaphore()
    for peer in peers:
        pl.semaphore_signal(
            barrier, inc=1, device_id=peer, device_id_type=pl.DeviceIdType.MESH
        )
    pl.semaphore_wait(barrier, len(peers))


def f32(value):
    return value.astype(jnp.float32)


REDUCE_COPIES = 1 + 6 + 12 + 14 + 7 + 3 + 7


def reduce_kernel(
    both_ref,
    out_ref,
    cot_ref,
    small_ref,
    both_sum,
    out_sum,
    cot_sum,
    small_sum,
    core_in,
    chip_sum,
    x_a,
    x_b,
    x_plus,
    x_minus,
    both_a,
    both_b,
    both_plus,
    both_minus,
    both_mid,
    both_z,
    out_a,
    out_b,
    out_plus,
    out_minus,
    out_mid,
    out_z,
    gain_in,
    small_mid,
    small_y,
    small_last,
    small_z,
    send_sems,
    recv_sems,
):
    tm, te, dp = places()
    y, z, x, core = (tm % 4, (tm // 4) * 2 + dp, te // 2, te % 2)
    meet(
        [t_peer(k) for k in range(1, 8)]
        + [y_peer(k) for k in range(1, 4)]
        + [z_peer(k) for k in range(1, 8)]
    )
    net = Copies(send_sems, recv_sems)
    lower, upper = (pl.ds(0, 2), pl.ds(2, 2))
    y_next, y_last, y_far = ((y + 1) % 4, (y + 3) % 4, (y + 2) % 4)
    x_next, x_last, x_far = ((x + 1) % 4, (x + 3) % 4, (x + 2) % 4)
    core_copy = net.send(cot_ref.at[:, 1 - core], core_in, sibling())
    first = []
    for ref, a, b in ((out_ref, out_a, out_b), (both_ref, both_a, both_b)):
        first.append(
            (
                net.send(ref.at[lower, y_far], a, y_peer(1)),
                net.send(ref.at[upper, y_far], b, y_peer(-1)),
            )
        )
    plain = []
    for ref, plus, minus in ((out_ref, out_plus, out_minus), (both_ref, both_plus, both_minus)):
        plain.append(
            (
                net.send(ref.at[upper, y_next], plus.at[upper], y_peer(1)),
                net.send(ref.at[lower, y_last], minus.at[lower], y_peer(-1)),
            )
        )
    gain_rows = pl.ds(32, 8)
    gain_in[te] = small_ref[gain_rows, :]
    gain_copies = [
        net.send(small_ref.at[gain_rows], gain_in.at[te], t_peer(k)) for k in range(1, 8)
    ]

    core_copy.wait_recv()

    def add_core(at):
        @pl.loop(0, 128, step=16)
        def _(row):
            rows = pl.ds(pl.multiple_of(row, 16), 16)
            chip_sum[at, rows] = (f32(cot_ref[at, core, rows]) + f32(core_in[at, rows])).astype(
                jnp.bfloat16
            )

    add_core(x_far)
    half_a, half_b = (pl.ds(0, 64), pl.ds(64, 64))
    x_first = (
        net.send(chip_sum.at[x_far, half_a], x_a, x_peer(1)),
        net.send(chip_sum.at[x_far, half_b], x_b, x_peer(-1)),
    )
    add_core(x_next)
    add_core(x_last)
    x_plain = (
        net.send(chip_sum.at[x_next, half_b], x_plus.at[half_b], x_peer(1)),
        net.send(chip_sum.at[x_last, half_a], x_minus.at[half_a], x_peer(-1)),
    )

    second = []
    for at, (ref, a, b, plus, minus) in enumerate(
        (
            (out_ref, out_a, out_b, out_plus, out_minus),
            (both_ref, both_a, both_b, both_plus, both_minus),
        )
    ):
        first[at][0].wait_recv()
        for i in range(2):
            a[i] = (f32(a[i]) + f32(ref[i, y_next])).astype(jnp.bfloat16)
        one = net.send(a, plus.at[lower], y_peer(1))
        first[at][1].wait_recv()
        for i in range(2):
            b[i] = (f32(b[i]) + f32(ref[i + 2, y_last])).astype(jnp.bfloat16)
        second.append((one, net.send(b, minus.at[upper], y_peer(-1))))

    x_first[0].wait_recv()

    def add_x(ref, at, start):
        @pl.loop(0, 64, step=16)
        def _(row):
            rows = pl.ds(pl.multiple_of(row, 16), 16)
            other = pl.ds(pl.multiple_of(row + start, 16), 16)
            ref[rows] = (f32(ref[rows]) + f32(chip_sum[at, other])).astype(jnp.bfloat16)

    add_x(x_a, x_next, 0)
    x_second = [net.send(x_a, x_plus.at[half_a], x_peer(1))]
    x_first[1].wait_recv()
    add_x(x_b, x_last, 64)
    x_second.append(net.send(x_b, x_minus.at[half_b], x_peer(-1)))

    for copy in gain_copies:
        copy.wait_recv()
    small_mid[pl.ds(0, 32), :] = small_ref[pl.ds(0, 32), :]
    total = gain_in[0]
    for at in range(1, 8):
        total = total + gain_in[at]
    small_mid[gain_rows, :] = total
    small_y[y] = small_mid[...]
    small_copies = [net.send(small_mid, small_y.at[y], y_peer(k)) for k in range(1, 4)]

    z_copies = []
    for at, (ref, plus, minus, mid, z_in) in enumerate(
        (
            (out_ref, out_plus, out_minus, out_mid, out_z),
            (both_ref, both_plus, both_minus, both_mid, both_z),
        )
    ):
        for copy in plain[at] + second[at]:
            copy.wait_recv()
        for i in range(4):
            total = (f32(ref[i, y]) + f32(plus[i]) + f32(minus[i])).astype(jnp.bfloat16)
            mid[2 * i] = total[:48]
            mid[2 * i + 1] = total[48:]
        z_in[z] = mid[z]
        z_copies.append(
            [net.send(mid.at[(z + k) % 8], z_in.at[z], z_peer(k)) for k in (4, 3, 5, 2, 6, 1, 7)]
        )

    for copy in small_copies:
        copy.wait_recv()
    total = small_y[0]
    for at in range(1, 4):
        total = total + small_y[at]
    small_last[...] = total
    small_z[z] = total
    last_copies = [net.send(small_last, small_z.at[z], z_peer(k)) for k in range(1, 8)]

    for copy in x_plain + tuple(x_second):
        copy.wait_recv()

    @pl.loop(0, 128, step=16)
    def _(row):
        rows = pl.ds(pl.multiple_of(row, 16), 16)
        cot_sum[rows] = (
            f32(cot_ref[x, core, rows])
            + f32(core_in[x, rows])
            + f32(x_plus[rows])
            + f32(x_minus[rows])
        )

    for copies, z_in, result in ((z_copies[0], out_z, out_sum), (z_copies[1], both_z, both_sum)):
        for copy in copies:
            copy.wait_recv()
        total = f32(z_in[0])
        for at in range(1, 8):
            total = total + f32(z_in[at])
        result[...] = total
    for copy in last_copies:
        copy.wait_recv()
    total = small_z[0]
    for at in range(1, 8):
        total = total + small_z[at]
    small_sum[...] = total
    net.finish()


def reduce_call(both, out, cot, small):
    span = out.shape[3]
    width = cot.shape[3]
    bf16 = jnp.bfloat16
    weights = []
    for lanes in (2 * span, span):
        weights += [
            pltpu.VMEM((2, 96, lanes), bf16),
            pltpu.VMEM((2, 96, lanes), bf16),
            pltpu.VMEM((4, 96, lanes), bf16),
            pltpu.VMEM((4, 96, lanes), bf16),
            pltpu.VMEM((8, 48, lanes), bf16),
            pltpu.VMEM((8, 48, lanes), bf16),
        ]
    return pl.pallas_call(
        reduce_kernel,
        out_shape=(
            jax.ShapeDtypeStruct((48, 2 * span), jnp.float32),
            jax.ShapeDtypeStruct((48, span), jnp.float32),
            jax.ShapeDtypeStruct((128, width), jnp.float32),
            jax.ShapeDtypeStruct((40, 256), jnp.float32),
        ),
        in_specs=[pl.BlockSpec(memory_space=pltpu.VMEM)] * 4,
        out_specs=[pl.BlockSpec(memory_space=pltpu.VMEM)] * 4,
        scratch_shapes=[
            pltpu.VMEM((4, 128, width), bf16),
            pltpu.VMEM((4, 128, width), bf16),
            pltpu.VMEM((64, width), bf16),
            pltpu.VMEM((64, width), bf16),
            pltpu.VMEM((128, width), bf16),
            pltpu.VMEM((128, width), bf16),
        ]
        + weights
        + [
            pltpu.VMEM((8, 8, 256), jnp.float32),
            pltpu.VMEM((40, 256), jnp.float32),
            pltpu.VMEM((4, 40, 256), jnp.float32),
            pltpu.VMEM((40, 256), jnp.float32),
            pltpu.VMEM((8, 40, 256), jnp.float32),
            pltpu.SemaphoreType.DMA((REDUCE_COPIES,)),
            pltpu.SemaphoreType.DMA((REDUCE_COPIES,)),
        ],
        compiler_params=pltpu.CompilerParams(
            collective_id=0, has_side_effects=True, vmem_limit_bytes=48 * 1024 * 1024
        ),
        name="reduce",
    )(both, out, cot, small)


def on_device(
    inputs,
    grad_blocks,
    block_device,
    block_sub,
    block_rows,
    seg_lengths,
    value_weight,
    gate_weight,
    out_weight,
    conv_kernel,
    norm_gain,
):
    frames_in = inputs[0]
    tok_count, width = frames_in.shape
    span = value_weight.shape[0]
    half = KERNEL // 2
    tm_count = lax.axis_size("tm")
    tm_index = lax.axis_index("tm")
    frame_total = tok_count * tm_count
    factor = 1.0 / math.sqrt(lax.axis_size("dp") * frame_total)
    blocks = grad_blocks[0]
    blk_count, row_share = (blocks.shape[0], blocks.shape[1])
    per_dev = tok_count // ROWS_BLK
    capacity = max(2, (blk_count + tm_count - 1) // tm_count + 1)
    devices = block_device[0, :, 0].reshape(tm_count, blk_count)
    subs = block_sub[0].reshape(tm_count, blk_count)
    counts = block_rows[0].reshape(tm_count, blk_count)
    own_counts = lax.dynamic_index_in_dim(counts, tm_index, 0, keepdims=False)
    own_device = lax.dynamic_index_in_dim(devices, tm_index, 0, keepdims=False)
    row_ids = lax.axis_index("tensor") * row_share + jnp.arange(row_share, dtype=jnp.int32)
    live_rows = (row_ids[None, :] < own_counts[:, None]).astype(jnp.bfloat16)
    flat_blocks = (blocks * live_rows[:, :, None]).reshape(blk_count, row_share * width)
    earlier = jnp.arange(blk_count)[:, None] > jnp.arange(blk_count)[None, :]
    same_dest = devices[:, :, None] == devices[:, None, :]
    ranks = jnp.sum((same_dest & earlier[None, :, :]).astype(jnp.int32), axis=2)
    own_rank = lax.dynamic_index_in_dim(ranks, tm_index, 0, keepdims=False)
    slot = own_device * capacity + own_rank
    placing = (jnp.arange(tm_count * capacity)[:, None] == slot[None, :]).astype(jnp.bfloat16)
    outgoing = jnp.dot(placing, flat_blocks, preferred_element_type=jnp.float32).astype(
        jnp.bfloat16
    )
    outgoing = outgoing.reshape(tm_count, capacity, row_share, width)
    incoming = lax.all_to_all(outgoing, "tm", split_axis=0, concat_axis=0, tiled=True)
    mine = (devices == tm_index).astype(jnp.float32)
    rank_hot = (ranks[:, :, None] == jnp.arange(capacity)[None, None, :]).astype(jnp.float32)
    sub_hot = (subs[:, :, None] == jnp.arange(per_dev)[None, None, :]).astype(jnp.float32)
    assign = jnp.einsum("sb,sbc,sbq->qsc", mine, rank_hot, sub_hot).astype(jnp.bfloat16)
    assign = assign.reshape(per_dev, tm_count * capacity)
    gathered = jnp.dot(
        assign,
        incoming.reshape(tm_count * capacity, row_share * width),
        preferred_element_type=jnp.float32,
    )
    out_cot = gathered.reshape(per_dev, row_share, width).astype(jnp.bfloat16)
    frames_f32 = frames_in.astype(jnp.float32)
    centered = frames_f32 - jnp.mean(frames_f32, axis=1, keepdims=True)
    inv_std = lax.rsqrt(jnp.mean(centered * centered, axis=1, keepdims=True) + epsilon)
    normed = centered * inv_std
    norm_out = (normed * norm_gain).astype(jnp.bfloat16)
    value_lin = contract_last(norm_out, value_weight)
    gate_lin = contract_last(norm_out, gate_weight)
    gate_sig = jax.nn.sigmoid(gate_lin)
    glu_out = (value_lin * gate_sig).astype(jnp.bfloat16)
    labels = segment_of(
        seg_lengths[0], tm_index * tok_count - half, tok_count + 2 * half, frame_total
    )
    centre = labels[half : half + tok_count]
    near_masks = [
        (labels[offset : offset + tok_count] == centre).astype(jnp.float32)[:, None]
        for offset in range(KERNEL)
    ]
    glu_wide = with_halo(glu_out, (("tm", 0),), half).astype(jnp.float32)
    kern_f32 = conv_kernel.astype(jnp.float32)
    conv_out = jnp.zeros((tok_count, span), jnp.float32)
    for offset in range(KERNEL):
        conv_out = (
            conv_out + kern_f32[offset] * glu_wide[offset : offset + tok_count] * near_masks[offset]
        )
    conv_sig = jax.nn.sigmoid(conv_out)
    swish_out = (conv_out * conv_sig).astype(jnp.bfloat16)
    full_cot = lax.all_gather(out_cot, "tensor", axis=1, tiled=True).reshape(tok_count, width)
    swish_cot = contract_last(full_cot, out_weight)
    conv_cot = swish_cot * conv_sig * (1.0 + conv_out * (1.0 - conv_sig))
    cot_wide = with_halo(conv_cot, (("tm", 0),), half)
    glu_cot = jnp.zeros((tok_count, span), jnp.float32)
    kern_rows = []
    for offset in range(KERNEL):
        kern_rows.append(
            jnp.sum(conv_cot * glu_wide[offset : offset + tok_count] * near_masks[offset], axis=0)
        )
        mirror = KERNEL - 1 - offset
        glu_cot = (
            glu_cot + kern_f32[offset] * cot_wide[mirror : mirror + tok_count] * near_masks[mirror]
        )
    value_cot = (glu_cot * gate_sig).astype(jnp.bfloat16)
    gate_cot = (glu_cot * value_lin * gate_sig * (1.0 - gate_sig)).astype(jnp.bfloat16)
    value_gate_cot = jnp.concatenate([value_cot, gate_cot], axis=1)
    over_frames = (((0,), (0,)), ((), ()))
    out_term = lax.dot_general(
        full_cot, swish_out, over_frames, preferred_element_type=jnp.float32
    ).astype(jnp.bfloat16)
    both_term = lax.dot_general(
        norm_out, value_gate_cot, over_frames, preferred_element_type=jnp.float32
    ).astype(jnp.bfloat16)
    norm_part = jnp.dot(
        value_gate_cot,
        jnp.concatenate([value_weight, gate_weight], axis=0),
        preferred_element_type=jnp.float32,
    )
    gain_part = jnp.sum(norm_part * normed, axis=0)
    small = jnp.concatenate(
        [
            jnp.pad(jnp.stack(kern_rows), ((0, 1), (0, 256 - span))),
            jnp.pad(gain_part.reshape(width // 256, 256), ((0, 2), (0, 0))),
        ],
        axis=0,
    )
    both_sum, out_sum, cot_sum, small_sum = reduce_call(
        both_term.reshape(4, 4, 96, 2 * span),
        out_term.reshape(4, 4, 96, span),
        norm_part.astype(jnp.bfloat16).reshape(4, 2, 128, width),
        small,
    )
    share = tok_count // lax.axis_size("tensor")
    start = lax.axis_index("tensor") * share
    input_f32 = norm_backward(
        lax.dynamic_slice_in_dim(full_cot, start, share, 0),
        cot_sum,
        lax.dynamic_slice_in_dim(normed, start, share, 0),
        lax.dynamic_slice_in_dim(inv_std, start, share, 0),
        norm_gain,
    )
    return (
        input_f32.astype(jnp.bfloat16)[None],
        both_sum[:, :span].T * factor,
        both_sum[:, span:].T * factor,
        out_sum.T * factor,
        small_sum[:KERNEL, :span] * factor,
        small_sum[32 : 32 + width // 256].reshape(width) * factor,
    )


def solution(mesh):
    in_specs = (
        P("dp", "tm", None),
        P("dp", "tm", "tensor", None),
        P("dp", None, None),
        P("dp", None),
        P("dp", None),
        P("dp", None),
        P("tensor", None),
        P("tensor", None),
        P("tensor", None),
        P(None, "tensor"),
        P(),
    )
    out_specs = (
        P("dp", ("tm", "tensor"), None),
        P("tensor", ("tm", "dp")),
        P("tensor", ("tm", "dp")),
        P("tensor", ("tm", "dp")),
        P(None, "tensor"),
        P(),
    )
    return jax.shard_map(
        on_device, mesh=mesh, in_specs=in_specs, out_specs=out_specs, check_vma=False
    )
```

```python
import math

import jax
import jax.numpy as jnp
from jax import lax
from jax.experimental import pallas as pl
from jax.experimental.pallas import tpu as pltpu
from jax.sharding import PartitionSpec as P

KERNEL = 31
ROWS_BLK = 128


epsilon = 1e-05


def contract_last(left, right):
    return lax.dot_general(
        left, right, (((1,), (1,)), ((), ())), preferred_element_type=jnp.float32
    )


def norm_backward(full_cot, norm_cot, normed, inv_std, norm_gain):
    scaled_cot = norm_cot * norm_gain
    return full_cot.astype(jnp.float32) + inv_std * (
        scaled_cot
        - jnp.mean(scaled_cot, axis=1, keepdims=True)
        - normed * jnp.mean(scaled_cot * normed, axis=1, keepdims=True)
    )


def places():
    tm, te, dp = (lax.axis_index("tm"), lax.axis_index("tensor"), lax.axis_index("dp"))
    return tm, te, dp


def y_peer(step):
    tm, te, dp = places()
    return {"tm": (tm // 4) * 4 + (tm + step) % 4, "tensor": te, "dp": dp}


def z_peer(step):
    tm, te, dp = places()
    there = ((tm // 4) * 2 + dp + step) % 8
    return {"tm": (there // 2) * 4 + tm % 4, "tensor": te, "dp": there % 2}


def t_peer(step):
    tm, te, dp = places()
    return {"tm": tm, "tensor": (te + step) % 8, "dp": dp}


def x_peer(step):
    tm, te, dp = places()
    return {"tm": tm, "tensor": (te + 2 * step) % 8, "dp": dp}


def sibling():
    tm, te, dp = places()
    return {"tm": tm, "tensor": (te // 2) * 2 + 1 - te % 2, "dp": dp}


class Copies:
    def __init__(self, send_sems, recv_sems):
        self.send_sems, self.recv_sems = send_sems, recv_sems
        self.made = []

    def send(self, src, dst, to):
        at = len(self.made)
        copy = pltpu.make_async_remote_copy(
            src_ref=src,
            dst_ref=dst,
            send_sem=self.send_sems.at[at],
            recv_sem=self.recv_sems.at[at],
            device_id=to,
            device_id_type=pl.DeviceIdType.MESH,
        )
        copy.start()
        self.made.append(copy)
        return copy

    def finish(self):
        for copy in self.made:
            copy.wait_send()


def meet(peers):
    barrier = pltpu.get_barrier_semaphore()
    for peer in peers:
        pl.semaphore_signal(
            barrier, inc=1, device_id=peer, device_id_type=pl.DeviceIdType.MESH
        )
    pl.semaphore_wait(barrier, len(peers))


def f32(value):
    return value.astype(jnp.float32)


REDUCE_COPIES = 1 + 6 + 12 + 14 + 7 + 3 + 7


def reduce_kernel(
    both_ref,
    out_ref,
    cot_ref,
    small_ref,
    both_sum,
    out_sum,
    cot_sum,
    small_sum,
    core_in,
    chip_sum,
    x_a,
    x_b,
    x_plus,
    x_minus,
    both_a,
    both_b,
    both_plus,
    both_minus,
    both_mid,
    both_z,
    out_a,
    out_b,
    out_plus,
    out_minus,
    out_mid,
    out_z,
    gain_in,
    small_mid,
    small_y,
    small_last,
    small_z,
    send_sems,
    recv_sems,
):
    tm, te, dp = places()
    y, z, x, core = (tm % 4, (tm // 4) * 2 + dp, te // 2, te % 2)
    meet(
        [t_peer(k) for k in range(1, 8)]
        + [y_peer(k) for k in range(1, 4)]
        + [z_peer(k) for k in range(1, 8)]
    )
    net = Copies(send_sems, recv_sems)
    lower, upper = (pl.ds(0, 2), pl.ds(2, 2))
    y_next, y_last, y_far = ((y + 1) % 4, (y + 3) % 4, (y + 2) % 4)
    x_next, x_last, x_far = ((x + 1) % 4, (x + 3) % 4, (x + 2) % 4)
    core_copy = net.send(cot_ref.at[:, 1 - core], core_in, sibling())
    first = []
    for ref, a, b in ((out_ref, out_a, out_b), (both_ref, both_a, both_b)):
        first.append(
            (
                net.send(ref.at[lower, y_far], a, y_peer(1)),
                net.send(ref.at[upper, y_far], b, y_peer(-1)),
            )
        )
    plain = []
    for ref, plus, minus in ((out_ref, out_plus, out_minus), (both_ref, both_plus, both_minus)):
        plain.append(
            (
                net.send(ref.at[upper, y_next], plus.at[upper], y_peer(1)),
                net.send(ref.at[lower, y_last], minus.at[lower], y_peer(-1)),
            )
        )
    gain_rows = pl.ds(32, 8)
    gain_in[te] = small_ref[gain_rows, :]
    gain_copies = [
        net.send(small_ref.at[gain_rows], gain_in.at[te], t_peer(k)) for k in range(1, 8)
    ]

    core_copy.wait_recv()

    def add_core(at):
        @pl.loop(0, 128, step=16)
        def _(row):
            rows = pl.ds(pl.multiple_of(row, 16), 16)
            chip_sum[at, rows] = (f32(cot_ref[at, core, rows]) + f32(core_in[at, rows])).astype(
                jnp.bfloat16
            )

    add_core(x_far)
    half_a, half_b = (pl.ds(0, 64), pl.ds(64, 64))
    x_first = (
        net.send(chip_sum.at[x_far, half_a], x_a, x_peer(1)),
        net.send(chip_sum.at[x_far, half_b], x_b, x_peer(-1)),
    )
    add_core(x_next)
    add_core(x_last)
    x_plain = (
        net.send(chip_sum.at[x_next, half_b], x_plus.at[half_b], x_peer(1)),
        net.send(chip_sum.at[x_last, half_a], x_minus.at[half_a], x_peer(-1)),
    )

    second = []
    for at, (ref, a, b, plus, minus) in enumerate(
        (
            (out_ref, out_a, out_b, out_plus, out_minus),
            (both_ref, both_a, both_b, both_plus, both_minus),
        )
    ):
        first[at][0].wait_recv()
        for i in range(2):
            a[i] = (f32(a[i]) + f32(ref[i, y_next])).astype(jnp.bfloat16)
        one = net.send(a, plus.at[lower], y_peer(1))
        first[at][1].wait_recv()
        for i in range(2):
            b[i] = (f32(b[i]) + f32(ref[i + 2, y_last])).astype(jnp.bfloat16)
        second.append((one, net.send(b, minus.at[upper], y_peer(-1))))

    x_first[0].wait_recv()

    def add_x(ref, at, start):
        @pl.loop(0, 64, step=16)
        def _(row):
            rows = pl.ds(pl.multiple_of(row, 16), 16)
            other = pl.ds(pl.multiple_of(row + start, 16), 16)
            ref[rows] = (f32(ref[rows]) + f32(chip_sum[at, other])).astype(jnp.bfloat16)

    add_x(x_a, x_next, 0)
    x_second = [net.send(x_a, x_plus.at[half_a], x_peer(1))]
    x_first[1].wait_recv()
    add_x(x_b, x_last, 64)
    x_second.append(net.send(x_b, x_minus.at[half_b], x_peer(-1)))

    for copy in gain_copies:
        copy.wait_recv()
    small_mid[pl.ds(0, 32), :] = small_ref[pl.ds(0, 32), :]
    total = gain_in[0]
    for at in range(1, 8):
        total = total + gain_in[at]
    small_mid[gain_rows, :] = total
    small_y[y] = small_mid[...]
    small_copies = [net.send(small_mid, small_y.at[y], y_peer(k)) for k in range(1, 4)]

    z_copies = []
    for at, (ref, plus, minus, mid, z_in) in enumerate(
        (
            (out_ref, out_plus, out_minus, out_mid, out_z),
            (both_ref, both_plus, both_minus, both_mid, both_z),
        )
    ):
        for copy in plain[at] + second[at]:
            copy.wait_recv()
        for i in range(4):
            total = (f32(ref[i, y]) + f32(plus[i]) + f32(minus[i])).astype(jnp.bfloat16)
            mid[2 * i] = total[:48]
            mid[2 * i + 1] = total[48:]
        z_in[z] = mid[z]
        z_copies.append(
            [net.send(mid.at[(z + k) % 8], z_in.at[z], z_peer(k)) for k in (4, 3, 5, 2, 6, 1, 7)]
        )

    for copy in small_copies:
        copy.wait_recv()
    total = small_y[0]
    for at in range(1, 4):
        total = total + small_y[at]
    small_last[...] = total
    small_z[z] = total
    last_copies = [net.send(small_last, small_z.at[z], z_peer(k)) for k in range(1, 8)]

    for copy in x_plain + tuple(x_second):
        copy.wait_recv()

    @pl.loop(0, 128, step=16)
    def _(row):
        rows = pl.ds(pl.multiple_of(row, 16), 16)
        cot_sum[rows] = (
            f32(cot_ref[x, core, rows])
            + f32(core_in[x, rows])
            + f32(x_plus[rows])
            + f32(x_minus[rows])
        )

    for copies, z_in, result in ((z_copies[0], out_z, out_sum), (z_copies[1], both_z, both_sum)):
        for copy in copies:
            copy.wait_recv()
        total = f32(z_in[0])
        for at in range(1, 8):
            total = total + f32(z_in[at])
        result[...] = total
    for copy in last_copies:
        copy.wait_recv()
    total = small_z[0]
    for at in range(1, 8):
        total = total + small_z[at]
    small_sum[...] = total
    net.finish()


def reduce_call(both, out, cot, small):
    span = out.shape[3]
    width = cot.shape[3]
    bf16 = jnp.bfloat16
    weights = []
    for lanes in (2 * span, span):
        weights += [
            pltpu.VMEM((2, 96, lanes), bf16),
            pltpu.VMEM((2, 96, lanes), bf16),
            pltpu.VMEM((4, 96, lanes), bf16),
            pltpu.VMEM((4, 96, lanes), bf16),
            pltpu.VMEM((8, 48, lanes), bf16),
            pltpu.VMEM((8, 48, lanes), bf16),
        ]
    return pl.pallas_call(
        reduce_kernel,
        out_shape=(
            jax.ShapeDtypeStruct((48, 2 * span), jnp.float32),
            jax.ShapeDtypeStruct((48, span), jnp.float32),
            jax.ShapeDtypeStruct((128, width), jnp.float32),
            jax.ShapeDtypeStruct((40, 256), jnp.float32),
        ),
        in_specs=[pl.BlockSpec(memory_space=pltpu.VMEM)] * 4,
        out_specs=[pl.BlockSpec(memory_space=pltpu.VMEM)] * 4,
        scratch_shapes=[
            pltpu.VMEM((4, 128, width), bf16),
            pltpu.VMEM((4, 128, width), bf16),
            pltpu.VMEM((64, width), bf16),
            pltpu.VMEM((64, width), bf16),
            pltpu.VMEM((128, width), bf16),
            pltpu.VMEM((128, width), bf16),
        ]
        + weights
        + [
            pltpu.VMEM((8, 8, 256), jnp.float32),
            pltpu.VMEM((40, 256), jnp.float32),
            pltpu.VMEM((4, 40, 256), jnp.float32),
            pltpu.VMEM((40, 256), jnp.float32),
            pltpu.VMEM((8, 40, 256), jnp.float32),
            pltpu.SemaphoreType.DMA((REDUCE_COPIES,)),
            pltpu.SemaphoreType.DMA((REDUCE_COPIES,)),
        ],
        compiler_params=pltpu.CompilerParams(
            collective_id=0, has_side_effects=True, vmem_limit_bytes=48 * 1024 * 1024
        ),
        name="reduce",
    )(both, out, cot, small)


CHUNKS = ((0, 512), (512, 512), (1024, 256), (1280, 256))
ROUTE_COPIES = 13 * len(CHUNKS) + 2
SLOTS = 320


def frame_peer(step):
    tm, te, dp = places()
    return {"tm": (tm + step) % 16, "tensor": te, "dp": dp}


def route_kernel(
    frames_ref,
    blocks_ref,
    slot_ref,
    dest_ref,
    value_ref,
    gate_ref,
    gain_ref,
    taps_ref,
    ahead_ref,
    behind_ref,
    full_ref,
    norm_ref,
    lin_ref,
    sig_ref,
    conv_ref,
    glu_0,
    glu_1,
    placing,
    summing,
    edge_out,
    edge_in,
    *rest,
):
    count = len(CHUNKS)
    y_out, y_in = (rest[:count], rest[count : 2 * count])
    z_out, z_in = (rest[2 * count : 3 * count], rest[3 * count : 4 * count])
    send_sems, recv_sems = rest[4 * count :]
    tm, te, dp = places()
    y, zh = (tm % 4, tm // 4)
    bf16 = jnp.bfloat16
    meet(
        [t_peer(k) for k in range(1, 8)]
        + [y_peer(k) for k in range(1, 4)]
        + [z_peer(k) for k in (2, 4, 6)]
        + [frame_peer(1), frame_peer(-1)]
    )
    net = Copies(send_sems, recv_sems)
    columns = [pl.ds(first, size) for first, size in CHUNKS]

    @pl.loop(0, 4)
    def _(k):
        first = ((y + k) % 4) * SLOTS

        @pl.loop(0, SLOTS, step=32)
        def _(row):
            ids = lax.broadcasted_iota(jnp.int32, (32, 1024), 0) + (first + row)
            placing[k, pl.ds(pl.multiple_of(row, 32), 32)] = jnp.where(
                ids == slot_ref[...], 1.0, 0.0
            ).astype(bf16)

    def place(c):
        @pl.loop(0, 4)
        def _(k):
            y_out[c][k] = jnp.dot(
                placing[k], blocks_ref[:, columns[c]], preferred_element_type=jnp.float32
            ).astype(bf16)

        copies = [
            net.send(y_out[c].at[k], y_in[c].at[y], y_peer(k)) for k in (2, 1, 3)
        ]
        y_in[c][y] = y_out[c][0]
        return copies

    def combine(c, copies):
        for copy in copies:
            copy.wait_recv()

        @pl.loop(0, 4)
        def _(k):
            rows = pl.ds(pl.multiple_of(((zh + k) % 4) * 128, 128), 128)
            total = jnp.zeros((128, CHUNKS[c][1]), jnp.float32)
            for at in range(4):
                total = total + jnp.dot(
                    summing[at, rows], y_in[c][at], preferred_element_type=jnp.float32
                )
            z_out[c][k] = total.astype(bf16)

        return [net.send(z_out[c].at[k], z_in[c].at[k - 1], z_peer(2 * k)) for k in (2, 1, 3)]

    def spread(c, copies):
        for copy in copies:
            copy.wait_recv()
        total = f32(z_out[c][0])
        for k in range(3):
            total = total + f32(z_in[c][k])
        total = total.astype(bf16)
        for block in range(8):
            full_ref[block, te, :, columns[c]] = total[16 * block : 16 * block + 16]
        own = full_ref.at[:, te, :, columns[c]]
        return [net.send(own, own, x_peer(k)) for k in (2, 1, 3)], [
            net.send(own, own, sibling())
        ]

    def relay(c, copies):
        for k, copy in zip((2, 1, 3), copies[0]):
            copy.wait_recv()
            there = full_ref.at[:, (te + 8 - 2 * k) % 8, :, columns[c]]
            copies[1].append(net.send(there, there, sibling()))
        return copies[1]

    @pl.loop(0, 4)
    def _(at):
        @pl.loop(0, 512, step=32)
        def _(row):
            ids = lax.broadcasted_iota(jnp.int32, (32, SLOTS), 0) + row
            summing[at, pl.ds(pl.multiple_of(row, 32), 32)] = jnp.where(
                ids == dest_ref[at], 1.0, 0.0
            ).astype(bf16)

    y_copies = [place(0), place(1)]

    @pl.loop(0, 1024, step=32)
    def _(row):
        rows = pl.ds(pl.multiple_of(row, 32), 32)
        cells = f32(frames_ref[rows])
        centered = cells - jnp.mean(cells, axis=1, keepdims=True)
        scale = lax.rsqrt(jnp.mean(centered * centered, axis=1, keepdims=True) + epsilon)
        norm_ref[rows] = ((centered * scale) * gain_ref[...]).astype(bf16)

    glu_1[...] = jnp.zeros(glu_1.shape, jnp.float32)

    @pl.loop(0, 1024, step=256)
    def _(row):
        rows = pl.ds(pl.multiple_of(row, 256), 256)
        wide = pl.ds(pl.multiple_of(row + 16, 16), 256)
        value_lin = contract_last(norm_ref[rows], value_ref[...])
        gate_sig = jax.nn.sigmoid(contract_last(norm_ref[rows], gate_ref[...]))
        glu = f32((value_lin * gate_sig).astype(bf16))
        lin_ref[rows] = value_lin
        sig_ref[rows] = gate_sig
        glu_0[wide] = glu[:, :128]
        glu_1[wide, :64] = glu[:, 128:]

    for at, first in ((0, 16), (1, 1024)):
        edge_out[at, :, :128] = glu_0[first : first + 16].astype(bf16)
        edge_out[at, :, 128:] = glu_1[first : first + 16].astype(bf16)
    edges = (
        net.send(edge_out.at[0], edge_in.at[1], frame_peer(-1)),
        net.send(edge_out.at[1], edge_in.at[0], frame_peer(1)),
    )

    z_copies = [combine(0, y_copies[0])]
    y_copies.append(place(2))

    for at, first in ((0, 0), (1, 1040)):
        edges[1 - at].wait_recv()
        glu_0[first : first + 16] = f32(edge_in[at, :, :128])
        glu_1[first : first + 16] = f32(edge_in[at, :, 128:])

    @pl.loop(0, 1024, step=32)
    def _(row):
        rows = pl.ds(pl.multiple_of(row, 32), 32)
        ahead, behind = (ahead_ref[rows], behind_ref[rows])
        zero = jnp.zeros((32, 128), jnp.float32)
        total_0, total_1 = (zero, zero)
        for k in range(KERNEL):
            off = k - KERNEL // 2
            near = ahead >= off if off > 0 else behind >= -off
            shifted = pl.ds(row + 16 + off, 32)
            total_0 = total_0 + taps_ref[k : k + 1, :128] * jnp.where(near, glu_0[shifted], 0.0)
            total_1 = total_1 + taps_ref[k : k + 1, 128:] * jnp.where(near, glu_1[shifted], 0.0)
        conv_ref[rows, :128] = total_0
        conv_ref[rows, 128:] = total_1

    z_copies.append(combine(1, y_copies[1]))
    y_copies.append(place(3))
    x_copies = [spread(0, z_copies[0])]
    z_copies.append(combine(2, y_copies[2]))
    x_copies.append(spread(1, z_copies[1]))
    last = relay(0, x_copies[0])
    z_copies.append(combine(3, y_copies[3]))
    x_copies.append(spread(2, z_copies[2]))
    last += relay(1, x_copies[1])
    x_copies.append(spread(3, z_copies[3]))
    last += relay(2, x_copies[2])
    last += relay(3, x_copies[3])
    for copy in last:
        copy.wait_recv()
    net.finish()


def route_call(frames, blocks, slots, dests, value_weight, gate_weight, gain, taps, ahead, behind):
    count, width = frames.shape
    span = value_weight.shape[0]
    bf16 = jnp.bfloat16
    return pl.pallas_call(
        route_kernel,
        out_shape=(
            jax.ShapeDtypeStruct((8, 8, 16, width), bf16),
            jax.ShapeDtypeStruct((count, width), bf16),
            jax.ShapeDtypeStruct((count, span), jnp.float32),
            jax.ShapeDtypeStruct((count, span), jnp.float32),
            jax.ShapeDtypeStruct((count, 256), jnp.float32),
            jax.ShapeDtypeStruct((count + 32, 128), jnp.float32),
            jax.ShapeDtypeStruct((count + 32, 128), jnp.float32),
        ),
        in_specs=[pl.BlockSpec(memory_space=pltpu.VMEM)] * 10,
        out_specs=[pl.BlockSpec(memory_space=pltpu.VMEM)] * 7,
        scratch_shapes=[
            pltpu.VMEM((4, SLOTS, 1024), bf16),
            pltpu.VMEM((4, 512, SLOTS), bf16),
            pltpu.VMEM((2, 16, 256), bf16),
            pltpu.VMEM((2, 16, 256), bf16),
        ]
        + [pltpu.VMEM((4, SLOTS, size), bf16) for _, size in CHUNKS] * 2
        + [pltpu.VMEM((4, 128, size), bf16) for _, size in CHUNKS]
        + [pltpu.VMEM((3, 128, size), bf16) for _, size in CHUNKS]
        + [
            pltpu.SemaphoreType.DMA((ROUTE_COPIES,)),
            pltpu.SemaphoreType.DMA((ROUTE_COPIES,)),
        ],
        compiler_params=pltpu.CompilerParams(
            collective_id=1, has_side_effects=True, vmem_limit_bytes=56 * 1024 * 1024
        ),
        name="route",
    )(frames, blocks, slots, dests, value_weight, gate_weight, gain, taps, ahead, behind)


def routing(block_device, block_sub, block_rows):
    tm, te, dp = places()
    devices = block_device[0, :, 0].reshape(16, 64)
    subs = block_sub[0].reshape(16, 64)
    counts = block_rows[0].reshape(16, 64)
    earlier = jnp.arange(64)[:, None] > jnp.arange(64)[None, :]

    def ranked(column):
        same = column[:, :, None] == column[:, None, :]
        return jnp.sum((same & earlier[None]).astype(jnp.int32), axis=2)

    own_y = lax.dynamic_slice_in_dim(devices, tm, 1, 0) % 4
    own_counts = lax.dynamic_slice_in_dim(counts, tm, 1, 0)[0]
    slot = (own_y * 20 + ranked(own_y))[0]
    rows = jnp.arange(16, dtype=jnp.int32)[None, :]
    live = te * 16 + rows < own_counts[:, None]
    slots = jnp.where(live, slot[:, None] * 16 + rows, -1).reshape(1, 1024)

    first = (tm // 4) * 4
    near = lax.dynamic_slice_in_dim(devices, first, 4, 0)
    near_sub = lax.dynamic_slice_in_dim(subs, first, 4, 0)
    near_y = near % 4
    rank = jnp.where(near_y == tm % 4, ranked(near_y), -1)
    block = (near // 4) * 8 + near_sub
    hot = rank[:, None, :] == jnp.arange(20, dtype=jnp.int32)[None, :, None]
    at = jnp.sum(jnp.where(hot, block[:, None, :] + 1, 0), axis=2)[:, :, None] - 1
    dests = jnp.where(at >= 0, at * 16 + rows[None], -1).reshape(4, 1, 320)
    return slots, dests


def segment_reach(lengths, first, count, total):
    position = first + jnp.arange(count, dtype=jnp.int32)[:, None]
    ends = jnp.cumsum(lengths)[None, :]
    end = jnp.min(jnp.where(ends > position, ends, total), axis=1)
    start = jnp.max(jnp.where(ends <= position, ends, 0), axis=1)
    position = position[:, 0]
    ahead = jnp.broadcast_to((end - 1 - position)[:, None], (count, 128))
    behind = jnp.broadcast_to((position - start)[:, None], (count, 128))
    return ahead, behind


def on_device(
    inputs,
    grad_blocks,
    block_device,
    block_sub,
    block_rows,
    seg_lengths,
    value_weight,
    gate_weight,
    out_weight,
    conv_kernel,
    norm_gain,
):
    frames_in = inputs[0]
    tok_count, width = frames_in.shape
    span = value_weight.shape[0]
    half = KERNEL // 2
    tm_count = lax.axis_size("tm")
    tm_index = lax.axis_index("tm")
    frame_total = tok_count * tm_count
    factor = 1.0 / math.sqrt(lax.axis_size("dp") * frame_total)
    slots, dests = routing(block_device, block_sub, block_rows)
    ahead, behind = segment_reach(seg_lengths[0], tm_index * tok_count, tok_count, frame_total)
    kern_f32 = conv_kernel.astype(jnp.float32)
    taps = jnp.pad(kern_f32, ((0, 1), (0, 256 - span)))
    full_cot, norm_out, value_lin, gate_sig, conv_out, glu_0, glu_1 = route_call(
        frames_in,
        grad_blocks[0].reshape(1024, width),
        slots,
        dests,
        value_weight,
        gate_weight,
        norm_gain[None],
        taps,
        ahead,
        behind,
    )
    full_cot = full_cot.reshape(tok_count, width)
    conv_out = conv_out[:, :span]
    glu_wide = jnp.concatenate([glu_0, glu_1[:, :64]], axis=1)[1:]
    frames_f32 = frames_in.astype(jnp.float32)
    centered = frames_f32 - jnp.mean(frames_f32, axis=1, keepdims=True)
    inv_std = lax.rsqrt(jnp.mean(centered * centered, axis=1, keepdims=True) + epsilon)
    normed = centered * inv_std
    near_masks = [
        ((ahead if k > half else behind)[:, :1] >= abs(k - half)).astype(jnp.float32)
        for k in range(KERNEL)
    ]
    conv_sig = jax.nn.sigmoid(conv_out)
    swish_out = (conv_out * conv_sig).astype(jnp.bfloat16)
    swish_cot = contract_last(full_cot, out_weight)
    conv_cot = swish_cot * conv_sig * (1.0 + conv_out * (1.0 - conv_sig))
    head = lax.ppermute(conv_cot[-15:], "tm", [(i, i + 1) for i in range(15)])
    tail = lax.ppermute(conv_cot[:15], "tm", [(i + 1, i) for i in range(15)])
    cot_wide = jnp.concatenate([head, conv_cot, tail], axis=0)
    glu_cot = jnp.zeros((tok_count, span), jnp.float32)
    kern_rows = []
    for offset in range(KERNEL):
        kern_rows.append(
            jnp.sum(conv_cot * glu_wide[offset : offset + tok_count] * near_masks[offset], axis=0)
        )
        mirror = KERNEL - 1 - offset
        glu_cot = (
            glu_cot + kern_f32[offset] * cot_wide[mirror : mirror + tok_count] * near_masks[mirror]
        )
    value_cot = (glu_cot * gate_sig).astype(jnp.bfloat16)
    gate_cot = (glu_cot * value_lin * gate_sig * (1.0 - gate_sig)).astype(jnp.bfloat16)
    value_gate_cot = jnp.concatenate([value_cot, gate_cot], axis=1)
    over_frames = (((0,), (0,)), ((), ()))
    out_term = lax.dot_general(
        full_cot, swish_out, over_frames, preferred_element_type=jnp.float32
    ).astype(jnp.bfloat16)
    both_term = lax.dot_general(
        norm_out, value_gate_cot, over_frames, preferred_element_type=jnp.float32
    ).astype(jnp.bfloat16)
    norm_part = jnp.dot(
        value_gate_cot,
        jnp.concatenate([value_weight, gate_weight], axis=0),
        preferred_element_type=jnp.float32,
    )
    gain_part = jnp.sum(norm_part * normed, axis=0)
    small = jnp.concatenate(
        [
            jnp.pad(jnp.stack(kern_rows), ((0, 1), (0, 256 - span))),
            jnp.pad(gain_part.reshape(width // 256, 256), ((0, 2), (0, 0))),
        ],
        axis=0,
    )
    both_sum, out_sum, cot_sum, small_sum = reduce_call(
        both_term.reshape(4, 4, 96, 2 * span),
        out_term.reshape(4, 4, 96, span),
        norm_part.astype(jnp.bfloat16).reshape(4, 2, 128, width),
        small,
    )
    share = tok_count // lax.axis_size("tensor")
    start = lax.axis_index("tensor") * share
    input_f32 = norm_backward(
        lax.dynamic_slice_in_dim(full_cot, start, share, 0),
        cot_sum,
        lax.dynamic_slice_in_dim(normed, start, share, 0),
        lax.dynamic_slice_in_dim(inv_std, start, share, 0),
        norm_gain,
    )
    return (
        input_f32.astype(jnp.bfloat16)[None],
        both_sum[:, :span].T * factor,
        both_sum[:, span:].T * factor,
        out_sum.T * factor,
        small_sum[:KERNEL, :span] * factor,
        small_sum[32 : 32 + width // 256].reshape(width) * factor,
    )


def solution(mesh):
    in_specs = (
        P("dp", "tm", None),
        P("dp", "tm", "tensor", None),
        P("dp", None, None),
        P("dp", None),
        P("dp", None),
        P("dp", None),
        P("tensor", None),
        P("tensor", None),
        P("tensor", None),
        P(None, "tensor"),
        P(),
    )
    out_specs = (
        P("dp", ("tm", "tensor"), None),
        P("tensor", ("tm", "dp")),
        P("tensor", ("tm", "dp")),
        P("tensor", ("tm", "dp")),
        P(None, "tensor"),
        P(),
    )
    return jax.shard_map(
        on_device, mesh=mesh, in_specs=in_specs, out_specs=out_specs, check_vma=False
    )
```

```python
import math

import jax
import jax.numpy as jnp
from jax import lax
from jax.experimental import pallas as pl
from jax.experimental.pallas import tpu as pltpu
from jax.sharding import PartitionSpec as P

KERNEL = 31


epsilon = 1e-05


def contract_last(left, right):
    return lax.dot_general(
        left, right, (((1,), (1,)), ((), ())), preferred_element_type=jnp.float32
    )


def places():
    tm, te, dp = (lax.axis_index("tm"), lax.axis_index("tensor"), lax.axis_index("dp"))
    return tm, te, dp


def y_peer(step):
    tm, te, dp = places()
    return {"tm": (tm // 4) * 4 + (tm + step) % 4, "tensor": te, "dp": dp}


def z_peer(step):
    tm, te, dp = places()
    there = ((tm // 4) * 2 + dp + step) % 8
    return {"tm": (there // 2) * 4 + tm % 4, "tensor": te, "dp": there % 2}


def t_peer(step):
    tm, te, dp = places()
    return {"tm": tm, "tensor": (te + step) % 8, "dp": dp}


def x_peer(step):
    tm, te, dp = places()
    return {"tm": tm, "tensor": (te + 2 * step) % 8, "dp": dp}


def sibling():
    tm, te, dp = places()
    return {"tm": tm, "tensor": (te // 2) * 2 + 1 - te % 2, "dp": dp}


class Copies:
    def __init__(self, send_sems, recv_sems):
        self.send_sems, self.recv_sems = send_sems, recv_sems
        self.made = []

    def send(self, src, dst, to):
        at = len(self.made)
        copy = pltpu.make_async_remote_copy(
            src_ref=src,
            dst_ref=dst,
            send_sem=self.send_sems.at[at],
            recv_sem=self.recv_sems.at[at],
            device_id=to,
            device_id_type=pl.DeviceIdType.MESH,
        )
        copy.start()
        self.made.append(copy)
        return copy

    def finish(self):
        for copy in self.made:
            copy.wait_send()


def meet(peers):
    barrier = pltpu.get_barrier_semaphore()
    for peer in peers:
        pl.semaphore_signal(
            barrier, inc=1, device_id=peer, device_id_type=pl.DeviceIdType.MESH
        )
    pl.semaphore_wait(barrier, len(peers))


def f32(value):
    return value.astype(jnp.float32)


def frame_peer(step):
    tm, te, dp = places()
    return {"tm": (tm + step) % 16, "tensor": te, "dp": dp}


CHUNKS = ((0, 512), (512, 512), (1024, 256), (1280, 256))
HALVES = ((0, 768), (768, 768))
SLOTS = 320
COPIES = 13 * len(CHUNKS) + 4 + 7 * len(HALVES) + 12 + 14 + 7 + 3 + 7


def joint_kernel(
    table_ref,
    lengths_ref,
    frames_hbm,
    blocks_hbm,
    value_hbm,
    gate_hbm,
    out_hbm,
    taps_ref,
    gain_ref,
    input_grad,
    value_grad,
    gate_grad,
    out_grad,
    kernel_grad,
    gain_grad,
    frames_ref,
    pair_ref,
    last_ref,
    taps,
    ahead_ref,
    behind_ref,
    norm_ref,
    lin_ref,
    sig_ref,
    conv_ref,
    glu_0,
    glu_1,
    full_ref,
    swish_ref,
    cot_ref,
    cot_0,
    cot_1,
    both_cot,
    tap_sums,
    gain_sums,
    summing,
    edge_out,
    edge_in,
    far_out,
    far_in,
    part_ref,
    core_in,
    chip_sum,
    x_a,
    x_b,
    x_plus,
    x_minus,
    both_ref,
    both_a,
    both_b,
    both_plus,
    both_minus,
    both_mid,
    both_z,
    out_ref,
    out_a,
    out_b,
    out_plus,
    out_minus,
    out_mid,
    out_z,
    small_ref,
    gain_in,
    small_mid,
    small_y,
    small_last,
    small_z,
    load_sems,
    send_sems,
    recv_sems,
    *rest,
):
    count = len(CHUNKS)
    y_out, y_in = (rest[:count], rest[count : 2 * count])
    z_out, z_in = (rest[2 * count : 3 * count], rest[3 * count : 4 * count])
    blocks = rest[4 * count :]
    tm, te, dp = places()
    y, zh, z = (tm % 4, tm // 4, (tm // 4) * 2 + dp)
    x, core = (te // 2, te % 2)
    bf16 = jnp.bfloat16
    factor = 1.0 / math.sqrt(32768.0)
    columns = [pl.ds(first, size) for first, size in CHUNKS]

    loads = []

    def load(src, dst):
        copy = pltpu.make_async_copy(src, dst, load_sems.at[len(loads)])
        copy.start()
        loads.append(copy)
        return copy

    block_loads = [load(blocks_hbm.at[:, :, columns[c]], blocks[c]) for c in range(count)]
    frames_load = load(frames_hbm, frames_ref)
    weight_loads = [
        load(value_hbm.at[pl.ds(0, 128)], pair_ref.at[pl.ds(0, 128)]),
        load(gate_hbm.at[pl.ds(0, 128)], pair_ref.at[pl.ds(128, 128)]),
        load(value_hbm.at[pl.ds(128, 64)], pair_ref.at[pl.ds(256, 64)]),
        load(gate_hbm.at[pl.ds(128, 64)], pair_ref.at[pl.ds(320, 64)]),
    ]
    out_load = load(out_hbm, last_ref.at[pl.ds(0, 192)])

    meet(
        [t_peer(k) for k in range(1, 8)]
        + [y_peer(k) for k in range(1, 4)]
        + [z_peer(k) for k in range(1, 8)]
        + [frame_peer(1), frame_peer(-1)]
    )
    net = Copies(send_sems, recv_sems)

    def place(c):
        block_loads[c].wait()
        copies = []
        for k in (2, 1, 3, 0):
            first = ((y + k) % 4) * 20
            target = y_in[c].at[y] if k == 0 else y_out[c].at[k - 1]

            @pl.loop(0, 20)
            def _(slot):
                source = table_ref[first + slot]
                live = table_ref[80 + first + slot]
                rows = blocks[c][source]
                ids = lax.broadcasted_iota(jnp.int32, rows.shape, 0)
                target[pl.ds(pl.multiple_of(slot * 16, 16), 16)] = jnp.where(
                    ids < live, f32(rows), 0.0
                ).astype(bf16)

            if k:
                copies.append(net.send(target, y_in[c].at[y], y_peer(k)))
        return copies

    def combine(c, copies):
        for copy in copies:
            copy.wait_recv()
        width = CHUNKS[c][1]

        @pl.loop(0, width, step=256)
        def _(col):
            cols = pl.ds(pl.multiple_of(col, 256), 256)
            total = jnp.dot(
                summing[...],
                y_in[c][:, :, cols].reshape(4 * SLOTS, 256),
                preferred_element_type=jnp.float32,
            ).astype(bf16)
            for at in range(4):
                z_out[c][at, :, cols] = total[128 * at : 128 * at + 128]

        return [
            net.send(z_out[c].at[(zh + k) % 4], z_in[c].at[k - 1], z_peer(2 * k))
            for k in (2, 1, 3)
        ]

    def spread(c, copies):
        for copy in copies:
            copy.wait_recv()
        total = f32(z_out[c][zh])
        for k in range(3):
            total = total + f32(z_in[c][k])
        total = total.astype(bf16)
        for block in range(8):
            full_ref[block, te, :, columns[c]] = total[16 * block : 16 * block + 16]
        own = full_ref.at[:, te, :, columns[c]]
        return [net.send(own, own, x_peer(k)) for k in (2, 1, 3)], [
            net.send(own, own, sibling())
        ]

    def relay(c, copies):
        for k, copy in zip((2, 1, 3), copies[0]):
            copy.wait_recv()
            there = full_ref.at[:, (te + 8 - 2 * k) % 8, :, columns[c]]
            copies[1].append(net.send(there, there, sibling()))
        return copies[1]

    def project(c, copies):
        for copy in copies:
            copy.wait_recv()

        @pl.loop(0, 8, step=4)
        def _(block):
            rows = pl.ds(pl.multiple_of(block * 128, 512), 512)
            term = contract_last(
                full_ref[pl.ds(block, 4), :, :, columns[c]].reshape(512, CHUNKS[c][1]),
                last_ref[:, columns[c]],
            )
            if c == 0:
                cot_ref[rows] = term
            else:
                cot_ref[rows] += term

    y_copies = [place(0), place(1)]

    @pl.loop(0, 10)
    def _(group):
        tiles = []
        for k in range(8):
            at = table_ref[160 + group * 8 + k] * 16
            gap = lax.broadcasted_iota(jnp.int32, (16, 512), 1) - lax.broadcasted_iota(
                jnp.int32, (16, 512), 0
            )
            tiles.append(jnp.where(gap == at, 1.0, 0.0))
        cols = pl.ds(pl.multiple_of(group * 128, 128), 128)
        summing[:, cols] = jnp.concatenate(tiles, axis=0).T.astype(bf16)

    frames_load.wait()

    @pl.loop(0, 1024, step=32)
    def _(row):
        rows = pl.ds(pl.multiple_of(row, 32), 32)
        cells = f32(frames_ref[rows])
        centered = cells - jnp.mean(cells, axis=1, keepdims=True)
        scale = lax.rsqrt(jnp.mean(centered * centered, axis=1, keepdims=True) + epsilon)
        norm_ref[rows] = ((centered * scale) * gain_ref[...]).astype(bf16)

    for copy in weight_loads:
        copy.wait()

    @pl.loop(0, 1024, step=256)
    def _(row):
        rows = pl.ds(pl.multiple_of(row, 256), 256)
        wide = pl.ds(pl.multiple_of(row + 16, 16), 256)
        lin = contract_last(norm_ref[rows], pair_ref[...])
        value_0, gate_0, value_1 = (lin[:, :128], lin[:, 128:256], lin[:, 256:])
        sig_0 = jax.nn.sigmoid(gate_0)
        sig_1 = jax.nn.sigmoid(pltpu.roll(value_1, 64, 1))
        lin_ref[rows, :128] = value_0
        lin_ref[rows, 128:] = value_1
        sig_ref[rows, :128] = sig_0
        sig_ref[rows, 128:] = sig_1
        glu_0[wide] = f32((value_0 * sig_0).astype(bf16))
        glu_1[wide] = f32((value_1 * sig_1).astype(bf16))

    for at, first in ((0, 16), (1, 1024)):
        edge_out[at, :, :128] = glu_0[first : first + 16].astype(bf16)
        edge_out[at, :, 128:] = glu_1[first : first + 16].astype(bf16)
    edges = (
        net.send(edge_out.at[0], edge_in.at[1], frame_peer(-1)),
        net.send(edge_out.at[1], edge_in.at[0], frame_peer(1)),
    )

    z_copies = [combine(0, y_copies[0])]
    y_copies.append(place(2))

    taps[...] = jnp.zeros(taps.shape, jnp.float32)
    taps[:KERNEL, :192] = f32(taps_ref[...])
    last_ref[192:] = jnp.zeros((64, 1536), bf16)
    tap_sums[...] = jnp.zeros(tap_sums.shape, jnp.float32)
    ends = [lengths_ref[0, 0]]
    for at in range(1, 22):
        ends.append(ends[-1] + lengths_ref[0, at])

    @pl.loop(0, 1024, step=64)
    def _(row):
        rows = pl.ds(pl.multiple_of(row, 64), 64)
        at = lax.broadcasted_iota(jnp.int32, (64, 128), 0) + (tm * 1024 + row)
        end, start = (jnp.full((64, 128), 16384, jnp.int32), jnp.zeros((64, 128), jnp.int32))
        for bound in ends:
            past = at >= bound
            start = jnp.where(past, bound, start)
            end = jnp.where(past, end, jnp.minimum(end, bound))
        ahead_ref[rows] = end - 1 - at
        behind_ref[rows] = at - start

    for at, first in ((0, 0), (1, 1040)):
        edges[1 - at].wait_recv()
        glu_0[first : first + 16] = f32(edge_in[at, :, :128])
        glu_1[first : first + 16] = f32(edge_in[at, :, 128:])

    def nearby(ahead, behind, off):
        return ahead >= off if off > 0 else behind >= -off

    @pl.loop(0, 1024, step=32)
    def _(row):
        rows = pl.ds(pl.multiple_of(row, 32), 32)
        ahead, behind = (ahead_ref[rows], behind_ref[rows])
        total_0 = jnp.zeros((32, 128), jnp.float32)
        total_1 = jnp.zeros((32, 128), jnp.float32)
        for k in range(KERNEL):
            off = k - KERNEL // 2
            near = nearby(ahead, behind, off)
            shifted = pl.ds(row + 16 + off, 32)
            total_0 = total_0 + taps[k : k + 1, :128] * jnp.where(near, glu_0[shifted], 0.0)
            total_1 = total_1 + taps[k : k + 1, 128:] * jnp.where(near, glu_1[shifted], 0.0)
        conv_ref[rows, :128] = total_0
        conv_ref[rows, 128:] = total_1
        swish_ref[rows, :128] = (total_0 * jax.nn.sigmoid(total_0)).astype(bf16)
        swish_ref[rows, 128:] = (total_1 * jax.nn.sigmoid(total_1)).astype(bf16)

    out_load.wait()
    z_copies.append(combine(1, y_copies[1]))
    y_copies.append(place(3))
    x_copies = [spread(0, z_copies[0])]
    z_copies.append(combine(2, y_copies[2]))
    x_copies.append(spread(1, z_copies[1]))
    last = [relay(0, x_copies[0])]
    project(0, last[0])
    z_copies.append(combine(3, y_copies[3]))
    x_copies.append(spread(2, z_copies[2]))
    last.append(relay(1, x_copies[1]))
    project(1, last[1])
    x_copies.append(spread(3, z_copies[3]))
    last.append(relay(2, x_copies[2]))
    project(2, last[2])
    last.append(relay(3, x_copies[3]))
    project(3, last[3])

    @pl.loop(0, 1024, step=64)
    def _(row):
        rows = pl.ds(pl.multiple_of(row, 64), 64)
        wide = pl.ds(pl.multiple_of(row + 16, 16), 64)
        conv = conv_ref[rows]
        sig = jax.nn.sigmoid(conv)
        cot = cot_ref[rows] * sig * (1.0 + conv * (1.0 - sig))
        cot_0[wide] = cot[:, :128]
        cot_1[wide] = cot[:, 128:]

    for at, first in ((0, 16), (1, 1024)):
        far_out[at, :, :128] = cot_0[first : first + 16]
        far_out[at, :, 128:] = cot_1[first : first + 16]
    edges = (
        net.send(far_out.at[0], far_in.at[1], frame_peer(-1)),
        net.send(far_out.at[1], far_in.at[0], frame_peer(1)),
    )

    over_frames = (((0,), (0,)), ((), ()))
    lower, upper = (pl.ds(0, 2), pl.ds(2, 2))
    y_next, y_last, y_far = ((y + 1) % 4, (y + 3) % 4, (y + 2) % 4)
    x_next, x_last, x_far = ((x + 1) % 4, (x + 3) % 4, (x + 2) % 4)

    def begin_y(ref, a, b, plus, minus):
        first = (
            net.send(ref.at[lower, y_far], a, y_peer(1)),
            net.send(ref.at[upper, y_far], b, y_peer(-1)),
        )
        plain = (
            net.send(ref.at[upper, y_next], plus.at[upper], y_peer(1)),
            net.send(ref.at[lower, y_last], minus.at[lower], y_peer(-1)),
        )
        return first, plain

    def pass_y(begun, ref, a, b, plus, minus):
        first, plain = begun
        first[0].wait_recv()
        for i in range(2):
            a[i] = (f32(a[i]) + f32(ref[i, y_next])).astype(bf16)
        one = net.send(a, plus.at[lower], y_peer(1))
        first[1].wait_recv()
        for i in range(2):
            b[i] = (f32(b[i]) + f32(ref[i + 2, y_last])).astype(bf16)
        return plain + (one, net.send(b, minus.at[upper], y_peer(-1)))

    def begin_z(passed, ref, plus, minus, mid, z_in_ref):
        for copy in passed:
            copy.wait_recv()
        for i in range(4):
            total = (f32(ref[i, y]) + f32(plus[i]) + f32(minus[i])).astype(bf16)
            mid[2 * i] = total[:48]
            mid[2 * i + 1] = total[48:]
        z_in_ref[z] = mid[z]
        return [
            net.send(mid.at[(z + k) % 8], z_in_ref.at[z], z_peer(k)) for k in (4, 3, 5, 2, 6, 1, 7)
        ]

    def end_z(copies, z_in_ref):
        for copy in copies:
            copy.wait_recv()
        total = f32(z_in_ref[0])
        for at in range(1, 8):
            total = total + f32(z_in_ref[at])
        return total * factor

    @pl.loop(0, 4)
    def _(at):
        cols = pl.ds(pl.multiple_of(at * 384, 128), 384)
        term = lax.dot_general(
            full_ref[:, :, :, cols].reshape(1024, 384),
            swish_ref[...],
            over_frames,
            preferred_element_type=jnp.float32,
        ).astype(bf16)
        for k in range(4):
            out_ref[at, k] = term[96 * k : 96 * k + 96]

    out_set = (out_a, out_b, out_plus, out_minus)
    both_set = (both_a, both_b, both_plus, both_minus)
    out_begun = begin_y(out_ref, *out_set)

    for at, first in ((0, 0), (1, 1040)):
        edges[1 - at].wait_recv()
        cot_0[first : first + 16] = far_in[at, :, :128]
        cot_1[first : first + 16] = far_in[at, :, 128:]

    def back(row):
        rows = pl.ds(pl.multiple_of(row, 32), 32)
        wide = pl.ds(pl.multiple_of(row + 16, 16), 32)
        ahead, behind = (ahead_ref[rows], behind_ref[rows])
        here_0, here_1 = (cot_0[wide], cot_1[wide])
        total_0 = jnp.zeros((32, 128), jnp.float32)
        total_1 = jnp.zeros((32, 128), jnp.float32)
        for k in range(KERNEL):
            off = k - KERNEL // 2
            near = nearby(ahead, behind, off)
            shifted = pl.ds(row + 16 + off, 32)
            m = KERNEL - 1 - k
            total_0 = total_0 + taps[m : m + 1, :128] * jnp.where(near, cot_0[shifted], 0.0)
            total_1 = total_1 + taps[m : m + 1, 128:] * jnp.where(near, cot_1[shifted], 0.0)
            term_0 = here_0 * jnp.where(near, glu_0[shifted], 0.0)
            term_1 = here_1 * jnp.where(near, glu_1[shifted], 0.0)
            tap_sums[k, :, :128] += jnp.sum(term_0.reshape(4, 8, 128), axis=0)
            tap_sums[k, :, 128:] += jnp.sum(term_1.reshape(4, 8, 128), axis=0)
        value_0, value_1 = (lin_ref[rows, :128], lin_ref[rows, 128:])
        sig_0, sig_1 = (sig_ref[rows, :128], sig_ref[rows, 128:])
        both_cot[rows, :128] = (total_0 * sig_0).astype(bf16)
        both_cot[rows, 128:256] = (total_0 * value_0 * sig_0 * (1.0 - sig_0)).astype(bf16)
        gate_1 = total_1 * value_1 * sig_1 * (1.0 - sig_1)
        both_cot[rows, 256:] = (total_1 * sig_1 + pltpu.roll(gate_1, 64, 1)).astype(bf16)

    @pl.loop(0, 512, step=32)
    def _(row):
        back(row)

    out_passed = pass_y(out_begun, out_ref, *out_set)

    @pl.loop(512, 1024, step=32)
    def _(row):
        back(row)

    gain_sums[...] = jnp.zeros(gain_sums.shape, jnp.float32)
    core_copies = []
    for at, (first, size) in enumerate(HALVES):
        @pl.loop(first, first + size, step=256)
        def _(col):
            cols = pl.ds(pl.multiple_of(col, 256), 256)
            for row in (0, 512):
                part = jnp.dot(
                    both_cot[row : row + 512],
                    pair_ref[:, cols],
                    preferred_element_type=jnp.float32,
                )
                gain_sums[:, cols] += jnp.sum(
                    (part * f32(norm_ref[row : row + 512, cols])).reshape(64, 8, 256), axis=0
                )
                part = part.astype(bf16)
                for k in range(4):
                    part_ref[row // 256 + k // 2, k % 2, :, cols] = part[128 * k : 128 * k + 128]

        cols = pl.ds(first, size)
        core_copies.append(
            net.send(part_ref.at[:, 1 - core, :, cols], core_in.at[:, :, cols], sibling())
        )

    @pl.loop(0, 4)
    def _(at):
        cols = pl.ds(pl.multiple_of(at * 384, 128), 384)
        term = lax.dot_general(
            norm_ref[:, cols], both_cot[...], over_frames, preferred_element_type=jnp.float32
        ).astype(bf16)
        for k in range(4):
            both_ref[at, k] = term[96 * k : 96 * k + 96]

    both_begun = begin_y(both_ref, *both_set)

    gain_rows = pl.ds(32, 8)
    small_ref[...] = jnp.zeros(small_ref.shape, jnp.float32)
    for k in range(KERNEL):
        small_ref[k : k + 1] = jnp.sum(tap_sums[k], axis=0, keepdims=True)
    gain_part = jnp.sum(gain_sums[...], axis=0, keepdims=True) / gain_ref[...]
    for k in range(6):
        small_ref[32 + k : 33 + k] = gain_part[:, 256 * k : 256 * k + 256]
    gain_in[te] = small_ref[gain_rows, :]
    gain_copies = [
        net.send(small_ref.at[gain_rows], gain_in.at[te], t_peer(k)) for k in range(1, 8)
    ]

    half_a, half_b = (pl.ds(0, 64), pl.ds(64, 64))
    x_begun = []
    for at, (first, size) in enumerate(HALVES):
        core_copies[at].wait_recv()
        cols = pl.ds(first, size)

        def add_core(to):
            @pl.loop(0, 128, step=32)
            def _(row):
                rows = pl.ds(pl.multiple_of(row, 32), 32)
                chip_sum[to, rows, cols] = (
                    f32(part_ref[to, core, rows, cols]) + f32(core_in[to, rows, cols])
                ).astype(bf16)

        add_core(x_far)
        begun = (
            net.send(chip_sum.at[x_far, half_a, cols], x_a.at[:, cols], x_peer(1)),
            net.send(chip_sum.at[x_far, half_b, cols], x_b.at[:, cols], x_peer(-1)),
        )
        add_core(x_next)
        add_core(x_last)
        plain = (
            net.send(chip_sum.at[x_next, half_b, cols], x_plus.at[half_b, cols], x_peer(1)),
            net.send(chip_sum.at[x_last, half_a, cols], x_minus.at[half_a, cols], x_peer(-1)),
        )
        x_begun.append((begun, plain))

    out_z_copies = begin_z(out_passed, out_ref, out_plus, out_minus, out_mid, out_z)
    both_passed = pass_y(both_begun, both_ref, *both_set)

    x_passed = []
    for at, (first, size) in enumerate(HALVES):
        begun, plain = x_begun[at]
        cols = pl.ds(first, size)

        def add_x(ref, to, start):
            @pl.loop(0, 64, step=32)
            def _(row):
                rows = pl.ds(pl.multiple_of(row, 32), 32)
                other = pl.ds(pl.multiple_of(row + start, 32), 32)
                ref[rows, cols] = (f32(ref[rows, cols]) + f32(chip_sum[to, other, cols])).astype(
                    bf16
                )

        begun[0].wait_recv()
        add_x(x_a, x_next, 0)
        one = net.send(x_a.at[:, cols], x_plus.at[half_a, cols], x_peer(1))
        begun[1].wait_recv()
        add_x(x_b, x_last, 64)
        x_passed.append(
            plain + (one, net.send(x_b.at[:, cols], x_minus.at[half_b, cols], x_peer(-1)))
        )

    for copy in gain_copies:
        copy.wait_recv()
    small_mid[pl.ds(0, 32), :] = small_ref[pl.ds(0, 32), :]
    total = gain_in[0]
    for at in range(1, 8):
        total = total + gain_in[at]
    small_mid[gain_rows, :] = total
    small_y[y] = small_mid[...]
    small_copies = [net.send(small_mid, small_y.at[y], y_peer(k)) for k in range(1, 4)]

    both_z_copies = begin_z(both_passed, both_ref, both_plus, both_minus, both_mid, both_z)

    for copy in small_copies:
        copy.wait_recv()
    total = small_y[0]
    for at in range(1, 4):
        total = total + small_y[at]
    small_last[...] = total
    small_z[z] = total
    last_copies = [net.send(small_last, small_z.at[z], z_peer(k)) for k in range(1, 8)]

    out_grad[...] = end_z(out_z_copies, out_z).T[:192]

    for copies in x_passed:
        for copy in copies:
            copy.wait_recv()

    @pl.loop(0, 8)
    def _(block):
        rows = pl.ds(pl.multiple_of(block * 16, 16), 16)
        summed = (
            f32(part_ref[x, core, rows])
            + f32(core_in[x, rows])
            + f32(x_plus[rows])
            + f32(x_minus[rows])
        )
        cells = f32(frames_ref[pl.ds(pl.multiple_of(te * 128 + block * 16, 16), 16)])
        centered = cells - jnp.mean(cells, axis=1, keepdims=True)
        inv_std = lax.rsqrt(jnp.mean(centered * centered, axis=1, keepdims=True) + epsilon)
        normed = centered * inv_std
        scaled = summed * gain_ref[...]
        input_grad[rows] = (
            f32(full_ref[te, block])
            + inv_std
            * (
                scaled
                - jnp.mean(scaled, axis=1, keepdims=True)
                - normed * jnp.mean(scaled * normed, axis=1, keepdims=True)
            )
        ).astype(bf16)

    both_sum = end_z(both_z_copies, both_z)
    tail = both_sum[:, 256:].T
    value_grad[:128] = both_sum[:, :128].T
    gate_grad[:128] = both_sum[:, 128:256].T
    value_grad[128:] = tail[:64]
    gate_grad[128:] = tail[64:]

    for copy in last_copies:
        copy.wait_recv()
    total = small_z[0]
    for at in range(1, 8):
        total = total + small_z[at]
    total = total * factor
    kernel_grad[...] = total[:KERNEL, :192]
    for k in range(6):
        gain_grad[:, 256 * k : 256 * k + 256] = total[32 + k : 33 + k]
    net.finish()


def joint_call(table, lengths, frames, blocks, value_weight, gate_weight, out_weight, taps, gain):
    count, width = frames.shape
    span = value_weight.shape[0]
    bf16, single = (jnp.bfloat16, jnp.float32)
    vmem = pl.BlockSpec(memory_space=pltpu.VMEM)
    smem = pl.BlockSpec(memory_space=pltpu.SMEM)
    where = pl.BlockSpec(memory_space=pl.ANY)

    def weight_scratch(lanes):
        return [
            pltpu.VMEM((4, 4, 96, lanes), bf16),
            pltpu.VMEM((2, 96, lanes), bf16),
            pltpu.VMEM((2, 96, lanes), bf16),
            pltpu.VMEM((4, 96, lanes), bf16),
            pltpu.VMEM((4, 96, lanes), bf16),
            pltpu.VMEM((8, 48, lanes), bf16),
            pltpu.VMEM((8, 48, lanes), bf16),
        ]

    return pl.pallas_call(
        joint_kernel,
        out_shape=(
            jax.ShapeDtypeStruct((128, width), bf16),
            jax.ShapeDtypeStruct((span, 48), single),
            jax.ShapeDtypeStruct((span, 48), single),
            jax.ShapeDtypeStruct((span, 48), single),
            jax.ShapeDtypeStruct((KERNEL, span), single),
            jax.ShapeDtypeStruct((1, width), single),
        ),
        in_specs=[smem, smem] + [where] * 5 + [vmem] * 2,
        out_specs=[vmem] * 6,
        scratch_shapes=[
            pltpu.VMEM((count, width), bf16),
            pltpu.VMEM((2 * span, width), bf16),
            pltpu.VMEM((256, width), bf16),
            pltpu.VMEM((32, 256), single),
            pltpu.VMEM((count, 128), jnp.int32),
            pltpu.VMEM((count, 128), jnp.int32),
            pltpu.VMEM((count, width), bf16),
            pltpu.VMEM((count, 256), single),
            pltpu.VMEM((count, 256), single),
            pltpu.VMEM((count, 256), single),
            pltpu.VMEM((count + 32, 128), single),
            pltpu.VMEM((count + 32, 128), single),
            pltpu.VMEM((8, 8, 16, width), bf16),
            pltpu.VMEM((count, 256), bf16),
            pltpu.VMEM((count, 256), single),
            pltpu.VMEM((count + 32, 128), single),
            pltpu.VMEM((count + 32, 128), single),
            pltpu.VMEM((count, 2 * span), bf16),
            pltpu.VMEM((KERNEL, 8, 256), single),
            pltpu.VMEM((8, width), single),
            pltpu.VMEM((512, 4 * SLOTS), bf16),
            pltpu.VMEM((2, 16, 256), bf16),
            pltpu.VMEM((2, 16, 256), bf16),
            pltpu.VMEM((2, 16, 256), single),
            pltpu.VMEM((2, 16, 256), single),
            pltpu.VMEM((4, 2, 128, width), bf16),
            pltpu.VMEM((4, 128, width), bf16),
            pltpu.VMEM((4, 128, width), bf16),
            pltpu.VMEM((64, width), bf16),
            pltpu.VMEM((64, width), bf16),
            pltpu.VMEM((128, width), bf16),
            pltpu.VMEM((128, width), bf16),
        ]
        + weight_scratch(2 * span)
        + weight_scratch(256)
        + [
            pltpu.VMEM((40, 256), single),
            pltpu.VMEM((8, 8, 256), single),
            pltpu.VMEM((40, 256), single),
            pltpu.VMEM((4, 40, 256), single),
            pltpu.VMEM((40, 256), single),
            pltpu.VMEM((8, 40, 256), single),
            pltpu.SemaphoreType.DMA((len(CHUNKS) + 6,)),
            pltpu.SemaphoreType.DMA((COPIES,)),
            pltpu.SemaphoreType.DMA((COPIES,)),
        ]
        + [pltpu.VMEM((3, SLOTS, size), bf16) for _, size in CHUNKS]
        + [pltpu.VMEM((4, SLOTS, size), bf16) for _, size in CHUNKS]
        + [pltpu.VMEM((4, 128, size), bf16) for _, size in CHUNKS]
        + [pltpu.VMEM((3, 128, size), bf16) for _, size in CHUNKS]
        + [pltpu.VMEM((64, 16, size), bf16) for _, size in CHUNKS],
        compiler_params=pltpu.CompilerParams(
            collective_id=0, has_side_effects=True, vmem_limit_bytes=60 * 1024 * 1024
        ),
        name="joint",
    )(table, lengths, frames, blocks, value_weight, gate_weight, out_weight, taps, gain)


def routing(block_device, block_sub, block_rows):
    tm, te, dp = places()
    first = (tm // 4) * 4
    devices = lax.dynamic_slice_in_dim(block_device.reshape(16, 64), first, 4, 0)
    subs = lax.dynamic_slice_in_dim(block_sub.reshape(16, 64), first, 4, 0)
    counts = lax.dynamic_slice_in_dim(block_rows.reshape(16, 64), tm, 1, 0)
    earlier = jnp.arange(64)[:, None] > jnp.arange(64)[None, :]
    column = devices % 4
    same = (column[:, :, None] == column[:, None, :]) & earlier[None]
    rank = jnp.sum(same.astype(jnp.int32), axis=2)
    slot = column * 20 + rank
    own = lax.dynamic_slice_in_dim(slot, tm % 4, 1, 0)
    own_hot = own == jnp.arange(80, dtype=jnp.int32)[:, None]
    source = jnp.sum(jnp.where(own_hot, jnp.arange(64, dtype=jnp.int32)[None], 0), axis=1)
    live = jnp.sum(jnp.where(own_hot, jnp.clip(counts - te * 16, 0, 16), 0), axis=1)
    place = (tm % 4) * 20 + jnp.arange(20, dtype=jnp.int32)
    hot = slot[:, None, :] == place[None, :, None]
    block = (devices // 4) * 8 + subs
    dest = jnp.sum(jnp.where(hot, block[:, None, :] + 1, 0), axis=2).reshape(80) - 1
    return jnp.concatenate([source, live, jnp.where(dest < 0, 64, dest)])


def on_device(
    inputs,
    grad_blocks,
    block_device,
    block_sub,
    block_rows,
    seg_lengths,
    value_weight,
    gate_weight,
    out_weight,
    conv_kernel,
    norm_gain,
):
    width = inputs.shape[2]
    input_grad, value_grad, gate_grad, out_grad, kernel_grad, gain_grad = joint_call(
        routing(block_device, block_sub, block_rows),
        seg_lengths,
        inputs[0],
        grad_blocks[0],
        value_weight,
        gate_weight,
        out_weight,
        conv_kernel,
        norm_gain[None],
    )
    return (
        input_grad[None],
        value_grad,
        gate_grad,
        out_grad,
        kernel_grad,
        gain_grad.reshape(width),
    )


def solution(mesh):
    in_specs = (
        P("dp", "tm", None),
        P("dp", "tm", "tensor", None),
        P("dp", None, None),
        P("dp", None),
        P("dp", None),
        P("dp", None),
        P("tensor", None),
        P("tensor", None),
        P("tensor", None),
        P(None, "tensor"),
        P(),
    )
    out_specs = (
        P("dp", ("tm", "tensor"), None),
        P("tensor", ("tm", "dp")),
        P("tensor", ("tm", "dp")),
        P("tensor", ("tm", "dp")),
        P(None, "tensor"),
        P(),
    )
    return jax.shard_map(
        on_device, mesh=mesh, in_specs=in_specs, out_specs=out_specs, check_vma=False
    )
```

```python
import math

import jax
import jax.numpy as jnp
from jax import lax
from jax.experimental import pallas as pl
from jax.experimental.pallas import tpu as pltpu
from jax.sharding import PartitionSpec as P

KERNEL = 31


epsilon = 1e-05


def contract_last(left, right):
    return lax.dot_general(
        left, right, (((1,), (1,)), ((), ())), preferred_element_type=jnp.float32
    )


def places():
    tm, te, dp = (lax.axis_index("tm"), lax.axis_index("tensor"), lax.axis_index("dp"))
    return tm, te, dp


def y_peer(step):
    tm, te, dp = places()
    return {"tm": (tm // 4) * 4 + (tm + step) % 4, "tensor": te, "dp": dp}


def z_peer(step):
    tm, te, dp = places()
    there = ((tm // 4) * 2 + dp + step) % 8
    return {"tm": (there // 2) * 4 + tm % 4, "tensor": te, "dp": there % 2}


def t_peer(step):
    tm, te, dp = places()
    return {"tm": tm, "tensor": (te + step) % 8, "dp": dp}


def x_peer(step):
    tm, te, dp = places()
    return {"tm": tm, "tensor": (te + 2 * step) % 8, "dp": dp}


def sibling():
    tm, te, dp = places()
    return {"tm": tm, "tensor": (te // 2) * 2 + 1 - te % 2, "dp": dp}


class Copies:
    def __init__(self, send_sems, recv_sems):
        self.send_sems, self.recv_sems = send_sems, recv_sems
        self.made = []

    def send(self, src, dst, to):
        at = len(self.made)
        copy = pltpu.make_async_remote_copy(
            src_ref=src,
            dst_ref=dst,
            send_sem=self.send_sems.at[at],
            recv_sem=self.recv_sems.at[at],
            device_id=to,
            device_id_type=pl.DeviceIdType.MESH,
        )
        copy.start()
        self.made.append(copy)
        return copy

    def finish(self):
        for copy in self.made:
            copy.wait_send()


def meet(peers):
    barrier = pltpu.get_barrier_semaphore()
    for peer in peers:
        pl.semaphore_signal(
            barrier, inc=1, device_id=peer, device_id_type=pl.DeviceIdType.MESH
        )
    pl.semaphore_wait(barrier, len(peers))


def f32(value):
    return value.astype(jnp.float32)


def frame_peer(step):
    tm, te, dp = places()
    return {"tm": (tm + step) % 16, "tensor": te, "dp": dp}


CHUNKS = tuple((first, 256) for first in range(0, 1536, 256))
HALVES = ((0, 768), (768, 768))
SLOTS = 320
COPIES = 16 * len(CHUNKS) + 4 + 7 * len(HALVES) + 18 + 21 + 7 + 3 + 7


def joint_kernel(
    table_ref,
    lengths_ref,
    frames_hbm,
    blocks_hbm,
    value_hbm,
    gate_hbm,
    out_hbm,
    taps_ref,
    gain_ref,
    input_grad,
    wide_sum,
    tail_sum,
    out_sum,
    small_sum,
    frames_ref,
    pair_ref,
    last_ref,
    taps,
    ahead_ref,
    behind_ref,
    norm_ref,
    lin_ref,
    sig_ref,
    conv_ref,
    glu_0,
    glu_1,
    full_ref,
    swish_ref,
    cot_ref,
    cot_0,
    cot_1,
    both_cot,
    tap_sums,
    gain_sums,
    summing,
    edge_out,
    edge_in,
    far_out,
    far_in,
    part_ref,
    core_in,
    chip_sum,
    x_a,
    x_b,
    x_plus,
    x_minus,
    wide_ref,
    wide_a,
    wide_b,
    wide_plus,
    wide_minus,
    wide_mid,
    wide_z,
    tail_ref,
    tail_a,
    tail_b,
    tail_plus,
    tail_minus,
    tail_mid,
    tail_z,
    out_ref,
    out_a,
    out_b,
    out_plus,
    out_minus,
    out_mid,
    out_z,
    small_ref,
    gain_in,
    small_mid,
    small_y,
    small_last,
    small_z,
    load_sems,
    send_sems,
    recv_sems,
    *rest,
):
    count = len(CHUNKS)
    y_out, y_in = (rest[:count], rest[count : 2 * count])
    z_out, z_in = (rest[2 * count : 3 * count], rest[3 * count : 4 * count])
    blocks, z_pass = (rest[4 * count : 5 * count], rest[5 * count :])
    tm, te, dp = places()
    y, zh, z = (tm % 4, tm // 4, (tm // 4) * 2 + dp)
    x, core = (te // 2, te % 2)
    bf16 = jnp.bfloat16
    factor = 1.0 / math.sqrt(32768.0)
    columns = [pl.ds(first, size) for first, size in CHUNKS]
    half_a, half_b = (pl.ds(0, 64), pl.ds(64, 64))
    zh_next, zh_last, zh_far = ((zh + 1) % 4, (zh + 3) % 4, (zh + 2) % 4)

    loads = []

    def load(src, dst):
        copy = pltpu.make_async_copy(src, dst, load_sems.at[len(loads)])
        copy.start()
        loads.append(copy)
        return copy

    block_loads = [load(blocks_hbm.at[:, :, columns[c]], blocks[c]) for c in range(count)]
    frames_load = load(frames_hbm, frames_ref)
    weight_loads = [
        load(value_hbm.at[pl.ds(0, 128)], pair_ref.at[pl.ds(0, 128)]),
        load(gate_hbm.at[pl.ds(0, 128)], pair_ref.at[pl.ds(128, 128)]),
        load(value_hbm.at[pl.ds(128, 64)], pair_ref.at[pl.ds(256, 64)]),
        load(gate_hbm.at[pl.ds(128, 64)], pair_ref.at[pl.ds(320, 64)]),
    ]
    out_load = load(out_hbm, last_ref.at[pl.ds(0, 192)])

    meet(
        [t_peer(k) for k in range(1, 8)]
        + [y_peer(k) for k in range(1, 4)]
        + [z_peer(k) for k in range(1, 8)]
        + [frame_peer(1), frame_peer(-1)]
    )
    net = Copies(send_sems, recv_sems)

    def place(c):
        block_loads[c].wait()
        copies = []
        for k in (2, 1, 3, 0):
            first = ((y + k) % 4) * 20
            target = y_in[c].at[y] if k == 0 else y_out[c].at[k - 1]

            @pl.loop(0, 20)
            def _(slot):
                source = table_ref[first + slot]
                live = table_ref[80 + first + slot]
                rows = blocks[c][source]
                ids = lax.broadcasted_iota(jnp.int32, rows.shape, 0)
                target[pl.ds(pl.multiple_of(slot * 16, 16), 16)] = jnp.where(
                    ids < live, f32(rows), 0.0
                ).astype(bf16)

            if k:
                copies.append(net.send(target, y_in[c].at[y], y_peer(k)))
        return copies

    def combine(c, copies):
        for copy in copies:
            copy.wait_recv()
        width = CHUNKS[c][1]

        @pl.loop(0, width, step=256)
        def _(col):
            cols = pl.ds(pl.multiple_of(col, 256), 256)
            total = jnp.dot(
                summing[...],
                y_in[c][:, :, cols].reshape(4 * SLOTS, 256),
                preferred_element_type=jnp.float32,
            ).astype(bf16)
            for at in range(4):
                z_out[c][at, :, cols] = total[128 * at : 128 * at + 128]

        sums, passing = (z_out[c], z_pass[c])
        return (
            net.send(sums.at[zh_far, half_a], passing.at[0], z_peer(2)),
            net.send(sums.at[zh_far, half_b], passing.at[1], z_peer(-2)),
            net.send(sums.at[zh_next, half_b], z_in[c].at[0, half_b], z_peer(2)),
            net.send(sums.at[zh_last, half_a], z_in[c].at[1, half_a], z_peer(-2)),
        )

    def forward(c, copies):
        sums, passing = (z_out[c], z_pass[c])
        copies[0].wait_recv()
        passing[0] = (f32(passing[0]) + f32(sums[zh_next, half_a])).astype(bf16)
        one = net.send(passing.at[0], z_in[c].at[0, half_a], z_peer(2))
        copies[1].wait_recv()
        passing[1] = (f32(passing[1]) + f32(sums[zh_last, half_b])).astype(bf16)
        return copies[2:] + (one, net.send(passing.at[1], z_in[c].at[1, half_b], z_peer(-2)))

    def spread(c, copies):
        for copy in copies:
            copy.wait_recv()
        total = (f32(z_out[c][zh]) + f32(z_in[c][0]) + f32(z_in[c][1])).astype(bf16)
        for block in range(8):
            full_ref[block, te, :, columns[c]] = total[16 * block : 16 * block + 16]
        own = full_ref.at[:, te, :, columns[c]]
        return [net.send(own, own, x_peer(k)) for k in (2, 1, 3)], [
            net.send(own, own, sibling())
        ]

    def relay(c, copies):
        for k, copy in zip((2, 1, 3), copies[0]):
            copy.wait_recv()
            there = full_ref.at[:, (te + 8 - 2 * k) % 8, :, columns[c]]
            copies[1].append(net.send(there, there, sibling()))
        return copies[1]

    def project(c, copies):
        for copy in copies:
            copy.wait_recv()

        @pl.loop(0, 8, step=4)
        def _(block):
            rows = pl.ds(pl.multiple_of(block * 128, 512), 512)
            term = contract_last(
                full_ref[pl.ds(block, 4), :, :, columns[c]].reshape(512, CHUNKS[c][1]),
                last_ref[:, columns[c]],
            )
            if c == 0:
                cot_ref[rows] = term
            else:
                cot_ref[rows] += term

    y_copies = [place(0), place(1), place(2)]

    @pl.loop(0, 10)
    def _(group):
        tiles = []
        for k in range(8):
            at = table_ref[160 + group * 8 + k] * 16
            gap = lax.broadcasted_iota(jnp.int32, (16, 512), 1) - lax.broadcasted_iota(
                jnp.int32, (16, 512), 0
            )
            tiles.append(jnp.where(gap == at, 1.0, 0.0))
        cols = pl.ds(pl.multiple_of(group * 128, 128), 128)
        summing[:, cols] = jnp.concatenate(tiles, axis=0).T.astype(bf16)

    frames_load.wait()

    @pl.loop(0, 1024, step=32)
    def _(row):
        rows = pl.ds(pl.multiple_of(row, 32), 32)
        cells = f32(frames_ref[rows])
        centered = cells - jnp.mean(cells, axis=1, keepdims=True)
        scale = lax.rsqrt(jnp.mean(centered * centered, axis=1, keepdims=True) + epsilon)
        norm_ref[rows] = ((centered * scale) * gain_ref[...]).astype(bf16)

    for copy in weight_loads:
        copy.wait()

    z_copies = [combine(0, y_copies[0])]
    y_copies.append(place(3))

    @pl.loop(0, 1024, step=256)
    def _(row):
        rows = pl.ds(pl.multiple_of(row, 256), 256)
        wide = pl.ds(pl.multiple_of(row + 16, 16), 256)
        lin = contract_last(norm_ref[rows], pair_ref[...])
        value_0, gate_0, value_1 = (lin[:, :128], lin[:, 128:256], lin[:, 256:])
        sig_0 = jax.nn.sigmoid(gate_0)
        sig_1 = jax.nn.sigmoid(pltpu.roll(value_1, 64, 1))
        lin_ref[rows, :128] = value_0
        lin_ref[rows, 128:] = value_1
        sig_ref[rows, :128] = sig_0
        sig_ref[rows, 128:] = sig_1
        glu_0[wide] = f32((value_0 * sig_0).astype(bf16))
        glu_1[wide] = f32((value_1 * sig_1).astype(bf16))

    for at, first in ((0, 16), (1, 1024)):
        edge_out[at, :, :128] = glu_0[first : first + 16].astype(bf16)
        edge_out[at, :, 128:] = glu_1[first : first + 16].astype(bf16)
    edges = (
        net.send(edge_out.at[0], edge_in.at[1], frame_peer(-1)),
        net.send(edge_out.at[1], edge_in.at[0], frame_peer(1)),
    )

    z_copies.append(combine(1, y_copies[1]))
    y_copies.append(place(4))
    z_passed = [forward(0, z_copies[0])]

    taps[...] = jnp.zeros(taps.shape, jnp.float32)
    taps[:KERNEL, :192] = f32(taps_ref[...])
    last_ref[192:] = jnp.zeros((64, 1536), bf16)
    tap_sums[...] = jnp.zeros(tap_sums.shape, jnp.float32)
    ends = [lengths_ref[0, 0]]
    for at in range(1, 22):
        ends.append(ends[-1] + lengths_ref[0, at])

    @pl.loop(0, 1024, step=64)
    def _(row):
        rows = pl.ds(pl.multiple_of(row, 64), 64)
        at = lax.broadcasted_iota(jnp.int32, (64, 128), 0) + (tm * 1024 + row)
        end, start = (jnp.full((64, 128), 16384, jnp.int32), jnp.zeros((64, 128), jnp.int32))
        for bound in ends:
            past = at >= bound
            start = jnp.where(past, bound, start)
            end = jnp.where(past, end, jnp.minimum(end, bound))
        ahead_ref[rows] = end - 1 - at
        behind_ref[rows] = at - start

    for at, first in ((0, 0), (1, 1040)):
        edges[1 - at].wait_recv()
        glu_0[first : first + 16] = f32(edge_in[at, :, :128])
        glu_1[first : first + 16] = f32(edge_in[at, :, 128:])

    def nearby(ahead, behind, off):
        return ahead >= off if off > 0 else behind >= -off

    @pl.loop(0, 1024, step=32)
    def _(row):
        rows = pl.ds(pl.multiple_of(row, 32), 32)
        ahead, behind = (ahead_ref[rows], behind_ref[rows])
        total_0 = jnp.zeros((32, 128), jnp.float32)
        total_1 = jnp.zeros((32, 128), jnp.float32)
        for k in range(KERNEL):
            off = k - KERNEL // 2
            near = nearby(ahead, behind, off)
            shifted = pl.ds(row + 16 + off, 32)
            total_0 = total_0 + taps[k : k + 1, :128] * jnp.where(near, glu_0[shifted], 0.0)
            total_1 = total_1 + taps[k : k + 1, 128:] * jnp.where(near, glu_1[shifted], 0.0)
        conv_ref[rows, :128] = total_0
        conv_ref[rows, 128:] = total_1
        swish_ref[rows, :128] = (total_0 * jax.nn.sigmoid(total_0)).astype(bf16)
        swish_ref[rows, 128:] = (total_1 * jax.nn.sigmoid(total_1)).astype(bf16)

    out_load.wait()
    x_copies, last = ([], [])
    for c in range(2, count + 4):
        if c < count:
            z_copies.append(combine(c, y_copies[c]))
            if len(y_copies) < count:
                y_copies.append(place(len(y_copies)))
        if c - 1 < count:
            z_passed.append(forward(c - 1, z_copies[c - 1]))
        if c - 2 < count:
            x_copies.append(spread(c - 2, z_passed[c - 2]))
        if 0 <= c - 3 < count:
            last.append(relay(c - 3, x_copies[c - 3]))
        if 0 <= c - 4 < count:
            project(c - 4, last[c - 4])

    @pl.loop(0, 1024, step=64)
    def _(row):
        rows = pl.ds(pl.multiple_of(row, 64), 64)
        wide = pl.ds(pl.multiple_of(row + 16, 16), 64)
        conv = conv_ref[rows]
        sig = jax.nn.sigmoid(conv)
        cot = cot_ref[rows] * sig * (1.0 + conv * (1.0 - sig))
        cot_0[wide] = cot[:, :128]
        cot_1[wide] = cot[:, 128:]

    for at, first in ((0, 16), (1, 1024)):
        far_out[at, :, :128] = cot_0[first : first + 16]
        far_out[at, :, 128:] = cot_1[first : first + 16]
    edges = (
        net.send(far_out.at[0], far_in.at[1], frame_peer(-1)),
        net.send(far_out.at[1], far_in.at[0], frame_peer(1)),
    )

    over_frames = (((0,), (0,)), ((), ()))
    lower, upper = (pl.ds(0, 2), pl.ds(2, 2))
    y_next, y_last, y_far = ((y + 1) % 4, (y + 3) % 4, (y + 2) % 4)
    x_next, x_last, x_far = ((x + 1) % 4, (x + 3) % 4, (x + 2) % 4)

    def begin_y(ref, a, b, plus, minus):
        first = (
            net.send(ref.at[lower, y_far], a, y_peer(1)),
            net.send(ref.at[upper, y_far], b, y_peer(-1)),
        )
        plain = (
            net.send(ref.at[upper, y_next], plus.at[upper], y_peer(1)),
            net.send(ref.at[lower, y_last], minus.at[lower], y_peer(-1)),
        )
        return first, plain

    def pass_y(begun, ref, a, b, plus, minus):
        first, plain = begun
        first[0].wait_recv()
        for i in range(2):
            a[i] = (f32(a[i]) + f32(ref[i, y_next])).astype(bf16)
        one = net.send(a, plus.at[lower], y_peer(1))
        first[1].wait_recv()
        for i in range(2):
            b[i] = (f32(b[i]) + f32(ref[i + 2, y_last])).astype(bf16)
        return plain + (one, net.send(b, minus.at[upper], y_peer(-1)))

    def begin_z(passed, ref, plus, minus, mid, z_in_ref):
        for copy in passed:
            copy.wait_recv()
        for i in range(4):
            total = (f32(ref[i, y]) + f32(plus[i]) + f32(minus[i])).astype(bf16)
            mid[2 * i] = total[:48]
            mid[2 * i + 1] = total[48:]
        z_in_ref[z] = mid[z]
        return [
            net.send(mid.at[(z + k) % 8], z_in_ref.at[z], z_peer(k)) for k in (4, 3, 5, 2, 6, 1, 7)
        ]

    def end_z(copies, z_in_ref):
        for copy in copies:
            copy.wait_recv()
        total = f32(z_in_ref[0])
        for at in range(1, 8):
            total = total + f32(z_in_ref[at])
        return total * factor

    @pl.loop(0, 4)
    def _(at):
        cols = pl.ds(pl.multiple_of(at * 384, 128), 384)
        term = lax.dot_general(
            full_ref[:, :, :, cols].reshape(1024, 384),
            swish_ref[...],
            over_frames,
            preferred_element_type=jnp.float32,
        ).astype(bf16)
        for k in range(4):
            out_ref[at, k] = term[96 * k : 96 * k + 96]

    out_set = (out_a, out_b, out_plus, out_minus)
    wide_set = (wide_a, wide_b, wide_plus, wide_minus)
    tail_set = (tail_a, tail_b, tail_plus, tail_minus)
    out_begun = begin_y(out_ref, *out_set)

    for at, first in ((0, 0), (1, 1040)):
        edges[1 - at].wait_recv()
        cot_0[first : first + 16] = far_in[at, :, :128]
        cot_1[first : first + 16] = far_in[at, :, 128:]

    def back(row, lanes, cot, glu):
        rows = pl.ds(pl.multiple_of(row, 32), 32)
        wide = pl.ds(pl.multiple_of(row + 16, 16), 32)
        ahead, behind = (ahead_ref[rows], behind_ref[rows])
        here = cot[wide]
        total = jnp.zeros((32, 128), jnp.float32)
        for k in range(KERNEL):
            off = k - KERNEL // 2
            near = nearby(ahead, behind, off)
            shifted = pl.ds(row + 16 + off, 32)
            m = KERNEL - 1 - k
            total = total + taps[m : m + 1, lanes] * jnp.where(near, cot[shifted], 0.0)
            term = here * jnp.where(near, glu[shifted], 0.0)
            tap_sums[k, :, lanes] += jnp.sum(term.reshape(4, 8, 128), axis=0)
        value, sig = (lin_ref[rows, lanes], sig_ref[rows, lanes])
        return rows, total * sig, total * value * sig * (1.0 - sig)

    @pl.loop(0, 1024, step=32)
    def _(row):
        rows, value_cot, gate_cot = back(row, slice(0, 128), cot_0, glu_0)
        both_cot[rows, :128] = value_cot.astype(bf16)
        both_cot[rows, 128:256] = gate_cot.astype(bf16)

    out_passed = pass_y(out_begun, out_ref, *out_set)

    @pl.loop(0, 4)
    def _(at):
        cols = pl.ds(pl.multiple_of(at * 384, 128), 384)
        term = lax.dot_general(
            norm_ref[:, cols],
            both_cot[:, :256],
            over_frames,
            preferred_element_type=jnp.float32,
        ).astype(bf16)
        for k in range(4):
            wide_ref[at, k] = term[96 * k : 96 * k + 96]

    wide_begun = begin_y(wide_ref, *wide_set)

    def back_tail(row):
        rows, value_cot, gate_cot = back(row, slice(128, 256), cot_1, glu_1)
        both_cot[rows, 256:] = (value_cot + pltpu.roll(gate_cot, 64, 1)).astype(bf16)

    @pl.loop(0, 512, step=32)
    def _(row):
        back_tail(row)

    out_z_copies = begin_z(out_passed, out_ref, out_plus, out_minus, out_mid, out_z)

    @pl.loop(512, 1024, step=32)
    def _(row):
        back_tail(row)

    wide_passed = pass_y(wide_begun, wide_ref, *wide_set)
    gain_sums[...] = jnp.zeros(gain_sums.shape, jnp.float32)
    core_copies = []
    for at, (first, size) in enumerate(HALVES):
        @pl.loop(first, first + size, step=256)
        def _(col):
            cols = pl.ds(pl.multiple_of(col, 256), 256)
            for row in (0, 512):
                part = jnp.dot(
                    both_cot[row : row + 512],
                    pair_ref[:, cols],
                    preferred_element_type=jnp.float32,
                )
                gain_sums[:, cols] += jnp.sum(
                    (part * f32(norm_ref[row : row + 512, cols])).reshape(64, 8, 256), axis=0
                )
                part = part.astype(bf16)
                for k in range(4):
                    part_ref[row // 256 + k // 2, k % 2, :, cols] = part[128 * k : 128 * k + 128]

        cols = pl.ds(first, size)
        core_copies.append(
            net.send(part_ref.at[:, 1 - core, :, cols], core_in.at[:, :, cols], sibling())
        )

    @pl.loop(0, 4)
    def _(at):
        cols = pl.ds(pl.multiple_of(at * 384, 128), 384)
        term = lax.dot_general(
            norm_ref[:, cols],
            both_cot[:, 256:],
            over_frames,
            preferred_element_type=jnp.float32,
        ).astype(bf16)
        for k in range(4):
            tail_ref[at, k] = term[96 * k : 96 * k + 96]

    tail_begun = begin_y(tail_ref, *tail_set)

    gain_rows = pl.ds(32, 8)
    small_ref[...] = jnp.zeros(small_ref.shape, jnp.float32)
    for k in range(KERNEL):
        small_ref[k : k + 1] = jnp.sum(tap_sums[k], axis=0, keepdims=True)
    gain_part = jnp.sum(gain_sums[...], axis=0, keepdims=True) / gain_ref[...]
    for k in range(6):
        small_ref[32 + k : 33 + k] = gain_part[:, 256 * k : 256 * k + 256]
    gain_in[te] = small_ref[gain_rows, :]
    gain_copies = [
        net.send(small_ref.at[gain_rows], gain_in.at[te], t_peer(k)) for k in range(1, 8)
    ]

    x_begun = []
    for at, (first, size) in enumerate(HALVES):
        core_copies[at].wait_recv()
        cols = pl.ds(first, size)

        def add_core(to):
            @pl.loop(0, 128, step=32)
            def _(row):
                rows = pl.ds(pl.multiple_of(row, 32), 32)
                chip_sum[to, rows, cols] = (
                    f32(part_ref[to, core, rows, cols]) + f32(core_in[to, rows, cols])
                ).astype(bf16)

        add_core(x_far)
        begun = (
            net.send(chip_sum.at[x_far, half_a, cols], x_a.at[:, cols], x_peer(1)),
            net.send(chip_sum.at[x_far, half_b, cols], x_b.at[:, cols], x_peer(-1)),
        )
        add_core(x_next)
        add_core(x_last)
        plain = (
            net.send(chip_sum.at[x_next, half_b, cols], x_plus.at[half_b, cols], x_peer(1)),
            net.send(chip_sum.at[x_last, half_a, cols], x_minus.at[half_a, cols], x_peer(-1)),
        )
        x_begun.append((begun, plain))

    wide_z_copies = begin_z(wide_passed, wide_ref, wide_plus, wide_minus, wide_mid, wide_z)
    tail_passed = pass_y(tail_begun, tail_ref, *tail_set)

    x_passed = []
    for at, (first, size) in enumerate(HALVES):
        begun, plain = x_begun[at]
        cols = pl.ds(first, size)

        def add_x(ref, to, start):
            @pl.loop(0, 64, step=32)
            def _(row):
                rows = pl.ds(pl.multiple_of(row, 32), 32)
                other = pl.ds(pl.multiple_of(row + start, 32), 32)
                ref[rows, cols] = (f32(ref[rows, cols]) + f32(chip_sum[to, other, cols])).astype(
                    bf16
                )

        begun[0].wait_recv()
        add_x(x_a, x_next, 0)
        one = net.send(x_a.at[:, cols], x_plus.at[half_a, cols], x_peer(1))
        begun[1].wait_recv()
        add_x(x_b, x_last, 64)
        x_passed.append(
            plain + (one, net.send(x_b.at[:, cols], x_minus.at[half_b, cols], x_peer(-1)))
        )

    for copy in gain_copies:
        copy.wait_recv()
    small_mid[pl.ds(0, 32), :] = small_ref[pl.ds(0, 32), :]
    total = gain_in[0]
    for at in range(1, 8):
        total = total + gain_in[at]
    small_mid[gain_rows, :] = total
    small_y[y] = small_mid[...]
    small_copies = [net.send(small_mid, small_y.at[y], y_peer(k)) for k in range(1, 4)]

    tail_z_copies = begin_z(tail_passed, tail_ref, tail_plus, tail_minus, tail_mid, tail_z)

    for copy in small_copies:
        copy.wait_recv()
    total = small_y[0]
    for at in range(1, 4):
        total = total + small_y[at]
    small_last[...] = total
    small_z[z] = total
    last_copies = [net.send(small_last, small_z.at[z], z_peer(k)) for k in range(1, 8)]

    out_sum[...] = end_z(out_z_copies, out_z)
    wide_sum[...] = end_z(wide_z_copies, wide_z)

    for copies in x_passed:
        for copy in copies:
            copy.wait_recv()

    @pl.loop(0, 8)
    def _(block):
        rows = pl.ds(pl.multiple_of(block * 16, 16), 16)
        summed = (
            f32(part_ref[x, core, rows])
            + f32(core_in[x, rows])
            + f32(x_plus[rows])
            + f32(x_minus[rows])
        )
        cells = f32(frames_ref[pl.ds(pl.multiple_of(te * 128 + block * 16, 16), 16)])
        centered = cells - jnp.mean(cells, axis=1, keepdims=True)
        inv_std = lax.rsqrt(jnp.mean(centered * centered, axis=1, keepdims=True) + epsilon)
        normed = centered * inv_std
        scaled = summed * gain_ref[...]
        input_grad[rows] = (
            f32(full_ref[te, block])
            + inv_std
            * (
                scaled
                - jnp.mean(scaled, axis=1, keepdims=True)
                - normed * jnp.mean(scaled * normed, axis=1, keepdims=True)
            )
        ).astype(bf16)

    tail_sum[...] = end_z(tail_z_copies, tail_z)

    for copy in last_copies:
        copy.wait_recv()
    total = small_z[0]
    for at in range(1, 8):
        total = total + small_z[at]
    small_sum[...] = total * factor
    net.finish()


def joint_call(table, lengths, frames, blocks, value_weight, gate_weight, out_weight, taps, gain):
    count, width = frames.shape
    span = value_weight.shape[0]
    bf16, single = (jnp.bfloat16, jnp.float32)
    vmem = pl.BlockSpec(memory_space=pltpu.VMEM)
    smem = pl.BlockSpec(memory_space=pltpu.SMEM)
    where = pl.BlockSpec(memory_space=pl.ANY)

    def weight_scratch(lanes):
        return [
            pltpu.VMEM((4, 4, 96, lanes), bf16),
            pltpu.VMEM((2, 96, lanes), bf16),
            pltpu.VMEM((2, 96, lanes), bf16),
            pltpu.VMEM((4, 96, lanes), bf16),
            pltpu.VMEM((4, 96, lanes), bf16),
            pltpu.VMEM((8, 48, lanes), bf16),
            pltpu.VMEM((8, 48, lanes), bf16),
        ]

    return pl.pallas_call(
        joint_kernel,
        out_shape=(
            jax.ShapeDtypeStruct((128, width), bf16),
            jax.ShapeDtypeStruct((48, 256), single),
            jax.ShapeDtypeStruct((48, 128), single),
            jax.ShapeDtypeStruct((48, 256), single),
            jax.ShapeDtypeStruct((40, 256), single),
        ),
        in_specs=[smem] * 2 + [where] * 5 + [vmem] * 2,
        out_specs=[vmem] * 5,
        scratch_shapes=[
            pltpu.VMEM((count, width), bf16),
            pltpu.VMEM((2 * span, width), bf16),
            pltpu.VMEM((256, width), bf16),
            pltpu.VMEM((32, 256), single),
            pltpu.VMEM((count, 128), jnp.int32),
            pltpu.VMEM((count, 128), jnp.int32),
            pltpu.VMEM((count, width), bf16),
            pltpu.VMEM((count, 256), single),
            pltpu.VMEM((count, 256), single),
            pltpu.VMEM((count, 256), single),
            pltpu.VMEM((count + 32, 128), single),
            pltpu.VMEM((count + 32, 128), single),
            pltpu.VMEM((8, 8, 16, width), bf16),
            pltpu.VMEM((count, 256), bf16),
            pltpu.VMEM((count, 256), single),
            pltpu.VMEM((count + 32, 128), single),
            pltpu.VMEM((count + 32, 128), single),
            pltpu.VMEM((count, 2 * span), bf16),
            pltpu.VMEM((KERNEL, 8, 256), single),
            pltpu.VMEM((8, width), single),
            pltpu.VMEM((512, 4 * SLOTS), bf16),
            pltpu.VMEM((2, 16, 256), bf16),
            pltpu.VMEM((2, 16, 256), bf16),
            pltpu.VMEM((2, 16, 256), single),
            pltpu.VMEM((2, 16, 256), single),
            pltpu.VMEM((4, 2, 128, width), bf16),
            pltpu.VMEM((4, 128, width), bf16),
            pltpu.VMEM((4, 128, width), bf16),
            pltpu.VMEM((64, width), bf16),
            pltpu.VMEM((64, width), bf16),
            pltpu.VMEM((128, width), bf16),
            pltpu.VMEM((128, width), bf16),
        ]
        + weight_scratch(256)
        + weight_scratch(128)
        + weight_scratch(256)
        + [
            pltpu.VMEM((40, 256), single),
            pltpu.VMEM((8, 8, 256), single),
            pltpu.VMEM((40, 256), single),
            pltpu.VMEM((4, 40, 256), single),
            pltpu.VMEM((40, 256), single),
            pltpu.VMEM((8, 40, 256), single),
            pltpu.SemaphoreType.DMA((len(CHUNKS) + 6,)),
            pltpu.SemaphoreType.DMA((COPIES,)),
            pltpu.SemaphoreType.DMA((COPIES,)),
        ]
        + [pltpu.VMEM((3, SLOTS, size), bf16) for _, size in CHUNKS]
        + [pltpu.VMEM((4, SLOTS, size), bf16) for _, size in CHUNKS]
        + [pltpu.VMEM((4, 128, size), bf16) for _, size in CHUNKS]
        + [pltpu.VMEM((2, 128, size), bf16) for _, size in CHUNKS]
        + [pltpu.VMEM((64, 16, size), bf16) for _, size in CHUNKS]
        + [pltpu.VMEM((2, 64, size), bf16) for _, size in CHUNKS],
        compiler_params=pltpu.CompilerParams(
            collective_id=0, has_side_effects=True, vmem_limit_bytes=60 * 1024 * 1024
        ),
        name="joint",
    )(table, lengths, frames, blocks, value_weight, gate_weight, out_weight, taps, gain)


def finish_kernel(
    input_ref,
    wide_ref,
    tail_ref,
    out_ref,
    small_ref,
    input_grad,
    value_grad,
    gate_grad,
    out_grad,
    kernel_grad,
    gain_grad,
):
    input_grad[...] = input_ref[...]
    tail = tail_ref[...]
    value_grad[:, :128] = wide_ref[:, :128]
    value_grad[:, 128:] = tail[:, :64]
    gate_grad[:, :128] = wide_ref[:, 128:]
    gate_grad[:, 128:] = pltpu.roll(tail, 64, 1)[:, :64]
    out_grad[...] = out_ref[:, :192]
    kernel_grad[...] = small_ref[:KERNEL, :192]
    for k in range(6):
        gain_grad[:, 256 * k : 256 * k + 256] = small_ref[32 + k : 33 + k]


def finish_call(*sums):
    single = jnp.float32
    width = sums[0].shape[1]
    vmem = pl.BlockSpec(memory_space=pltpu.VMEM)
    return pl.pallas_call(
        finish_kernel,
        out_shape=(jax.ShapeDtypeStruct(sums[0].shape, jnp.bfloat16),)
        + (jax.ShapeDtypeStruct((48, 192), single),) * 3
        + (
            jax.ShapeDtypeStruct((KERNEL, 192), single),
            jax.ShapeDtypeStruct((1, width), single),
        ),
        in_specs=[vmem] * 5,
        out_specs=[vmem] * 6,
        name="finish",
    )(*sums)


def routing(block_device, block_sub, block_rows):
    tm, te, dp = places()
    first = (tm // 4) * 4
    devices = lax.dynamic_slice_in_dim(block_device.reshape(16, 64), first, 4, 0)
    subs = lax.dynamic_slice_in_dim(block_sub.reshape(16, 64), first, 4, 0)
    counts = lax.dynamic_slice_in_dim(block_rows.reshape(16, 64), tm, 1, 0)
    earlier = jnp.arange(64)[:, None] > jnp.arange(64)[None, :]
    column = devices % 4
    same = (column[:, :, None] == column[:, None, :]) & earlier[None]
    rank = jnp.sum(same.astype(jnp.int32), axis=2)
    slot = column * 20 + rank
    own = lax.dynamic_slice_in_dim(slot, tm % 4, 1, 0)
    own_hot = own == jnp.arange(80, dtype=jnp.int32)[:, None]
    source = jnp.sum(jnp.where(own_hot, jnp.arange(64, dtype=jnp.int32)[None], 0), axis=1)
    live = jnp.sum(jnp.where(own_hot, jnp.clip(counts - te * 16, 0, 16), 0), axis=1)
    place = (tm % 4) * 20 + jnp.arange(20, dtype=jnp.int32)
    hot = slot[:, None, :] == place[None, :, None]
    block = (devices // 4) * 8 + subs
    dest = jnp.sum(jnp.where(hot, block[:, None, :] + 1, 0), axis=2).reshape(80) - 1
    return jnp.concatenate([source, live, jnp.where(dest < 0, 64, dest)])


def on_device(
    inputs,
    grad_blocks,
    block_device,
    block_sub,
    block_rows,
    seg_lengths,
    value_weight,
    gate_weight,
    out_weight,
    conv_kernel,
    norm_gain,
):
    width = inputs.shape[2]
    sums = joint_call(
        routing(block_device, block_sub, block_rows),
        seg_lengths,
        inputs[0],
        grad_blocks[0],
        value_weight,
        gate_weight,
        out_weight,
        conv_kernel,
        norm_gain[None],
    )
    input_grad, value_grad, gate_grad, out_grad, kernel_grad, gain_grad = finish_call(*sums)
    return (
        input_grad[None],
        value_grad.T,
        gate_grad.T,
        out_grad.T,
        kernel_grad,
        gain_grad.reshape(width),
    )


def solution(mesh):
    in_specs = (
        P("dp", "tm", None),
        P("dp", "tm", "tensor", None),
        P("dp", None, None),
        P("dp", None),
        P("dp", None),
        P("dp", None),
        P("tensor", None),
        P("tensor", None),
        P("tensor", None),
        P(None, "tensor"),
        P(),
    )
    out_specs = (
        P("dp", ("tm", "tensor"), None),
        P("tensor", ("tm", "dp")),
        P("tensor", ("tm", "dp")),
        P("tensor", ("tm", "dp")),
        P(None, "tensor"),
        P(),
    )
    return jax.shard_map(
        on_device, mesh=mesh, in_specs=in_specs, out_specs=out_specs, check_vma=False
    )
```

```python
import math

import jax
import jax.numpy as jnp
from jax import lax
from jax.experimental import pallas as pl
from jax.experimental.pallas import tpu as pltpu
from jax.sharding import PartitionSpec as P

KERNEL = 31


epsilon = 1e-05


def contract_last(left, right):
    return lax.dot_general(
        left, right, (((1,), (1,)), ((), ())), preferred_element_type=jnp.float32
    )


def places():
    tm, te, dp = (lax.axis_index("tm"), lax.axis_index("tensor"), lax.axis_index("dp"))
    return tm, te, dp


def y_peer(step):
    tm, te, dp = places()
    return {"tm": (tm // 4) * 4 + (tm + step) % 4, "tensor": te, "dp": dp}


def z_peer(step):
    tm, te, dp = places()
    there = ((tm // 4) * 2 + dp + step) % 8
    return {"tm": (there // 2) * 4 + tm % 4, "tensor": te, "dp": there % 2}


def t_peer(step):
    tm, te, dp = places()
    return {"tm": tm, "tensor": (te + step) % 8, "dp": dp}


def x_peer(step):
    tm, te, dp = places()
    return {"tm": tm, "tensor": (te + 2 * step) % 8, "dp": dp}


def sibling():
    tm, te, dp = places()
    return {"tm": tm, "tensor": (te // 2) * 2 + 1 - te % 2, "dp": dp}


class Copies:
    def __init__(self, send_sems, recv_sems):
        self.send_sems, self.recv_sems = send_sems, recv_sems
        self.made = []

    def send(self, src, dst, to):
        at = len(self.made)
        copy = pltpu.make_async_remote_copy(
            src_ref=src,
            dst_ref=dst,
            send_sem=self.send_sems.at[at],
            recv_sem=self.recv_sems.at[at],
            device_id=to,
            device_id_type=pl.DeviceIdType.MESH,
        )
        copy.start()
        self.made.append(copy)
        return copy

    def finish(self):
        for copy in self.made:
            copy.wait_send()


def meet(peers):
    barrier = pltpu.get_barrier_semaphore()
    for peer in peers:
        pl.semaphore_signal(
            barrier, inc=1, device_id=peer, device_id_type=pl.DeviceIdType.MESH
        )
    pl.semaphore_wait(barrier, len(peers))


def f32(value):
    return value.astype(jnp.float32)


def frame_peer(step):
    tm, te, dp = places()
    return {"tm": (tm + step) % 16, "tensor": te, "dp": dp}


CHUNKS = tuple((first, 256) for first in range(0, 1536, 256))
HALVES = ((0, 768), (768, 768))
SLOTS = 320
COPIES = 16 * len(CHUNKS) + 4 + 7 * len(HALVES) + 18 + 21 + 7 + 3 + 7 + 3 + 7


def joint_kernel(
    table_ref,
    lengths_ref,
    frames_hbm,
    blocks_hbm,
    value_hbm,
    gate_hbm,
    out_hbm,
    taps_ref,
    gain_ref,
    input_grad,
    wide_sum,
    tail_sum,
    out_sum,
    small_sum,
    frames_ref,
    pair_ref,
    last_ref,
    taps,
    ahead_ref,
    behind_ref,
    norm_ref,
    lin_ref,
    sig_ref,
    conv_ref,
    glu_0,
    glu_1,
    full_ref,
    swish_ref,
    cot_ref,
    cot_0,
    cot_1,
    both_cot,
    tap_sums,
    gain_sums,
    summing,
    edge_out,
    edge_in,
    far_out,
    far_in,
    part_ref,
    core_in,
    chip_sum,
    x_a,
    x_b,
    x_plus,
    x_minus,
    wide_ref,
    wide_a,
    wide_b,
    wide_plus,
    wide_minus,
    wide_mid,
    wide_z,
    tail_ref,
    tail_a,
    tail_b,
    tail_plus,
    tail_minus,
    tail_mid,
    tail_z,
    out_ref,
    out_a,
    out_b,
    out_plus,
    out_minus,
    out_mid,
    out_z,
    gain_row,
    own_normed,
    own_scale,
    kern_ref,
    kern_y,
    kern_mid,
    kern_z,
    gain_out,
    gain_in,
    gain_mid,
    gain_y,
    gain_last,
    gain_z,
    load_sems,
    send_sems,
    recv_sems,
    *rest,
):
    count = len(CHUNKS)
    y_out, y_in = (rest[:count], rest[count : 2 * count])
    z_out, z_in = (rest[2 * count : 3 * count], rest[3 * count : 4 * count])
    blocks, z_pass = (rest[4 * count : 5 * count], rest[5 * count :])
    tm, te, dp = places()
    y, zh, z = (tm % 4, tm // 4, (tm // 4) * 2 + dp)
    x, core = (te // 2, te % 2)
    bf16 = jnp.bfloat16
    factor = 1.0 / math.sqrt(32768.0)
    columns = [pl.ds(first, size) for first, size in CHUNKS]
    half_a, half_b = (pl.ds(0, 64), pl.ds(64, 64))
    zh_next, zh_last, zh_far = ((zh + 1) % 4, (zh + 3) % 4, (zh + 2) % 4)

    for k in range(6):
        gain_row[:, 256 * k : 256 * k + 256] = gain_ref[256 * k : 256 * k + 256].reshape(1, 256)
    loads = []

    def load(src, dst):
        copy = pltpu.make_async_copy(src, dst, load_sems.at[len(loads)])
        copy.start()
        loads.append(copy)
        return copy

    block_loads = [load(blocks_hbm.at[:, :, columns[c]], blocks[c]) for c in range(count)]
    frames_load = load(frames_hbm, frames_ref)
    weight_loads = [
        load(value_hbm.at[pl.ds(0, 128)], pair_ref.at[pl.ds(0, 128)]),
        load(gate_hbm.at[pl.ds(0, 128)], pair_ref.at[pl.ds(128, 128)]),
        load(value_hbm.at[pl.ds(128, 64)], pair_ref.at[pl.ds(256, 64)]),
        load(gate_hbm.at[pl.ds(128, 64)], pair_ref.at[pl.ds(320, 64)]),
    ]
    out_load = load(out_hbm, last_ref.at[pl.ds(0, 192)])

    meet(
        [t_peer(k) for k in range(1, 8)]
        + [y_peer(k) for k in range(1, 4)]
        + [z_peer(k) for k in range(1, 8)]
        + [frame_peer(1), frame_peer(-1)]
    )
    net = Copies(send_sems, recv_sems)

    def place(c):
        block_loads[c].wait()
        copies = []
        for k in (2, 1, 3, 0):
            first = ((y + k) % 4) * 20
            target = y_in[c].at[y] if k == 0 else y_out[c].at[k - 1]

            @pl.loop(0, 20)
            def _(slot):
                source = table_ref[first + slot]
                live = table_ref[80 + first + slot]
                rows = blocks[c][source]
                ids = lax.broadcasted_iota(jnp.int32, rows.shape, 0)
                target[pl.ds(pl.multiple_of(slot * 16, 16), 16)] = jnp.where(
                    ids < live, f32(rows), 0.0
                ).astype(bf16)

            if k:
                copies.append(net.send(target, y_in[c].at[y], y_peer(k)))
        return copies

    def combine(c, copies):
        for copy in copies:
            copy.wait_recv()
        width = CHUNKS[c][1]

        @pl.loop(0, width, step=256)
        def _(col):
            cols = pl.ds(pl.multiple_of(col, 256), 256)
            total = jnp.dot(
                summing[...],
                y_in[c][:, :, cols].reshape(4 * SLOTS, 256),
                preferred_element_type=jnp.float32,
            ).astype(bf16)
            for at in range(4):
                z_out[c][at, :, cols] = total[128 * at : 128 * at + 128]

        sums, passing = (z_out[c], z_pass[c])
        return (
            net.send(sums.at[zh_far, half_a], passing.at[0], z_peer(2)),
            net.send(sums.at[zh_far, half_b], passing.at[1], z_peer(-2)),
            net.send(sums.at[zh_next, half_b], z_in[c].at[0, half_b], z_peer(2)),
            net.send(sums.at[zh_last, half_a], z_in[c].at[1, half_a], z_peer(-2)),
        )

    def forward(c, copies):
        sums, passing = (z_out[c], z_pass[c])
        copies[0].wait_recv()
        passing[0] = (f32(passing[0]) + f32(sums[zh_next, half_a])).astype(bf16)
        one = net.send(passing.at[0], z_in[c].at[0, half_a], z_peer(2))
        copies[1].wait_recv()
        passing[1] = (f32(passing[1]) + f32(sums[zh_last, half_b])).astype(bf16)
        return copies[2:] + (one, net.send(passing.at[1], z_in[c].at[1, half_b], z_peer(-2)))

    def spread(c, copies):
        for copy in copies:
            copy.wait_recv()
        total = (f32(z_out[c][zh]) + f32(z_in[c][0]) + f32(z_in[c][1])).astype(bf16)
        for block in range(8):
            full_ref[block, te, :, columns[c]] = total[16 * block : 16 * block + 16]
        own = full_ref.at[:, te, :, columns[c]]
        return [net.send(own, own, x_peer(k)) for k in (2, 1, 3)], [
            net.send(own, own, sibling())
        ]

    def relay(c, copies):
        for k, copy in zip((2, 1, 3), copies[0]):
            copy.wait_recv()
            there = full_ref.at[:, (te + 8 - 2 * k) % 8, :, columns[c]]
            copies[1].append(net.send(there, there, sibling()))
        return copies[1]

    def project(c, copies):
        for copy in copies:
            copy.wait_recv()

        @pl.loop(0, 8, step=4)
        def _(block):
            rows = pl.ds(pl.multiple_of(block * 128, 512), 512)
            term = contract_last(
                full_ref[pl.ds(block, 4), :, :, columns[c]].reshape(512, CHUNKS[c][1]),
                last_ref[:, columns[c]],
            )
            if c == 0:
                cot_ref[rows] = term
            else:
                cot_ref[rows] += term

    y_copies = [place(0), place(1), place(2)]

    @pl.loop(0, 10)
    def _(group):
        tiles = []
        for k in range(8):
            at = table_ref[160 + group * 8 + k] * 16
            gap = lax.broadcasted_iota(jnp.int32, (16, 512), 1) - lax.broadcasted_iota(
                jnp.int32, (16, 512), 0
            )
            tiles.append(jnp.where(gap == at, 1.0, 0.0))
        cols = pl.ds(pl.multiple_of(group * 128, 128), 128)
        summing[:, cols] = jnp.concatenate(tiles, axis=0).T.astype(bf16)

    frames_load.wait()

    @pl.loop(0, 1024, step=32)
    def _(row):
        rows = pl.ds(pl.multiple_of(row, 32), 32)
        cells = f32(frames_ref[rows])
        centered = cells - jnp.mean(cells, axis=1, keepdims=True)
        scale = lax.rsqrt(jnp.mean(centered * centered, axis=1, keepdims=True) + epsilon)
        norm_ref[rows] = ((centered * scale) * gain_row[...]).astype(bf16)

    for copy in weight_loads:
        copy.wait()

    z_copies = [combine(0, y_copies[0])]
    y_copies.append(place(3))

    @pl.loop(0, 1024, step=256)
    def _(row):
        rows = pl.ds(pl.multiple_of(row, 256), 256)
        wide = pl.ds(pl.multiple_of(row + 16, 16), 256)
        lin = contract_last(norm_ref[rows], pair_ref[...])
        value_0, gate_0, value_1 = (lin[:, :128], lin[:, 128:256], lin[:, 256:])
        sig_0 = jax.nn.sigmoid(gate_0)
        sig_1 = jax.nn.sigmoid(pltpu.roll(value_1, 64, 1))
        lin_ref[rows, :128] = value_0
        lin_ref[rows, 128:] = value_1
        sig_ref[rows, :128] = sig_0
        sig_ref[rows, 128:] = sig_1
        glu_0[wide] = f32((value_0 * sig_0).astype(bf16))
        glu_1[wide] = f32((value_1 * sig_1).astype(bf16))

    for at, first in ((0, 16), (1, 1024)):
        edge_out[at, :, :128] = glu_0[first : first + 16].astype(bf16)
        edge_out[at, :, 128:] = glu_1[first : first + 16].astype(bf16)
    edges = (
        net.send(edge_out.at[0], edge_in.at[1], frame_peer(-1)),
        net.send(edge_out.at[1], edge_in.at[0], frame_peer(1)),
    )

    z_copies.append(combine(1, y_copies[1]))
    y_copies.append(place(4))
    z_passed = [forward(0, z_copies[0])]

    @pl.loop(0, 128, step=32)
    def _(row):
        rows = pl.ds(pl.multiple_of(row, 32), 32)
        cells = f32(frames_ref[pl.ds(pl.multiple_of(te * 128 + row, 32), 32)])
        centered = cells - jnp.mean(cells, axis=1, keepdims=True)
        scale = lax.rsqrt(jnp.mean(centered * centered, axis=1, keepdims=True) + epsilon)
        own_normed[rows] = centered * scale
        own_scale[rows] = jnp.broadcast_to(scale, (32, 128))

    taps[...] = jnp.zeros(taps.shape, jnp.float32)
    taps[:KERNEL, :192] = f32(taps_ref[...])
    last_ref[192:] = jnp.zeros((64, 1536), bf16)
    tap_sums[...] = jnp.zeros(tap_sums.shape, jnp.float32)
    ends = [lengths_ref[0, 0]]
    for at in range(1, 22):
        ends.append(ends[-1] + lengths_ref[0, at])

    @pl.loop(0, 1024, step=64)
    def _(row):
        rows = pl.ds(pl.multiple_of(row, 64), 64)
        at = lax.broadcasted_iota(jnp.int32, (64, 128), 0) + (tm * 1024 + row)
        end, start = (jnp.full((64, 128), 16384, jnp.int32), jnp.zeros((64, 128), jnp.int32))
        for bound in ends:
            past = at >= bound
            start = jnp.where(past, bound, start)
            end = jnp.where(past, end, jnp.minimum(end, bound))
        ahead_ref[rows] = end - 1 - at
        behind_ref[rows] = at - start

    for at, first in ((0, 0), (1, 1040)):
        edges[1 - at].wait_recv()
        glu_0[first : first + 16] = f32(edge_in[at, :, :128])
        glu_1[first : first + 16] = f32(edge_in[at, :, 128:])

    def nearby(ahead, behind, off):
        return ahead >= off if off > 0 else behind >= -off

    @pl.loop(0, 1024, step=32)
    def _(row):
        rows = pl.ds(pl.multiple_of(row, 32), 32)
        ahead, behind = (ahead_ref[rows], behind_ref[rows])
        total_0 = jnp.zeros((32, 128), jnp.float32)
        total_1 = jnp.zeros((32, 128), jnp.float32)
        for k in range(KERNEL):
            off = k - KERNEL // 2
            near = nearby(ahead, behind, off)
            shifted = pl.ds(row + 16 + off, 32)
            total_0 = total_0 + taps[k : k + 1, :128] * jnp.where(near, glu_0[shifted], 0.0)
            total_1 = total_1 + taps[k : k + 1, 128:] * jnp.where(near, glu_1[shifted], 0.0)
        conv_ref[rows, :128] = total_0
        conv_ref[rows, 128:] = total_1
        swish_ref[rows, :128] = (total_0 * jax.nn.sigmoid(total_0)).astype(bf16)
        swish_ref[rows, 128:] = (total_1 * jax.nn.sigmoid(total_1)).astype(bf16)

    out_load.wait()
    x_copies, last = ([], [])
    for c in range(2, count + 4):
        if c < count:
            z_copies.append(combine(c, y_copies[c]))
            if len(y_copies) < count:
                y_copies.append(place(len(y_copies)))
        if c - 1 < count:
            z_passed.append(forward(c - 1, z_copies[c - 1]))
        if c - 2 < count:
            x_copies.append(spread(c - 2, z_passed[c - 2]))
        if 0 <= c - 3 < count:
            last.append(relay(c - 3, x_copies[c - 3]))
        if 0 <= c - 4 < count:
            project(c - 4, last[c - 4])

    @pl.loop(0, 1024, step=64)
    def _(row):
        rows = pl.ds(pl.multiple_of(row, 64), 64)
        wide = pl.ds(pl.multiple_of(row + 16, 16), 64)
        conv = conv_ref[rows]
        sig = jax.nn.sigmoid(conv)
        cot = cot_ref[rows] * sig * (1.0 + conv * (1.0 - sig))
        cot_0[wide] = cot[:, :128]
        cot_1[wide] = cot[:, 128:]

    for at, first in ((0, 16), (1, 1024)):
        far_out[at, :, :128] = cot_0[first : first + 16]
        far_out[at, :, 128:] = cot_1[first : first + 16]
    edges = (
        net.send(far_out.at[0], far_in.at[1], frame_peer(-1)),
        net.send(far_out.at[1], far_in.at[0], frame_peer(1)),
    )

    over_frames = (((0,), (0,)), ((), ()))
    lower, upper = (pl.ds(0, 2), pl.ds(2, 2))
    y_next, y_last, y_far = ((y + 1) % 4, (y + 3) % 4, (y + 2) % 4)
    x_next, x_last, x_far = ((x + 1) % 4, (x + 3) % 4, (x + 2) % 4)

    def begin_y(ref, a, b, plus, minus):
        first = (
            net.send(ref.at[lower, y_far], a, y_peer(1)),
            net.send(ref.at[upper, y_far], b, y_peer(-1)),
        )
        plain = (
            net.send(ref.at[upper, y_next], plus.at[upper], y_peer(1)),
            net.send(ref.at[lower, y_last], minus.at[lower], y_peer(-1)),
        )
        return first, plain

    def pass_y(begun, ref, a, b, plus, minus):
        first, plain = begun
        first[0].wait_recv()
        for i in range(2):
            a[i] = (f32(a[i]) + f32(ref[i, y_next])).astype(bf16)
        one = net.send(a, plus.at[lower], y_peer(1))
        first[1].wait_recv()
        for i in range(2):
            b[i] = (f32(b[i]) + f32(ref[i + 2, y_last])).astype(bf16)
        return plain + (one, net.send(b, minus.at[upper], y_peer(-1)))

    def begin_z(passed, ref, plus, minus, mid, z_in_ref):
        for copy in passed:
            copy.wait_recv()
        for i in range(4):
            total = (f32(ref[i, y]) + f32(plus[i]) + f32(minus[i])).astype(bf16)
            mid[2 * i] = total[:48]
            mid[2 * i + 1] = total[48:]
        z_in_ref[z] = mid[z]
        return [
            net.send(mid.at[(z + k) % 8], z_in_ref.at[z], z_peer(k)) for k in (4, 3, 5, 2, 6, 1, 7)
        ]

    def end_z(copies, z_in_ref):
        for copy in copies:
            copy.wait_recv()
        total = f32(z_in_ref[0])
        for at in range(1, 8):
            total = total + f32(z_in_ref[at])
        return total * factor

    @pl.loop(0, 4)
    def _(at):
        cols = pl.ds(pl.multiple_of(at * 384, 128), 384)
        term = lax.dot_general(
            full_ref[:, :, :, cols].reshape(1024, 384),
            swish_ref[...],
            over_frames,
            preferred_element_type=jnp.float32,
        ).astype(bf16)
        for k in range(4):
            out_ref[at, k] = term[96 * k : 96 * k + 96]

    out_set = (out_a, out_b, out_plus, out_minus)
    wide_set = (wide_a, wide_b, wide_plus, wide_minus)
    tail_set = (tail_a, tail_b, tail_plus, tail_minus)
    out_begun = begin_y(out_ref, *out_set)

    for at, first in ((0, 0), (1, 1040)):
        edges[1 - at].wait_recv()
        cot_0[first : first + 16] = far_in[at, :, :128]
        cot_1[first : first + 16] = far_in[at, :, 128:]

    def back(row, lanes, cot, glu):
        rows = pl.ds(pl.multiple_of(row, 32), 32)
        wide = pl.ds(pl.multiple_of(row + 16, 16), 32)
        ahead, behind = (ahead_ref[rows], behind_ref[rows])
        here = cot[wide]
        total = jnp.zeros((32, 128), jnp.float32)
        for k in range(KERNEL):
            off = k - KERNEL // 2
            near = nearby(ahead, behind, off)
            shifted = pl.ds(row + 16 + off, 32)
            m = KERNEL - 1 - k
            total = total + taps[m : m + 1, lanes] * jnp.where(near, cot[shifted], 0.0)
            term = here * jnp.where(near, glu[shifted], 0.0)
            tap_sums[k, :, lanes] += jnp.sum(term.reshape(4, 8, 128), axis=0)
        value, sig = (lin_ref[rows, lanes], sig_ref[rows, lanes])
        return rows, total * sig, total * value * sig * (1.0 - sig)

    @pl.loop(0, 1024, step=32)
    def _(row):
        rows, value_cot, gate_cot = back(row, slice(0, 128), cot_0, glu_0)
        both_cot[rows, :128] = value_cot.astype(bf16)
        both_cot[rows, 128:256] = gate_cot.astype(bf16)

    out_passed = pass_y(out_begun, out_ref, *out_set)

    @pl.loop(0, 4)
    def _(at):
        cols = pl.ds(pl.multiple_of(at * 384, 128), 384)
        term = lax.dot_general(
            norm_ref[:, cols],
            both_cot[:, :256],
            over_frames,
            preferred_element_type=jnp.float32,
        ).astype(bf16)
        for k in range(4):
            wide_ref[at, k] = term[96 * k : 96 * k + 96]

    wide_begun = begin_y(wide_ref, *wide_set)

    def back_tail(row):
        rows, value_cot, gate_cot = back(row, slice(128, 256), cot_1, glu_1)
        both_cot[rows, 256:] = (value_cot + pltpu.roll(gate_cot, 64, 1)).astype(bf16)

    @pl.loop(0, 512, step=32)
    def _(row):
        back_tail(row)

    out_z_copies = begin_z(out_passed, out_ref, out_plus, out_minus, out_mid, out_z)

    @pl.loop(512, 1024, step=32)
    def _(row):
        back_tail(row)

    wide_passed = pass_y(wide_begun, wide_ref, *wide_set)
    kern_ref[...] = jnp.zeros(kern_ref.shape, jnp.float32)
    for k in range(KERNEL):
        kern_ref[k : k + 1] = jnp.sum(tap_sums[k], axis=0, keepdims=True)
    kern_y[y] = kern_ref[...]
    kern_copies = [net.send(kern_ref, kern_y.at[y], y_peer(k)) for k in (2, 1, 3)]

    def shares(refs, copies):
        for copy in copies:
            copy.wait_recv()
        total = refs[0]
        for at in range(1, refs.shape[0]):
            total = total + refs[at]
        return total

    gain_sums[...] = jnp.zeros(gain_sums.shape, jnp.float32)
    core_copies = []

    def norm_part(at):
        first, size = HALVES[at]

        @pl.loop(first, first + size, step=256)
        def _(col):
            cols = pl.ds(pl.multiple_of(col, 256), 256)
            for row in (0, 512):
                part = jnp.dot(
                    both_cot[row : row + 512],
                    pair_ref[:, cols],
                    preferred_element_type=jnp.float32,
                )
                gain_sums[:, cols] += jnp.sum(
                    (part * f32(norm_ref[row : row + 512, cols])).reshape(64, 8, 256), axis=0
                )
                part = part.astype(bf16)
                for k in range(4):
                    part_ref[row // 256 + k // 2, k % 2, :, cols] = part[128 * k : 128 * k + 128]

        cols = pl.ds(first, size)
        core_copies.append(
            net.send(part_ref.at[:, 1 - core, :, cols], core_in.at[:, :, cols], sibling())
        )

    def begin_x(at):
        core_copies[at].wait_recv()
        first, size = HALVES[at]
        cols = pl.ds(first, size)

        def add_core(to):
            @pl.loop(0, 128, step=32)
            def _(row):
                rows = pl.ds(pl.multiple_of(row, 32), 32)
                chip_sum[to, rows, cols] = (
                    f32(part_ref[to, core, rows, cols]) + f32(core_in[to, rows, cols])
                ).astype(bf16)

        add_core(x_far)
        begun = (
            net.send(chip_sum.at[x_far, half_a, cols], x_a.at[:, cols], x_peer(1)),
            net.send(chip_sum.at[x_far, half_b, cols], x_b.at[:, cols], x_peer(-1)),
        )
        add_core(x_next)
        add_core(x_last)
        plain = (
            net.send(chip_sum.at[x_next, half_b, cols], x_plus.at[half_b, cols], x_peer(1)),
            net.send(chip_sum.at[x_last, half_a, cols], x_minus.at[half_a, cols], x_peer(-1)),
        )
        return begun, plain

    def pass_x(at, pending):
        begun, plain = pending
        first, size = HALVES[at]
        cols = pl.ds(first, size)

        def add_x(ref, to, start):
            @pl.loop(0, 64, step=32)
            def _(row):
                rows = pl.ds(pl.multiple_of(row, 32), 32)
                other = pl.ds(pl.multiple_of(row + start, 32), 32)
                ref[rows, cols] = (f32(ref[rows, cols]) + f32(chip_sum[to, other, cols])).astype(
                    bf16
                )

        begun[0].wait_recv()
        add_x(x_a, x_next, 0)
        one = net.send(x_a.at[:, cols], x_plus.at[half_a, cols], x_peer(1))
        begun[1].wait_recv()
        add_x(x_b, x_last, 64)
        return plain + (one, net.send(x_b.at[:, cols], x_minus.at[half_b, cols], x_peer(-1)))

    norm_part(0)
    norm_part(1)
    x_begun = [begin_x(0)]

    gain_ref_in = jnp.sum(gain_sums[...], axis=0, keepdims=True) / gain_row[...]
    gain_out[...] = jnp.zeros(gain_out.shape, jnp.float32)
    for k in range(6):
        gain_out[k : k + 1] = gain_ref_in[:, 256 * k : 256 * k + 256]
    gain_in[te] = gain_out[...]
    gain_copies = [net.send(gain_out, gain_in.at[te], t_peer(k)) for k in range(1, 8)]
    x_begun.append(begin_x(1))

    @pl.loop(0, 4)
    def _(at):
        cols = pl.ds(pl.multiple_of(at * 384, 128), 384)
        term = lax.dot_general(
            norm_ref[:, cols],
            both_cot[:, 256:],
            over_frames,
            preferred_element_type=jnp.float32,
        ).astype(bf16)
        for k in range(4):
            tail_ref[at, k] = term[96 * k : 96 * k + 96]

    tail_begun = begin_y(tail_ref, *tail_set)
    kern_mid[...] = shares(kern_y, kern_copies)
    kern_z[z] = kern_mid[...]
    kern_copies = [net.send(kern_mid, kern_z.at[z], z_peer(k)) for k in (4, 3, 5, 2, 6, 1, 7)]
    wide_z_copies = begin_z(wide_passed, wide_ref, wide_plus, wide_minus, wide_mid, wide_z)
    gain_mid[...] = shares(gain_in, gain_copies)
    gain_y[y] = gain_mid[...]
    gain_copies = [net.send(gain_mid, gain_y.at[y], y_peer(k)) for k in (2, 1, 3)]
    x_passed = [pass_x(0, x_begun[0])]
    tail_passed = pass_y(tail_begun, tail_ref, *tail_set)
    x_passed.append(pass_x(1, x_begun[1]))
    gain_last[...] = shares(gain_y, gain_copies)
    gain_z[z] = gain_last[...]
    gain_copies = [net.send(gain_last, gain_z.at[z], z_peer(k)) for k in (4, 3, 5, 2, 6, 1, 7)]
    tail_z_copies = begin_z(tail_passed, tail_ref, tail_plus, tail_minus, tail_mid, tail_z)

    out_sum[...] = end_z(out_z_copies, out_z)
    wide_sum[...] = end_z(wide_z_copies, wide_z)
    small_sum[pl.ds(0, 32), :] = shares(kern_z, kern_copies) * factor

    for copies in x_passed:
        for copy in copies:
            copy.wait_recv()

    @pl.loop(0, 8)
    def _(block):
        rows = pl.ds(pl.multiple_of(block * 16, 16), 16)
        summed = (
            f32(part_ref[x, core, rows])
            + f32(core_in[x, rows])
            + f32(x_plus[rows])
            + f32(x_minus[rows])
        )
        normed = own_normed[rows]
        scaled = summed * gain_row[...]
        input_grad[rows] = (
            f32(full_ref[te, block])
            + own_scale[rows, :1]
            * (
                scaled
                - jnp.mean(scaled, axis=1, keepdims=True)
                - normed * jnp.mean(scaled * normed, axis=1, keepdims=True)
            )
        ).astype(bf16)

    tail_sum[...] = end_z(tail_z_copies, tail_z)
    small_sum[pl.ds(32, 8), :] = shares(gain_z, gain_copies) * factor
    net.finish()


def joint_call(table, lengths, frames, blocks, value_weight, gate_weight, out_weight, taps, gain):
    count, width = frames.shape
    span = value_weight.shape[0]
    bf16, single = (jnp.bfloat16, jnp.float32)
    vmem = pl.BlockSpec(memory_space=pltpu.VMEM)
    smem = pl.BlockSpec(memory_space=pltpu.SMEM)
    where = pl.BlockSpec(memory_space=pl.ANY)

    def weight_scratch(lanes):
        return [
            pltpu.VMEM((4, 4, 96, lanes), bf16),
            pltpu.VMEM((2, 96, lanes), bf16),
            pltpu.VMEM((2, 96, lanes), bf16),
            pltpu.VMEM((4, 96, lanes), bf16),
            pltpu.VMEM((4, 96, lanes), bf16),
            pltpu.VMEM((8, 48, lanes), bf16),
            pltpu.VMEM((8, 48, lanes), bf16),
        ]

    return pl.pallas_call(
        joint_kernel,
        out_shape=(
            jax.ShapeDtypeStruct((128, width), bf16),
            jax.ShapeDtypeStruct((48, 256), single),
            jax.ShapeDtypeStruct((48, 128), single),
            jax.ShapeDtypeStruct((48, 256), single),
            jax.ShapeDtypeStruct((40, 256), single),
        ),
        in_specs=[smem] * 2 + [where] * 5 + [vmem] * 2,
        out_specs=[vmem] * 5,
        scratch_shapes=[
            pltpu.VMEM((count, width), bf16),
            pltpu.VMEM((2 * span, width), bf16),
            pltpu.VMEM((256, width), bf16),
            pltpu.VMEM((32, 256), single),
            pltpu.VMEM((count, 128), jnp.int32),
            pltpu.VMEM((count, 128), jnp.int32),
            pltpu.VMEM((count, width), bf16),
            pltpu.VMEM((count, 256), single),
            pltpu.VMEM((count, 256), single),
            pltpu.VMEM((count, 256), single),
            pltpu.VMEM((count + 32, 128), single),
            pltpu.VMEM((count + 32, 128), single),
            pltpu.VMEM((8, 8, 16, width), bf16),
            pltpu.VMEM((count, 256), bf16),
            pltpu.VMEM((count, 256), single),
            pltpu.VMEM((count + 32, 128), single),
            pltpu.VMEM((count + 32, 128), single),
            pltpu.VMEM((count, 2 * span), bf16),
            pltpu.VMEM((KERNEL, 8, 256), single),
            pltpu.VMEM((8, width), single),
            pltpu.VMEM((512, 4 * SLOTS), bf16),
            pltpu.VMEM((2, 16, 256), bf16),
            pltpu.VMEM((2, 16, 256), bf16),
            pltpu.VMEM((2, 16, 256), single),
            pltpu.VMEM((2, 16, 256), single),
            pltpu.VMEM((4, 2, 128, width), bf16),
            pltpu.VMEM((4, 128, width), bf16),
            pltpu.VMEM((4, 128, width), bf16),
            pltpu.VMEM((64, width), bf16),
            pltpu.VMEM((64, width), bf16),
            pltpu.VMEM((128, width), bf16),
            pltpu.VMEM((128, width), bf16),
        ]
        + weight_scratch(256)
        + weight_scratch(128)
        + weight_scratch(256)
        + [
            pltpu.VMEM((1, width), single),
            pltpu.VMEM((128, width), single),
            pltpu.VMEM((128, 128), single),
            pltpu.VMEM((32, 256), single),
            pltpu.VMEM((4, 32, 256), single),
            pltpu.VMEM((32, 256), single),
            pltpu.VMEM((8, 32, 256), single),
            pltpu.VMEM((8, 256), single),
            pltpu.VMEM((8, 8, 256), single),
            pltpu.VMEM((8, 256), single),
            pltpu.VMEM((4, 8, 256), single),
            pltpu.VMEM((8, 256), single),
            pltpu.VMEM((8, 8, 256), single),
            pltpu.SemaphoreType.DMA((len(CHUNKS) + 6,)),
            pltpu.SemaphoreType.DMA((COPIES,)),
            pltpu.SemaphoreType.DMA((COPIES,)),
        ]
        + [pltpu.VMEM((3, SLOTS, size), bf16) for _, size in CHUNKS]
        + [pltpu.VMEM((4, SLOTS, size), bf16) for _, size in CHUNKS]
        + [pltpu.VMEM((4, 128, size), bf16) for _, size in CHUNKS]
        + [pltpu.VMEM((2, 128, size), bf16) for _, size in CHUNKS]
        + [pltpu.VMEM((64, 16, size), bf16) for _, size in CHUNKS]
        + [pltpu.VMEM((2, 64, size), bf16) for _, size in CHUNKS],
        compiler_params=pltpu.CompilerParams(
            collective_id=0, has_side_effects=True, vmem_limit_bytes=60 * 1024 * 1024
        ),
        name="joint",
    )(table, lengths, frames, blocks, value_weight, gate_weight, out_weight, taps, gain)


def finish_kernel(
    input_ref,
    wide_ref,
    tail_ref,
    out_ref,
    small_ref,
    input_grad,
    value_grad,
    gate_grad,
    out_grad,
    kernel_grad,
    gain_grad,
):
    input_grad[...] = input_ref[...]
    tail = tail_ref[...]
    value_grad[:, :128] = wide_ref[:, :128]
    value_grad[:, 128:] = tail[:, :64]
    gate_grad[:, :128] = wide_ref[:, 128:]
    gate_grad[:, 128:] = pltpu.roll(tail, 64, 1)[:, :64]
    out_grad[...] = out_ref[:, :192]
    kernel_grad[...] = small_ref[:KERNEL, :192]
    for k in range(6):
        gain_grad[256 * k : 256 * k + 256] = small_ref[32 + k]


def finish_call(*sums):
    single = jnp.float32
    width = sums[0].shape[1]
    vmem = pl.BlockSpec(memory_space=pltpu.VMEM)
    return pl.pallas_call(
        finish_kernel,
        out_shape=(jax.ShapeDtypeStruct(sums[0].shape, jnp.bfloat16),)
        + (jax.ShapeDtypeStruct((48, 192), single),) * 3
        + (
            jax.ShapeDtypeStruct((KERNEL, 192), single),
            jax.ShapeDtypeStruct((width,), single),
        ),
        in_specs=[vmem] * 5,
        out_specs=[vmem] * 6,
        name="finish",
    )(*sums)


def routing(block_device, block_sub, block_rows):
    tm, te, dp = places()
    first = (tm // 4) * 4
    code = block_device.reshape(1, 1024) + 16 * block_sub + 128 * block_rows
    code = code.reshape(16, 64)
    near = lax.dynamic_slice_in_dim(code, first, 4, 0)
    devices, subs = (near % 16, (near // 16) % 8)
    counts = lax.dynamic_slice_in_dim(code, tm, 1, 0) // 128
    earlier = jnp.arange(64)[:, None] > jnp.arange(64)[None, :]
    column = devices % 4
    same = (column[:, :, None] == column[:, None, :]) & earlier[None]
    rank = jnp.sum(same.astype(jnp.int32), axis=2)
    slot = column * 20 + rank
    own = lax.dynamic_slice_in_dim(slot, tm % 4, 1, 0)
    own_hot = own == jnp.arange(80, dtype=jnp.int32)[:, None]
    source = jnp.sum(jnp.where(own_hot, jnp.arange(64, dtype=jnp.int32)[None], 0), axis=1)
    live = jnp.sum(jnp.where(own_hot, jnp.clip(counts - te * 16, 0, 16), 0), axis=1)
    place = (tm % 4) * 20 + jnp.arange(20, dtype=jnp.int32)
    hot = slot[:, None, :] == place[None, :, None]
    block = (devices // 4) * 8 + subs
    dest = jnp.sum(jnp.where(hot, block[:, None, :] + 1, 0), axis=2).reshape(80) - 1
    return jnp.concatenate([source, live, jnp.where(dest < 0, 64, dest)])


def on_device(
    inputs,
    grad_blocks,
    block_device,
    block_sub,
    block_rows,
    seg_lengths,
    value_weight,
    gate_weight,
    out_weight,
    conv_kernel,
    norm_gain,
):
    sums = joint_call(
        routing(block_device, block_sub, block_rows),
        seg_lengths,
        inputs[0],
        grad_blocks[0],
        value_weight,
        gate_weight,
        out_weight,
        conv_kernel,
        norm_gain,
    )
    input_grad, value_grad, gate_grad, out_grad, kernel_grad, gain_grad = finish_call(*sums)
    return (
        input_grad[None],
        value_grad.T,
        gate_grad.T,
        out_grad.T,
        kernel_grad,
        gain_grad,
    )


def solution(mesh):
    in_specs = (
        P("dp", "tm", None),
        P("dp", "tm", "tensor", None),
        P("dp", None, None),
        P("dp", None),
        P("dp", None),
        P("dp", None),
        P("tensor", None),
        P("tensor", None),
        P("tensor", None),
        P(None, "tensor"),
        P(),
    )
    out_specs = (
        P("dp", ("tm", "tensor"), None),
        P("tensor", ("tm", "dp")),
        P("tensor", ("tm", "dp")),
        P("tensor", ("tm", "dp")),
        P(None, "tensor"),
        P(),
    )
    return jax.shard_map(
        on_device, mesh=mesh, in_specs=in_specs, out_specs=out_specs, check_vma=False
    )
```

```python
import math

import jax
import jax.numpy as jnp
from jax import lax
from jax.experimental import pallas as pl
from jax.experimental.pallas import tpu as pltpu
from jax.sharding import PartitionSpec as P

KERNEL = 31


epsilon = 1e-05


def contract_last(left, right):
    return lax.dot_general(
        left, right, (((1,), (1,)), ((), ())), preferred_element_type=jnp.float32
    )


def places():
    tm, te, dp = (lax.axis_index("tm"), lax.axis_index("tensor"), lax.axis_index("dp"))
    return tm, te, dp


def y_peer(step):
    tm, te, dp = places()
    return {"tm": (tm // 4) * 4 + (tm + step) % 4, "tensor": te, "dp": dp}


def z_peer(step):
    tm, te, dp = places()
    there = ((tm // 4) * 2 + dp + step) % 8
    return {"tm": (there // 2) * 4 + tm % 4, "tensor": te, "dp": there % 2}


def t_peer(step):
    tm, te, dp = places()
    return {"tm": tm, "tensor": (te + step) % 8, "dp": dp}


def x_peer(step):
    tm, te, dp = places()
    return {"tm": tm, "tensor": (te + 2 * step) % 8, "dp": dp}


def sibling():
    tm, te, dp = places()
    return {"tm": tm, "tensor": (te // 2) * 2 + 1 - te % 2, "dp": dp}


class Copies:
    def __init__(self, send_sems, recv_sems):
        self.send_sems, self.recv_sems = send_sems, recv_sems
        self.made = []

    def send(self, src, dst, to):
        at = len(self.made)
        copy = pltpu.make_async_remote_copy(
            src_ref=src,
            dst_ref=dst,
            send_sem=self.send_sems.at[at],
            recv_sem=self.recv_sems.at[at],
            device_id=to,
            device_id_type=pl.DeviceIdType.MESH,
        )
        copy.start()
        self.made.append(copy)
        return copy

    def finish(self):
        for copy in self.made:
            copy.wait_send()


def meet(peers):
    barrier = pltpu.get_barrier_semaphore()
    for peer in peers:
        pl.semaphore_signal(
            barrier, inc=1, device_id=peer, device_id_type=pl.DeviceIdType.MESH
        )
    pl.semaphore_wait(barrier, len(peers))


def f32(value):
    return value.astype(jnp.float32)


def frame_peer(step):
    tm, te, dp = places()
    return {"tm": (tm + step) % 16, "tensor": te, "dp": dp}


CHUNKS = tuple((first, 256) for first in range(0, 1536, 256))
HALVES = ((0, 768), (768, 768))
SLOTS = 320
COPIES = 16 * len(CHUNKS) + 4 + 7 * len(HALVES) + 18 + 21 + 7 + 3 + 7 + 3 + 7


def joint_kernel(
    table_ref,
    lengths_ref,
    frames_hbm,
    blocks_hbm,
    value_hbm,
    gate_hbm,
    out_hbm,
    taps_ref,
    gain_ref,
    input_grad,
    wide_sum,
    tail_sum,
    out_sum,
    small_sum,
    frames_ref,
    pair_ref,
    last_ref,
    taps,
    ahead_ref,
    behind_ref,
    norm_ref,
    lin_ref,
    sig_ref,
    conv_ref,
    glu_0,
    glu_1,
    full_ref,
    swish_ref,
    cot_ref,
    cot_0,
    cot_1,
    both_cot,
    tap_sums,
    gain_sums,
    summing,
    edge_out,
    edge_in,
    far_out,
    far_in,
    part_ref,
    core_in,
    chip_sum,
    x_a,
    x_b,
    x_plus,
    x_minus,
    wide_ref,
    wide_a,
    wide_b,
    wide_plus,
    wide_minus,
    wide_mid,
    wide_z,
    tail_ref,
    tail_a,
    tail_b,
    tail_plus,
    tail_minus,
    tail_mid,
    tail_z,
    out_ref,
    out_a,
    out_b,
    out_plus,
    out_minus,
    out_mid,
    out_z,
    gain_row,
    own_normed,
    own_scale,
    kern_ref,
    kern_y,
    kern_mid,
    kern_z,
    gain_out,
    gain_in,
    gain_mid,
    gain_y,
    gain_last,
    gain_z,
    load_sems,
    send_sems,
    recv_sems,
    *rest,
):
    count = len(CHUNKS)
    y_out, y_in = (rest[:count], rest[count : 2 * count])
    z_out, z_in = (rest[2 * count : 3 * count], rest[3 * count : 4 * count])
    blocks, z_pass = (rest[4 * count : 5 * count], rest[5 * count :])
    tm, te, dp = places()
    y, zh, z = (tm % 4, tm // 4, (tm // 4) * 2 + dp)
    x, core = (te // 2, te % 2)
    bf16 = jnp.bfloat16
    factor = 1.0 / math.sqrt(32768.0)
    columns = [pl.ds(first, size) for first, size in CHUNKS]
    half_a, half_b = (pl.ds(0, 64), pl.ds(64, 64))
    zh_next, zh_last, zh_far = ((zh + 1) % 4, (zh + 3) % 4, (zh + 2) % 4)

    for k in range(6):
        gain_row[:, 256 * k : 256 * k + 256] = gain_ref[256 * k : 256 * k + 256].reshape(1, 256)
    loads = []

    def load(src, dst):
        copy = pltpu.make_async_copy(src, dst, load_sems.at[len(loads)])
        copy.start()
        loads.append(copy)
        return copy

    block_loads = [load(blocks_hbm.at[:, :, columns[c]], blocks[c]) for c in range(count)]
    frames_load = load(frames_hbm, frames_ref)
    weight_loads = [
        load(value_hbm.at[pl.ds(0, 128)], pair_ref.at[pl.ds(0, 128)]),
        load(gate_hbm.at[pl.ds(0, 128)], pair_ref.at[pl.ds(128, 128)]),
        load(value_hbm.at[pl.ds(128, 64)], pair_ref.at[pl.ds(256, 64)]),
        load(gate_hbm.at[pl.ds(128, 64)], pair_ref.at[pl.ds(320, 64)]),
    ]
    out_load = load(out_hbm, last_ref.at[pl.ds(0, 192)])

    meet(
        [t_peer(k) for k in range(1, 8)]
        + [y_peer(k) for k in range(1, 4)]
        + [z_peer(k) for k in range(1, 8)]
        + [frame_peer(1), frame_peer(-1)]
    )
    net = Copies(send_sems, recv_sems)

    def place(c):
        block_loads[c].wait()
        copies = []
        for k in (2, 1, 3, 0):
            first = ((y + k) % 4) * 20
            target = y_in[c].at[y] if k == 0 else y_out[c].at[k - 1]

            @pl.loop(0, 20)
            def _(slot):
                source = table_ref[first + slot]
                live = table_ref[80 + first + slot]
                rows = blocks[c][source]
                ids = lax.broadcasted_iota(jnp.int32, rows.shape, 0)
                target[pl.ds(pl.multiple_of(slot * 16, 16), 16)] = jnp.where(
                    ids < live, f32(rows), 0.0
                ).astype(bf16)

            if k:
                copies.append(net.send(target, y_in[c].at[y], y_peer(k)))
        return copies

    def combine(c, copies):
        for copy in copies:
            copy.wait_recv()
        width = CHUNKS[c][1]

        @pl.loop(0, width, step=256)
        def _(col):
            cols = pl.ds(pl.multiple_of(col, 256), 256)
            total = jnp.dot(
                summing[...],
                y_in[c][:, :, cols].reshape(4 * SLOTS, 256),
                preferred_element_type=jnp.float32,
            ).astype(bf16)
            for at in range(4):
                z_out[c][at, :, cols] = total[128 * at : 128 * at + 128]

        sums, passing = (z_out[c], z_pass[c])
        return (
            net.send(sums.at[zh_far, half_a], passing.at[0], z_peer(2)),
            net.send(sums.at[zh_far, half_b], passing.at[1], z_peer(-2)),
            net.send(sums.at[zh_next, half_b], z_in[c].at[0, half_b], z_peer(2)),
            net.send(sums.at[zh_last, half_a], z_in[c].at[1, half_a], z_peer(-2)),
        )

    def forward(c, copies):
        sums, passing = (z_out[c], z_pass[c])
        copies[0].wait_recv()
        passing[0] = (f32(passing[0]) + f32(sums[zh_next, half_a])).astype(bf16)
        one = net.send(passing.at[0], z_in[c].at[0, half_a], z_peer(2))
        copies[1].wait_recv()
        passing[1] = (f32(passing[1]) + f32(sums[zh_last, half_b])).astype(bf16)
        return copies[2:] + (one, net.send(passing.at[1], z_in[c].at[1, half_b], z_peer(-2)))

    def spread(c, copies):
        for copy in copies:
            copy.wait_recv()
        total = (f32(z_out[c][zh]) + f32(z_in[c][0]) + f32(z_in[c][1])).astype(bf16)
        for block in range(8):
            full_ref[block, te, :, columns[c]] = total[16 * block : 16 * block + 16]
        own = full_ref.at[:, te, :, columns[c]]
        return [net.send(own, own, x_peer(k)) for k in (2, 1, 3)], [
            net.send(own, own, sibling())
        ]

    def relay(c, copies):
        for k, copy in zip((2, 1, 3), copies[0]):
            copy.wait_recv()
            there = full_ref.at[:, (te + 8 - 2 * k) % 8, :, columns[c]]
            copies[1].append(net.send(there, there, sibling()))
        return copies[1]

    def project(c, copies):
        for copy in copies:
            copy.wait_recv()

        @pl.loop(0, 8, step=4)
        def _(block):
            rows = pl.ds(pl.multiple_of(block * 128, 512), 512)
            term = contract_last(
                full_ref[pl.ds(block, 4), :, :, columns[c]].reshape(512, CHUNKS[c][1]),
                last_ref[:, columns[c]],
            )
            if c == 0:
                cot_ref[rows] = term
            else:
                cot_ref[rows] += term

    y_copies = [place(0), place(1)]

    @pl.loop(0, 10)
    def _(group):
        tiles = []
        for k in range(8):
            at = table_ref[160 + group * 8 + k] * 16
            gap = lax.broadcasted_iota(jnp.int32, (16, 512), 1) - lax.broadcasted_iota(
                jnp.int32, (16, 512), 0
            )
            tiles.append(jnp.where(gap == at, 1.0, 0.0))
        cols = pl.ds(pl.multiple_of(group * 128, 128), 128)
        summing[:, cols] = jnp.concatenate(tiles, axis=0).T.astype(bf16)

    frames_load.wait()

    @pl.loop(0, 1024, step=32)
    def _(row):
        rows = pl.ds(pl.multiple_of(row, 32), 32)
        cells = f32(frames_ref[rows])
        centered = cells - jnp.mean(cells, axis=1, keepdims=True)
        scale = lax.rsqrt(jnp.mean(centered * centered, axis=1, keepdims=True) + epsilon)
        norm_ref[rows] = ((centered * scale) * gain_row[...]).astype(bf16)

    for copy in weight_loads:
        copy.wait()

    z_copies = [combine(0, y_copies[0])]
    y_copies.append(place(2))

    @pl.loop(0, 1024, step=256)
    def _(row):
        rows = pl.ds(pl.multiple_of(row, 256), 256)
        wide = pl.ds(pl.multiple_of(row + 16, 16), 256)
        lin = contract_last(norm_ref[rows], pair_ref[...])
        value_0, gate_0, value_1 = (lin[:, :128], lin[:, 128:256], lin[:, 256:])
        sig_0 = jax.nn.sigmoid(gate_0)
        sig_1 = jax.nn.sigmoid(pltpu.roll(value_1, 64, 1))
        lin_ref[rows, :128] = value_0
        lin_ref[rows, 128:] = value_1
        sig_ref[rows, :128] = sig_0
        sig_ref[rows, 128:] = sig_1
        glu_0[wide] = f32((value_0 * sig_0).astype(bf16))
        glu_1[wide] = f32((value_1 * sig_1).astype(bf16))

    for at, first in ((0, 16), (1, 1024)):
        edge_out[at, :, :128] = glu_0[first : first + 16].astype(bf16)
        edge_out[at, :, 128:] = glu_1[first : first + 16].astype(bf16)
    edges = (
        net.send(edge_out.at[0], edge_in.at[1], frame_peer(-1)),
        net.send(edge_out.at[1], edge_in.at[0], frame_peer(1)),
    )

    z_copies.append(combine(1, y_copies[1]))
    y_copies.append(place(3))
    z_passed = [forward(0, z_copies[0])]

    @pl.loop(0, 128, step=32)
    def _(row):
        rows = pl.ds(pl.multiple_of(row, 32), 32)
        cells = f32(frames_ref[pl.ds(pl.multiple_of(te * 128 + row, 32), 32)])
        centered = cells - jnp.mean(cells, axis=1, keepdims=True)
        scale = lax.rsqrt(jnp.mean(centered * centered, axis=1, keepdims=True) + epsilon)
        own_normed[rows] = centered * scale
        own_scale[rows] = jnp.broadcast_to(scale, (32, 128))

    taps[...] = jnp.zeros(taps.shape, jnp.float32)
    taps[:KERNEL, :192] = f32(taps_ref[...])
    last_ref[192:] = jnp.zeros((64, 1536), bf16)
    tap_sums[...] = jnp.zeros(tap_sums.shape, jnp.float32)
    ends = [lengths_ref[0, 0]]
    for at in range(1, 22):
        ends.append(ends[-1] + lengths_ref[0, at])

    @pl.loop(0, 1024, step=64)
    def _(row):
        rows = pl.ds(pl.multiple_of(row, 64), 64)
        at = lax.broadcasted_iota(jnp.int32, (64, 128), 0) + (tm * 1024 + row)
        end, start = (jnp.full((64, 128), 16384, jnp.int32), jnp.zeros((64, 128), jnp.int32))
        for bound in ends:
            past = at >= bound
            start = jnp.where(past, bound, start)
            end = jnp.where(past, end, jnp.minimum(end, bound))
        ahead_ref[rows] = end - 1 - at
        behind_ref[rows] = at - start

    for at, first in ((0, 0), (1, 1040)):
        edges[1 - at].wait_recv()
        glu_0[first : first + 16] = f32(edge_in[at, :, :128])
        glu_1[first : first + 16] = f32(edge_in[at, :, 128:])

    def nearby(ahead, behind, off):
        return ahead >= off if off > 0 else behind >= -off

    @pl.loop(0, 1024, step=32)
    def _(row):
        rows = pl.ds(pl.multiple_of(row, 32), 32)
        ahead, behind = (ahead_ref[rows], behind_ref[rows])
        total_0 = jnp.zeros((32, 128), jnp.float32)
        total_1 = jnp.zeros((32, 128), jnp.float32)
        for k in range(KERNEL):
            off = k - KERNEL // 2
            near = nearby(ahead, behind, off)
            shifted = pl.ds(row + 16 + off, 32)
            total_0 = total_0 + taps[k : k + 1, :128] * jnp.where(near, glu_0[shifted], 0.0)
            total_1 = total_1 + taps[k : k + 1, 128:] * jnp.where(near, glu_1[shifted], 0.0)
        conv_ref[rows, :128] = total_0
        conv_ref[rows, 128:] = total_1
        swish_ref[rows, :128] = (total_0 * jax.nn.sigmoid(total_0)).astype(bf16)
        swish_ref[rows, 128:] = (total_1 * jax.nn.sigmoid(total_1)).astype(bf16)

    out_load.wait()
    x_copies, last = ([], [])
    for c in range(2, count + 4):
        if c < count:
            z_copies.append(combine(c, y_copies[c]))
            if len(y_copies) < count:
                y_copies.append(place(len(y_copies)))
        if c - 1 < count:
            z_passed.append(forward(c - 1, z_copies[c - 1]))
        if c - 2 < count:
            x_copies.append(spread(c - 2, z_passed[c - 2]))
        if 0 <= c - 3 < count:
            last.append(relay(c - 3, x_copies[c - 3]))
        if 0 <= c - 4 < count:
            project(c - 4, last[c - 4])

    @pl.loop(0, 1024, step=64)
    def _(row):
        rows = pl.ds(pl.multiple_of(row, 64), 64)
        wide = pl.ds(pl.multiple_of(row + 16, 16), 64)
        conv = conv_ref[rows]
        sig = jax.nn.sigmoid(conv)
        cot = cot_ref[rows] * sig * (1.0 + conv * (1.0 - sig))
        cot_0[wide] = cot[:, :128]
        cot_1[wide] = cot[:, 128:]

    for at, first in ((0, 16), (1, 1024)):
        far_out[at, :, :128] = cot_0[first : first + 16]
        far_out[at, :, 128:] = cot_1[first : first + 16]
    edges = (
        net.send(far_out.at[0], far_in.at[1], frame_peer(-1)),
        net.send(far_out.at[1], far_in.at[0], frame_peer(1)),
    )

    over_frames = (((0,), (0,)), ((), ()))
    lower, upper = (pl.ds(0, 2), pl.ds(2, 2))
    y_next, y_last, y_far = ((y + 1) % 4, (y + 3) % 4, (y + 2) % 4)
    x_next, x_last, x_far = ((x + 1) % 4, (x + 3) % 4, (x + 2) % 4)

    def begin_y(ref, a, b, plus, minus):
        first = (
            net.send(ref.at[lower, y_far], a, y_peer(1)),
            net.send(ref.at[upper, y_far], b, y_peer(-1)),
        )
        plain = (
            net.send(ref.at[upper, y_next], plus.at[upper], y_peer(1)),
            net.send(ref.at[lower, y_last], minus.at[lower], y_peer(-1)),
        )
        return first, plain

    def pass_y(begun, ref, a, b, plus, minus):
        first, plain = begun
        first[0].wait_recv()
        for i in range(2):
            a[i] = (f32(a[i]) + f32(ref[i, y_next])).astype(bf16)
        one = net.send(a, plus.at[lower], y_peer(1))
        first[1].wait_recv()
        for i in range(2):
            b[i] = (f32(b[i]) + f32(ref[i + 2, y_last])).astype(bf16)
        return plain + (one, net.send(b, minus.at[upper], y_peer(-1)))

    def begin_z(passed, ref, plus, minus, mid, z_in_ref):
        for copy in passed:
            copy.wait_recv()
        for i in range(4):
            total = (f32(ref[i, y]) + f32(plus[i]) + f32(minus[i])).astype(bf16)
            mid[2 * i] = total[:48]
            mid[2 * i + 1] = total[48:]
        z_in_ref[z] = mid[z]
        return [
            net.send(mid.at[(z + k) % 8], z_in_ref.at[z], z_peer(k)) for k in (4, 3, 5, 2, 6, 1, 7)
        ]

    def end_z(copies, z_in_ref):
        for copy in copies:
            copy.wait_recv()
        total = f32(z_in_ref[0])
        for at in range(1, 8):
            total = total + f32(z_in_ref[at])
        return total * factor

    @pl.loop(0, 4)
    def _(at):
        cols = pl.ds(pl.multiple_of(at * 384, 128), 384)
        term = lax.dot_general(
            full_ref[:, :, :, cols].reshape(1024, 384),
            swish_ref[...],
            over_frames,
            preferred_element_type=jnp.float32,
        ).astype(bf16)
        for k in range(4):
            out_ref[at, k] = term[96 * k : 96 * k + 96]

    out_set = (out_a, out_b, out_plus, out_minus)
    wide_set = (wide_a, wide_b, wide_plus, wide_minus)
    tail_set = (tail_a, tail_b, tail_plus, tail_minus)
    out_begun = begin_y(out_ref, *out_set)

    for at, first in ((0, 0), (1, 1040)):
        edges[1 - at].wait_recv()
        cot_0[first : first + 16] = far_in[at, :, :128]
        cot_1[first : first + 16] = far_in[at, :, 128:]

    def back(row, lanes, cot, glu):
        rows = pl.ds(pl.multiple_of(row, 32), 32)
        wide = pl.ds(pl.multiple_of(row + 16, 16), 32)
        ahead, behind = (ahead_ref[rows], behind_ref[rows])
        here = cot[wide]
        total = jnp.zeros((32, 128), jnp.float32)
        for k in range(KERNEL):
            off = k - KERNEL // 2
            near = nearby(ahead, behind, off)
            shifted = pl.ds(row + 16 + off, 32)
            m = KERNEL - 1 - k
            total = total + taps[m : m + 1, lanes] * jnp.where(near, cot[shifted], 0.0)
            term = here * jnp.where(near, glu[shifted], 0.0)
            tap_sums[k, :, lanes] += jnp.sum(term.reshape(4, 8, 128), axis=0)
        value, sig = (lin_ref[rows, lanes], sig_ref[rows, lanes])
        return rows, total * sig, total * value * sig * (1.0 - sig)

    @pl.loop(0, 1024, step=32)
    def _(row):
        rows, value_cot, gate_cot = back(row, slice(0, 128), cot_0, glu_0)
        both_cot[rows, :128] = value_cot.astype(bf16)
        both_cot[rows, 128:256] = gate_cot.astype(bf16)

    out_passed = pass_y(out_begun, out_ref, *out_set)

    @pl.loop(0, 4)
    def _(at):
        cols = pl.ds(pl.multiple_of(at * 384, 128), 384)
        term = lax.dot_general(
            norm_ref[:, cols],
            both_cot[:, :256],
            over_frames,
            preferred_element_type=jnp.float32,
        ).astype(bf16)
        for k in range(4):
            wide_ref[at, k] = term[96 * k : 96 * k + 96]

    wide_begun = begin_y(wide_ref, *wide_set)

    def back_tail(row):
        rows, value_cot, gate_cot = back(row, slice(128, 256), cot_1, glu_1)
        both_cot[rows, 256:] = (value_cot + pltpu.roll(gate_cot, 64, 1)).astype(bf16)

    @pl.loop(0, 512, step=32)
    def _(row):
        back_tail(row)

    out_z_copies = begin_z(out_passed, out_ref, out_plus, out_minus, out_mid, out_z)

    @pl.loop(512, 1024, step=32)
    def _(row):
        back_tail(row)

    wide_passed = pass_y(wide_begun, wide_ref, *wide_set)
    kern_ref[...] = jnp.zeros(kern_ref.shape, jnp.float32)
    for k in range(KERNEL):
        kern_ref[k : k + 1] = jnp.sum(tap_sums[k], axis=0, keepdims=True)
    kern_y[y] = kern_ref[...]
    kern_copies = [net.send(kern_ref, kern_y.at[y], y_peer(k)) for k in (2, 1, 3)]

    def shares(refs, copies):
        for copy in copies:
            copy.wait_recv()
        total = refs[0]
        for at in range(1, refs.shape[0]):
            total = total + refs[at]
        return total

    gain_sums[...] = jnp.zeros(gain_sums.shape, jnp.float32)
    core_copies = []

    def norm_part(at):
        first, size = HALVES[at]

        @pl.loop(first, first + size, step=256)
        def _(col):
            cols = pl.ds(pl.multiple_of(col, 256), 256)
            for row in (0, 512):
                part = jnp.dot(
                    both_cot[row : row + 512],
                    pair_ref[:, cols],
                    preferred_element_type=jnp.float32,
                )
                gain_sums[:, cols] += jnp.sum(
                    (part * f32(norm_ref[row : row + 512, cols])).reshape(64, 8, 256), axis=0
                )
                part = part.astype(bf16)
                for k in range(4):
                    part_ref[row // 256 + k // 2, k % 2, :, cols] = part[128 * k : 128 * k + 128]

        cols = pl.ds(first, size)
        core_copies.append(
            net.send(part_ref.at[:, 1 - core, :, cols], core_in.at[:, :, cols], sibling())
        )

    def begin_x(at):
        core_copies[at].wait_recv()
        first, size = HALVES[at]
        cols = pl.ds(first, size)

        def add_core(to):
            @pl.loop(0, 128, step=32)
            def _(row):
                rows = pl.ds(pl.multiple_of(row, 32), 32)
                chip_sum[to, rows, cols] = (
                    f32(part_ref[to, core, rows, cols]) + f32(core_in[to, rows, cols])
                ).astype(bf16)

        add_core(x_far)
        begun = (
            net.send(chip_sum.at[x_far, half_a, cols], x_a.at[:, cols], x_peer(1)),
            net.send(chip_sum.at[x_far, half_b, cols], x_b.at[:, cols], x_peer(-1)),
        )
        add_core(x_next)
        add_core(x_last)
        plain = (
            net.send(chip_sum.at[x_next, half_b, cols], x_plus.at[half_b, cols], x_peer(1)),
            net.send(chip_sum.at[x_last, half_a, cols], x_minus.at[half_a, cols], x_peer(-1)),
        )
        return begun, plain

    def pass_x(at, pending):
        begun, plain = pending
        first, size = HALVES[at]
        cols = pl.ds(first, size)

        def add_x(ref, to, start):
            @pl.loop(0, 64, step=32)
            def _(row):
                rows = pl.ds(pl.multiple_of(row, 32), 32)
                other = pl.ds(pl.multiple_of(row + start, 32), 32)
                ref[rows, cols] = (f32(ref[rows, cols]) + f32(chip_sum[to, other, cols])).astype(
                    bf16
                )

        begun[0].wait_recv()
        add_x(x_a, x_next, 0)
        one = net.send(x_a.at[:, cols], x_plus.at[half_a, cols], x_peer(1))
        begun[1].wait_recv()
        add_x(x_b, x_last, 64)
        return plain + (one, net.send(x_b.at[:, cols], x_minus.at[half_b, cols], x_peer(-1)))

    norm_part(0)
    norm_part(1)
    x_begun = [begin_x(0)]

    gain_ref_in = jnp.sum(gain_sums[...], axis=0, keepdims=True) / gain_row[...]
    gain_out[...] = jnp.zeros(gain_out.shape, jnp.float32)
    for k in range(6):
        gain_out[k : k + 1] = gain_ref_in[:, 256 * k : 256 * k + 256]
    gain_in[te] = gain_out[...]
    gain_copies = [net.send(gain_out, gain_in.at[te], t_peer(k)) for k in range(1, 8)]
    x_begun.append(begin_x(1))

    @pl.loop(0, 4)
    def _(at):
        cols = pl.ds(pl.multiple_of(at * 384, 128), 384)
        term = lax.dot_general(
            norm_ref[:, cols],
            both_cot[:, 256:],
            over_frames,
            preferred_element_type=jnp.float32,
        ).astype(bf16)
        for k in range(4):
            tail_ref[at, k] = term[96 * k : 96 * k + 96]

    tail_begun = begin_y(tail_ref, *tail_set)
    kern_mid[...] = shares(kern_y, kern_copies)
    kern_z[z] = kern_mid[...]
    kern_copies = [net.send(kern_mid, kern_z.at[z], z_peer(k)) for k in (4, 3, 5, 2, 6, 1, 7)]
    wide_z_copies = begin_z(wide_passed, wide_ref, wide_plus, wide_minus, wide_mid, wide_z)
    gain_mid[...] = shares(gain_in, gain_copies)
    gain_y[y] = gain_mid[...]
    gain_copies = [net.send(gain_mid, gain_y.at[y], y_peer(k)) for k in (2, 1, 3)]
    x_passed = [pass_x(0, x_begun[0])]
    tail_passed = pass_y(tail_begun, tail_ref, *tail_set)
    x_passed.append(pass_x(1, x_begun[1]))
    gain_last[...] = shares(gain_y, gain_copies)
    gain_z[z] = gain_last[...]
    gain_copies = [net.send(gain_last, gain_z.at[z], z_peer(k)) for k in (4, 3, 5, 2, 6, 1, 7)]
    tail_z_copies = begin_z(tail_passed, tail_ref, tail_plus, tail_minus, tail_mid, tail_z)

    out_sum[...] = end_z(out_z_copies, out_z)
    wide_sum[...] = end_z(wide_z_copies, wide_z)
    small_sum[pl.ds(0, 32), :] = shares(kern_z, kern_copies) * factor

    for copies in x_passed:
        for copy in copies:
            copy.wait_recv()

    @pl.loop(0, 8)
    def _(block):
        rows = pl.ds(pl.multiple_of(block * 16, 16), 16)
        summed = (
            f32(part_ref[x, core, rows])
            + f32(core_in[x, rows])
            + f32(x_plus[rows])
            + f32(x_minus[rows])
        )
        normed = own_normed[rows]
        scaled = summed * gain_row[...]
        input_grad[rows] = (
            f32(full_ref[te, block])
            + own_scale[rows, :1]
            * (
                scaled
                - jnp.mean(scaled, axis=1, keepdims=True)
                - normed * jnp.mean(scaled * normed, axis=1, keepdims=True)
            )
        ).astype(bf16)

    tail_sum[...] = end_z(tail_z_copies, tail_z)
    small_sum[pl.ds(32, 8), :] = shares(gain_z, gain_copies) * factor
    net.finish()


def joint_call(table, lengths, frames, blocks, value_weight, gate_weight, out_weight, taps, gain):
    count, width = frames.shape
    span = value_weight.shape[0]
    bf16, single = (jnp.bfloat16, jnp.float32)
    vmem = pl.BlockSpec(memory_space=pltpu.VMEM)
    smem = pl.BlockSpec(memory_space=pltpu.SMEM)
    where = pl.BlockSpec(memory_space=pl.ANY)

    def weight_scratch(lanes):
        return [
            pltpu.VMEM((4, 4, 96, lanes), bf16),
            pltpu.VMEM((2, 96, lanes), bf16),
            pltpu.VMEM((2, 96, lanes), bf16),
            pltpu.VMEM((4, 96, lanes), bf16),
            pltpu.VMEM((4, 96, lanes), bf16),
            pltpu.VMEM((8, 48, lanes), bf16),
            pltpu.VMEM((8, 48, lanes), bf16),
        ]

    return pl.pallas_call(
        joint_kernel,
        out_shape=(
            jax.ShapeDtypeStruct((128, width), bf16),
            jax.ShapeDtypeStruct((48, 256), single),
            jax.ShapeDtypeStruct((48, 128), single),
            jax.ShapeDtypeStruct((48, 256), single),
            jax.ShapeDtypeStruct((40, 256), single),
        ),
        in_specs=[smem] * 2 + [where] * 5 + [vmem] * 2,
        out_specs=[vmem] * 5,
        scratch_shapes=[
            pltpu.VMEM((count, width), bf16),
            pltpu.VMEM((2 * span, width), bf16),
            pltpu.VMEM((256, width), bf16),
            pltpu.VMEM((32, 256), single),
            pltpu.VMEM((count, 128), jnp.int32),
            pltpu.VMEM((count, 128), jnp.int32),
            pltpu.VMEM((count, width), bf16),
            pltpu.VMEM((count, 256), single),
            pltpu.VMEM((count, 256), single),
            pltpu.VMEM((count, 256), single),
            pltpu.VMEM((count + 32, 128), single),
            pltpu.VMEM((count + 32, 128), single),
            pltpu.VMEM((8, 8, 16, width), bf16),
            pltpu.VMEM((count, 256), bf16),
            pltpu.VMEM((count, 256), single),
            pltpu.VMEM((count + 32, 128), single),
            pltpu.VMEM((count + 32, 128), single),
            pltpu.VMEM((count, 2 * span), bf16),
            pltpu.VMEM((KERNEL, 8, 256), single),
            pltpu.VMEM((8, width), single),
            pltpu.VMEM((512, 4 * SLOTS), bf16),
            pltpu.VMEM((2, 16, 256), bf16),
            pltpu.VMEM((2, 16, 256), bf16),
            pltpu.VMEM((2, 16, 256), single),
            pltpu.VMEM((2, 16, 256), single),
            pltpu.VMEM((4, 2, 128, width), bf16),
            pltpu.VMEM((4, 128, width), bf16),
            pltpu.VMEM((4, 128, width), bf16),
            pltpu.VMEM((64, width), bf16),
            pltpu.VMEM((64, width), bf16),
            pltpu.VMEM((128, width), bf16),
            pltpu.VMEM((128, width), bf16),
        ]
        + weight_scratch(256)
        + weight_scratch(128)
        + weight_scratch(256)
        + [
            pltpu.VMEM((1, width), single),
            pltpu.VMEM((128, width), single),
            pltpu.VMEM((128, 128), single),
            pltpu.VMEM((32, 256), single),
            pltpu.VMEM((4, 32, 256), single),
            pltpu.VMEM((32, 256), single),
            pltpu.VMEM((8, 32, 256), single),
            pltpu.VMEM((8, 256), single),
            pltpu.VMEM((8, 8, 256), single),
            pltpu.VMEM((8, 256), single),
            pltpu.VMEM((4, 8, 256), single),
            pltpu.VMEM((8, 256), single),
            pltpu.VMEM((8, 8, 256), single),
            pltpu.SemaphoreType.DMA((len(CHUNKS) + 6,)),
            pltpu.SemaphoreType.DMA((COPIES,)),
            pltpu.SemaphoreType.DMA((COPIES,)),
        ]
        + [pltpu.VMEM((3, SLOTS, size), bf16) for _, size in CHUNKS]
        + [pltpu.VMEM((4, SLOTS, size), bf16) for _, size in CHUNKS]
        + [pltpu.VMEM((4, 128, size), bf16) for _, size in CHUNKS]
        + [pltpu.VMEM((2, 128, size), bf16) for _, size in CHUNKS]
        + [pltpu.VMEM((64, 16, size), bf16) for _, size in CHUNKS]
        + [pltpu.VMEM((2, 64, size), bf16) for _, size in CHUNKS],
        compiler_params=pltpu.CompilerParams(
            collective_id=0, has_side_effects=True, vmem_limit_bytes=60 * 1024 * 1024
        ),
        name="joint",
    )(table, lengths, frames, blocks, value_weight, gate_weight, out_weight, taps, gain)


def finish_kernel(
    input_ref,
    wide_ref,
    tail_ref,
    out_ref,
    small_ref,
    input_grad,
    value_grad,
    gate_grad,
    out_grad,
    kernel_grad,
    gain_grad,
):
    input_grad[...] = input_ref[...]
    tail = tail_ref[...]
    value_grad[:, :128] = wide_ref[:, :128]
    value_grad[:, 128:] = tail[:, :64]
    gate_grad[:, :128] = wide_ref[:, 128:]
    gate_grad[:, 128:] = pltpu.roll(tail, 64, 1)[:, :64]
    out_grad[...] = out_ref[:, :192]
    kernel_grad[...] = small_ref[:KERNEL, :192]
    for k in range(6):
        gain_grad[256 * k : 256 * k + 256] = small_ref[32 + k]


def finish_call(*sums):
    single = jnp.float32
    width = sums[0].shape[1]
    vmem = pl.BlockSpec(memory_space=pltpu.VMEM)
    return pl.pallas_call(
        finish_kernel,
        out_shape=(jax.ShapeDtypeStruct(sums[0].shape, jnp.bfloat16),)
        + (jax.ShapeDtypeStruct((48, 192), single),) * 3
        + (
            jax.ShapeDtypeStruct((KERNEL, 192), single),
            jax.ShapeDtypeStruct((width,), single),
        ),
        in_specs=[vmem] * 5,
        out_specs=[vmem] * 6,
        name="finish",
    )(*sums)


def routing(block_device, block_sub, block_rows):
    tm, te, dp = places()
    first = (tm // 4) * 4
    code = block_device.reshape(1, 1024) + 16 * block_sub + 128 * block_rows
    code = code.reshape(16, 64)
    near = lax.dynamic_slice_in_dim(code, first, 4, 0)
    devices, subs = (near % 16, (near // 16) % 8)
    counts = lax.dynamic_slice_in_dim(code, tm, 1, 0) // 128
    earlier = jnp.arange(64)[:, None] > jnp.arange(64)[None, :]
    column = devices % 4
    same = (column[:, :, None] == column[:, None, :]) & earlier[None]
    rank = jnp.sum(same.astype(jnp.int32), axis=2)
    slot = column * 20 + rank
    own = lax.dynamic_slice_in_dim(slot, tm % 4, 1, 0)
    own_hot = own == jnp.arange(80, dtype=jnp.int32)[:, None]
    source = jnp.sum(jnp.where(own_hot, jnp.arange(64, dtype=jnp.int32)[None], 0), axis=1)
    live = jnp.sum(jnp.where(own_hot, jnp.clip(counts - te * 16, 0, 16), 0), axis=1)
    place = (tm % 4) * 20 + jnp.arange(20, dtype=jnp.int32)
    hot = slot[:, None, :] == place[None, :, None]
    block = (devices // 4) * 8 + subs
    dest = jnp.sum(jnp.where(hot, block[:, None, :] + 1, 0), axis=2).reshape(80) - 1
    return jnp.concatenate([source, live, jnp.where(dest < 0, 64, dest)])


def on_device(
    inputs,
    grad_blocks,
    block_device,
    block_sub,
    block_rows,
    seg_lengths,
    value_weight,
    gate_weight,
    out_weight,
    conv_kernel,
    norm_gain,
):
    sums = joint_call(
        routing(block_device, block_sub, block_rows),
        seg_lengths,
        inputs[0],
        grad_blocks[0],
        value_weight,
        gate_weight,
        out_weight,
        conv_kernel,
        norm_gain,
    )
    input_grad, value_grad, gate_grad, out_grad, kernel_grad, gain_grad = finish_call(*sums)
    return (
        input_grad[None],
        value_grad.T,
        gate_grad.T,
        out_grad.T,
        kernel_grad,
        gain_grad,
    )


def solution(mesh):
    in_specs = (
        P("dp", "tm", None),
        P("dp", "tm", "tensor", None),
        P("dp", None, None),
        P("dp", None),
        P("dp", None),
        P("dp", None),
        P("tensor", None),
        P("tensor", None),
        P("tensor", None),
        P(None, "tensor"),
        P(),
    )
    out_specs = (
        P("dp", ("tm", "tensor"), None),
        P("tensor", ("tm", "dp")),
        P("tensor", ("tm", "dp")),
        P("tensor", ("tm", "dp")),
        P(None, "tensor"),
        P(),
    )
    return jax.shard_map(
        on_device, mesh=mesh, in_specs=in_specs, out_specs=out_specs, check_vma=False
    )
```
